32 devices in a mesh: section: 4 (over y, x), ctx: 4 (over z), tp: 2 (over core).
Axes of the slice: x: 2, y: 2, z: 4, core: 2. Of those that a mesh axis runs over, the one named last changes fastest.
Arguments:
- section_input: float32 [4, 512, 4096], P('section', 'ctx', 'tp'), may hold values from -60 to 60
- long_filter: bfloat16 [4, 512, 256], P('section', 'ctx', 'tp'), may hold values from -2 to 2
- short_filter: bfloat16 [4, 3, 3, 4096], P('section', None, None, 'tp'), may hold values from -12 to 12
- skip_gain: float32 [4, 4096], P('section', 'tp'), may hold values from -1 to 1
Outputs:
- received: float32 [4, 512, 4096], P('section', 'ctx', 'tp')
The draws below stay inside these ranges and needn't reach their ends.
All inputs are finite; a program needn't handle non-finite values.
Results may differ from the reference program's by a relative error of at most 0.009.
Values may be sent and summed in bfloat16 or wider, within the bound.
No kernel may reach another device: no remote copies, remote signals or barrier semaphores. Data moves between devices by JAX's collectives and lax.ppermute only.
A program may use at most 64 MiB of HBM per device.

```python
import math
import jax
import jax.numpy as jnp
from jax import lax

CHAN = 4096
GROUP = 16
TAPS = 3
BLOCK = 128
SEQ = 512
FILTERS = 256
N_SECTION = 4


def channel_scale(key, spread):
    ranks = jax.random.permutation(jax.random.fold_in(key, 11), CHAN).astype(jnp.float32)
    return jnp.exp(math.log(spread) * ((ranks + 0.5) / CHAN - 0.5))


def draw_section_input(key, part):
    key_entries, key_rows = jax.random.split(key)
    column_scale = channel_scale(key, 10.0)[None, None, :]
    row_scale = jnp.exp(jax.random.uniform(key_rows, (N_SECTION, SEQ, 1), jnp.float32, math.log(0.3), math.log(3.0)))
    entries = jax.random.truncated_normal(key_entries, -6.0, 6.0, (N_SECTION, SEQ, CHAN), jnp.float32)
    return entries * row_scale * column_scale


def draw_short_filter(key, part):
    key_entries = jax.random.fold_in(key, 23)
    column_scale = channel_scale(key, 10.0)
    entries = jax.random.truncated_normal(key_entries, -3.0, 3.0, (N_SECTION, 3, TAPS, CHAN), jnp.float32)
    return (entries / column_scale[None, None, None, :]).astype(jnp.bfloat16)


def draw_long_filter(key, part):
    key_rates, key_entries = jax.random.split(key)
    lags = jnp.arange(SEQ, dtype=jnp.float32)[None, :, None]
    log_span = jax.random.uniform(key_rates, (N_SECTION, 1, FILTERS), jnp.float32, math.log(30.0), math.log(256.0 * SEQ))
    entries = jax.random.truncated_normal(key_entries, -6.0, 6.0, (N_SECTION, SEQ, FILTERS), jnp.float32)
    decay_rate = jnp.exp(-log_span)
    energy = jnp.expm1(-2.0 * decay_rate) / jnp.expm1(-2.0 * decay_rate * SEQ)
    return (entries * jnp.exp(-decay_rate * lags) * jnp.sqrt(energy)).astype(jnp.bfloat16)


def levels(rng, dims, cuts, least, high):
    factor_of = 1.0
    for dim, parts in cuts:
        heights = jax.random.uniform(jax.random.fold_in(jax.random.fold_in(rng, 6), dim), (parts,), jnp.float32, least / len(cuts), high / len(cuts))
        factor_of = factor_of * jnp.repeat(jnp.exp(heights), dims[dim] // parts).reshape((-1,) + (1,) * (len(dims) - 1 - dim))
    return factor_of


def setup_inputs(seed: int = 0) -> dict:
    keys = jax.random.split(jax.random.key(seed), 5)
    section_input = draw_section_input(jax.random.fold_in(keys[4], 71), 0)
    long_filter = draw_long_filter(jax.random.fold_in(keys[4], 71), 0)
    short_filter = draw_short_filter(jax.random.fold_in(keys[4], 71), 0)
    skip_gain = jnp.clip(jax.random.uniform(keys[3], (N_SECTION, CHAN), jnp.float32, -1.0, 1.0) * levels(keys[3], (N_SECTION, CHAN), ((0, 4), (1, 2)), -0.4, 0.0), -1.0, 1.0)
    return dict(section_input=section_input, long_filter=long_filter, short_filter=short_filter, skip_gain=skip_gain)


TWO_PI = 6.283185307179586

def unit_pair(position, period):
    mirror = period - position
    folded = jnp.minimum(position, mirror)
    angle_value = folded.astype(jnp.float32) * (TWO_PI / period)
    cosine = jnp.where(4 * folded == period, 0.0, jnp.cos(angle_value)).astype(jnp.float32)
    sine_part = jnp.where((folded == 0) | (2 * folded == period), 0.0, jnp.sin(angle_value)).astype(jnp.float32)
    sine_part = jnp.where(position > mirror, -sine_part, sine_part)
    return (cosine, -sine_part)

def first_section(table_re, table_im, data):
    plain = data.astype(jnp.float32)
    real_out = jnp.einsum('ka,abc->kbc', table_re.astype(jnp.float32), plain)
    imag_out = jnp.einsum('ka,abc->kbc', table_im.astype(jnp.float32), plain)
    return (real_out.astype(jnp.bfloat16), imag_out.astype(jnp.bfloat16))

def rotate(turn_re, turn_im, data_re, data_im):
    plain_re = data_re.astype(jnp.float32)
    plain_im = data_im.astype(jnp.float32)
    real_out = turn_re[:, :, None] * plain_re - turn_im[:, :, None] * plain_im
    imag_out = turn_re[:, :, None] * plain_im + turn_im[:, :, None] * plain_re
    return (real_out.astype(jnp.bfloat16), imag_out.astype(jnp.bfloat16))

def mix_rows(form, table_re, table_im, data_re, data_im):

    def product_of(left, right):
        return jnp.einsum(form, left.astype(jnp.float32), right.astype(jnp.float32))
    real_out = product_of(table_re, data_re) - product_of(table_im, data_im)
    imag_out = product_of(table_re, data_im) + product_of(table_im, data_re)
    return (real_out, imag_out)

def apply_filter(spec_re, spec_im, filt_re, filt_im):
    rows_count, inner_width, channels = spec_re.shape
    filters = filt_re.shape[2]
    grouped_shape = (rows_count, inner_width, filters, channels // filters)
    grouped_re = spec_re.reshape(grouped_shape)
    grouped_im = spec_im.reshape(grouped_shape)
    gain_re = filt_re[..., None]
    gain_im = filt_im[..., None]
    out_re = (grouped_re * gain_re - grouped_im * gain_im).reshape(spec_re.shape)
    out_im = (grouped_re * gain_im + grouped_im * gain_re).reshape(spec_re.shape)
    return (out_re.astype(jnp.bfloat16), out_im.astype(jnp.bfloat16))

def convolve(product, kernel):
    half_span = SEQ // BLOCK
    full_span = 2 * half_span
    freq_total = full_span * BLOCK
    block_ids = jnp.arange(half_span, dtype=jnp.int32)
    freq_rows = jnp.arange(full_span, dtype=jnp.int32)
    inner_ids = jnp.arange(BLOCK, dtype=jnp.int32)
    outer_re, outer_im = unit_pair(freq_rows[:, None] * block_ids[None, :] % full_span, full_span)
    outer_re = outer_re.astype(jnp.bfloat16)
    outer_im = outer_im.astype(jnp.bfloat16)
    inner_re, inner_im = unit_pair(inner_ids[:, None] * inner_ids[None, :] % BLOCK, BLOCK)
    inner_re = inner_re.astype(jnp.bfloat16)
    inner_im = inner_im.astype(jnp.bfloat16)
    turn_re, turn_im = unit_pair(freq_rows[:, None] * inner_ids[None, :] % freq_total, freq_total)
    kernel_blocks = kernel.reshape(half_span, BLOCK, FILTERS)
    kern_re, kern_im = first_section(outer_re, outer_im, kernel_blocks)
    kern_re, kern_im = rotate(turn_re, turn_im, kern_re, kern_im)
    filt_re, filt_im = mix_rows('qb,rbc->rqc', inner_re, inner_im, kern_re, kern_im)
    block_width = math.gcd(CHAN, 256)
    block_count = CHAN // block_width
    signal_blocks = product.reshape(half_span, BLOCK, block_count, block_width).transpose(2, 0, 1, 3)
    filt_re_blocks = filt_re.reshape(full_span, BLOCK, block_count, block_width // GROUP).transpose(2, 0, 1, 3)
    filt_im_blocks = filt_im.reshape(full_span, BLOCK, block_count, block_width // GROUP).transpose(2, 0, 1, 3)

    def one_block(pieces):
        signal_part, filt_re_part, filt_im_part = pieces
        first_re, first_im = first_section(outer_re, outer_im, signal_part)
        turned_re, turned_im = rotate(turn_re, turn_im, first_re, first_im)
        spec_re, spec_im = mix_rows('qb,rbc->rqc', inner_re, inner_im, turned_re, turned_im)
        weight_re, weight_im = apply_filter(spec_re, spec_im, filt_re_part, filt_im_part)
        back_re, back_im = mix_rows('bq,rqc->rbc', inner_re, -inner_im, weight_re, weight_im)
        unturn_re, unturn_im = rotate(turn_re, -turn_im, back_re, back_im)
        conv_part = jnp.einsum('ka,kbc->abc', outer_re.astype(jnp.float32), unturn_re.astype(jnp.float32))
        conv_part = conv_part + jnp.einsum('ka,kbc->abc', outer_im.astype(jnp.float32), unturn_im.astype(jnp.float32))
        return (conv_part * (1.0 / freq_total)).astype(jnp.bfloat16)
    results = lax.map(one_block, (signal_blocks, filt_re_blocks, filt_im_blocks))
    return results.transpose(1, 2, 0, 3).reshape(SEQ, CHAN)

def layer(acts, kernel, short_taps, skip_row):
    squares = lax.optimization_barrier(jnp.sum(acts * acts, axis=1, keepdims=True)) / CHAN
    normed = (acts * lax.rsqrt(squares + 1e-06)).astype(jnp.bfloat16)
    padded = jnp.concatenate([jnp.zeros((TAPS - 1, CHAN), jnp.bfloat16), normed], axis=0).astype(jnp.float32)
    taps_all = short_taps.astype(jnp.float32)
    featured = []
    for feature_id in range(3):
        running = jnp.zeros((SEQ, CHAN), jnp.float32)
        for offset in range(TAPS):
            begin_row = TAPS - 1 - offset
            running = running + taps_all[feature_id, offset][None, :] * padded[begin_row:begin_row + SEQ]
        featured.append(running)
    query = featured[0].astype(jnp.bfloat16)
    product = (featured[1] * featured[2]).astype(jnp.bfloat16)
    conv = convolve(product, kernel)
    return acts + query.astype(jnp.float32) * (conv.astype(jnp.float32) + skip_row[None, :] * product.astype(jnp.float32))

def reference(section_input, long_filter, short_filter, skip_gain):
    finished = []
    for section_id in range(N_SECTION):
        finished.append(layer(section_input[section_id], long_filter[section_id], short_filter[section_id], skip_gain[section_id]))
    return jnp.roll(jnp.stack(finished), 1, axis=0)
```

```python
import functools

import jax
import jax.numpy as jnp
import ml_dtypes
import numpy as np
from jax import lax
from jax.experimental import pallas as pl
from jax.experimental.pallas import tpu as pltpu
from jax.sharding import PartitionSpec as P

CHAN = 4096
TAPS = 3
BLOCK = 128


TWO_PI = 6.283185307179586


def from_behind(block, axis, distance):
    devices = range(lax.axis_size(axis))
    route = [(i - distance, i) for i in devices if i - distance in devices]
    return lax.ppermute(block, axis, route)


def passed_along(x, axis, by):
    peers = lax.axis_size(axis)
    return lax.ppermute(x, axis, [(i, (i + by) % peers) for i in range(peers)])


def unit_pair(position, period):
    mirror = period - position
    folded = jnp.minimum(position, mirror)
    angle_value = folded.astype(jnp.float32) * (TWO_PI / period)
    cosine = jnp.where(4 * folded == period, 0.0, jnp.cos(angle_value))
    sine_part = jnp.where((folded == 0) | (2 * folded == period), 0.0, jnp.sin(angle_value))
    sine_part = jnp.where(position > mirror, -sine_part, sine_part)
    return (cosine, -sine_part)


def first_section(table_re, table_im, data):
    real_out = jnp.einsum("ka,abc->kbc", table_re, data, preferred_element_type=jnp.float32)
    imag_out = jnp.einsum("ka,abc->kbc", table_im, data, preferred_element_type=jnp.float32)
    return (real_out.astype(jnp.bfloat16), imag_out.astype(jnp.bfloat16))


def rotate(turn_re, turn_im, data_re, data_im):
    plain_re = data_re.astype(jnp.float32)
    plain_im = data_im.astype(jnp.float32)
    real_out = turn_re[:, :, None] * plain_re - turn_im[:, :, None] * plain_im
    imag_out = turn_re[:, :, None] * plain_im + turn_im[:, :, None] * plain_re
    return (real_out.astype(jnp.bfloat16), imag_out.astype(jnp.bfloat16))


def mix_rows(form, table_re, table_im, data_re, data_im):

    def product_of(left, right):
        return jnp.einsum(form, left, right, preferred_element_type=jnp.float32)

    real_out = product_of(table_re, data_re) - product_of(table_im, data_im)
    imag_out = product_of(table_re, data_im) + product_of(table_im, data_re)
    return (real_out, imag_out)


def apply_filter(spec_re, spec_im, filt_re, filt_im):
    rows_count, inner_width, channels = spec_re.shape
    filters = filt_re.shape[2]
    grouped_shape = (rows_count, inner_width, filters, channels // filters)
    grouped_re = spec_re.reshape(grouped_shape)
    grouped_im = spec_im.reshape(grouped_shape)
    gain_re = filt_re[..., None]
    gain_im = filt_im[..., None]
    out_re = (grouped_re * gain_re - grouped_im * gain_im).reshape(spec_re.shape)
    out_im = (grouped_re * gain_im + grouped_im * gain_re).reshape(spec_re.shape)
    return (out_re.astype(jnp.bfloat16), out_im.astype(jnp.bfloat16))


def spectral_middle(parts, local_freq, inner_re, inner_im, freq_total):
    sig_re, sig_im, kern_re, kern_im = parts
    inner_ids = jnp.arange(BLOCK, dtype=jnp.int32)
    turn_re, turn_im = unit_pair(local_freq[:, None] * inner_ids[None, :] % freq_total, freq_total)
    turned_re, turned_im = rotate(turn_re, turn_im, sig_re, sig_im)
    kturn_re, kturn_im = rotate(turn_re, turn_im, kern_re, kern_im)
    spec_re, spec_im = mix_rows("qb,rbc->rqc", inner_re, inner_im, turned_re, turned_im)
    filt_re, filt_im = mix_rows("qb,rbc->rqc", inner_re, inner_im, kturn_re, kturn_im)
    weight_re, weight_im = apply_filter(spec_re, spec_im, filt_re, filt_im)
    back_re, back_im = mix_rows("bq,rqc->rbc", inner_re, -inner_im, weight_re, weight_im)
    return rotate(turn_re, -turn_im, back_re, back_im)


def block_columns(signal, kernel):
    return (
        lax.all_to_all(signal, "ctx", split_axis=1, concat_axis=0, tiled=True),
        lax.all_to_all(kernel, "ctx", split_axis=1, concat_axis=0, tiled=True),
    )


def token_rows(conv_vals):
    return lax.all_to_all(conv_vals, "ctx", split_axis=0, concat_axis=1, tiled=True)


def general_local(section_input, long_filter, short_filter, skip_gain):
    acts_local = section_input[0]
    tok_rows, chan_local = acts_local.shape
    filt_local = long_filter.shape[2]
    n_ctx = lax.axis_size("ctx")
    ctx_rank = lax.axis_index("ctx")
    blocks_local = tok_rows // BLOCK
    half_span = blocks_local * n_ctx
    full_span = 2 * half_span
    freq_total = full_span * BLOCK
    rows_local = full_span // n_ctx
    partial_squares = jnp.sum(acts_local * acts_local, axis=1)
    total_squares = lax.psum(partial_squares, "tp")
    normed = (acts_local * lax.rsqrt(total_squares / CHAN + 1e-06)[:, None]).astype(jnp.bfloat16)
    earlier = from_behind(normed[tok_rows - (TAPS - 1) :], "ctx", 1)
    extended = jnp.concatenate([earlier, normed], axis=0)
    taps_all = short_filter[0].astype(jnp.float32)
    featured = []
    for feature_id in range(3):
        running = jnp.zeros((tok_rows, chan_local), jnp.float32)
        for offset in range(TAPS):
            begin_row = TAPS - 1 - offset
            running = (
                running
                + taps_all[feature_id, offset][None, :] * extended[begin_row : begin_row + tok_rows]
            )
        featured.append(running)
    query = featured[0].astype(jnp.bfloat16)
    product = (featured[1] * featured[2]).astype(jnp.bfloat16)
    block_ids = jnp.arange(half_span, dtype=jnp.int32)
    inner_ids = jnp.arange(BLOCK, dtype=jnp.int32)
    inner_re, inner_im = unit_pair(inner_ids[:, None] * inner_ids[None, :] % BLOCK, BLOCK)
    inner_re = inner_re.astype(jnp.bfloat16)
    inner_im = inner_im.astype(jnp.bfloat16)
    signal = product.reshape(blocks_local, BLOCK, chan_local)
    kernel = long_filter[0].reshape(blocks_local, BLOCK, filt_local)
    signal_cols, kernel_cols = block_columns(signal, kernel)
    freq_rows = jnp.arange(full_span, dtype=jnp.int32)
    outer_re, outer_im = unit_pair(freq_rows[:, None] * block_ids[None, :] % full_span, full_span)
    table_re = outer_re.astype(jnp.bfloat16)
    table_im = outer_im.astype(jnp.bfloat16)
    sig_re, sig_im = first_section(table_re, table_im, signal_cols)
    kern_re, kern_im = first_section(table_re, table_im, kernel_cols)
    got = (
        lax.all_to_all(sig_re, "ctx", split_axis=0, concat_axis=1, tiled=True),
        lax.all_to_all(sig_im, "ctx", split_axis=0, concat_axis=1, tiled=True),
        lax.all_to_all(kern_re, "ctx", split_axis=0, concat_axis=1, tiled=True),
        lax.all_to_all(kern_im, "ctx", split_axis=0, concat_axis=1, tiled=True),
    )
    local_freq = ctx_rank * rows_local + jnp.arange(rows_local, dtype=jnp.int32)
    back_re, back_im = spectral_middle(got, local_freq, inner_re, inner_im, freq_total)
    gathered_re, gathered_im = (
        lax.all_to_all(back_re, "ctx", split_axis=1, concat_axis=0, tiled=True),
        lax.all_to_all(back_im, "ctx", split_axis=1, concat_axis=0, tiled=True),
    )
    conv_vals = jnp.einsum("ka,kbc->abc", table_re, gathered_re, preferred_element_type=jnp.float32)
    conv_vals = conv_vals + jnp.einsum(
        "ka,kbc->abc", table_im, gathered_im, preferred_element_type=jnp.float32
    )
    conv_vals = (conv_vals * (1.0 / freq_total)).astype(jnp.bfloat16)
    conv_tokens = token_rows(conv_vals).reshape(tok_rows, chan_local)
    finished = acts_local + query.astype(jnp.float32) * (
        conv_tokens.astype(jnp.float32) + skip_gain[0][None, :] * product.astype(jnp.float32)
    )
    received = passed_along(finished.astype(jnp.bfloat16), "section", 1).astype(finished.dtype)
    return received[None]


EXTRA = 16
LANES = 128


def odd_tables(length):
    phase = (2 * np.arange(length)[:, None] + 1) * np.arange(length)[None, :] % (4 * length)
    turn = phase * (2.0 * np.pi / (4 * length))
    ahead = np.concatenate([np.cos(turn), -np.sin(turn)], axis=0)
    return ahead.astype(ml_dtypes.bfloat16), (ahead.T / length).astype(ml_dtypes.bfloat16)


def spread_table(filters, channels):
    owner = np.arange(channels) // (channels // filters)
    return (np.arange(filters)[:, None] == owner[None, :]).astype(ml_dtypes.bfloat16)


def column_of(row):
    return jnp.transpose(jnp.broadcast_to(row[:1], (LANES, row.shape[1])))


def cut_kernel(peers, place, x_ref, filt_ref, *refs):
    outs, sums_ref, turned = refs[:peers], refs[peers], refs[peers + 1]
    rank = place[0]
    rows, chans = x_ref.shape
    width = chans // peers
    filters = filt_ref.shape[1] // peers
    turned[...] = jnp.transpose(filt_ref[...].astype(jnp.float32)).astype(jnp.bfloat16)
    total = jnp.zeros((rows, LANES), jnp.float32)
    for step in range(peers):
        target = lax.rem(rank + step, peers)
        part = x_ref[:, pl.ds(pl.multiple_of(target * width, width), width)]
        square = part * part
        for first in range(0, width, LANES):
            total = total + square[:, first : first + LANES]
        outs[step][:rows, :] = part.astype(jnp.bfloat16)
        own = turned[pl.ds(pl.multiple_of(target * filters, filters), filters), :]
        extra = [own[first : first + EXTRA] for first in range(0, filters, EXTRA)]
        extra.append(jnp.zeros((EXTRA, width - rows * len(extra)), jnp.bfloat16))
        outs[step][rows:, :] = jnp.concatenate(extra, axis=1)
    column = jnp.sum(total, axis=1, keepdims=True)
    sums_ref[...] = jnp.transpose(jnp.broadcast_to(column, (rows, LANES)))[:8, :]


def layer_kernel(peers, place, *refs):
    blocks = refs[:peers]
    sums = refs[peers : 2 * peers]
    taps_ref, skip_ref, ahead_ref, return_ref, spread_ref = refs[2 * peers : 2 * peers + 5]
    outs = refs[2 * peers + 5 : 3 * peers + 5]
    held, query, product, spread_filter, spec, filt_spec, weighted, conv = refs[3 * peers + 5 :]
    rank = place[0]
    rows = blocks[0].shape[0] - EXTRA
    width = blocks[0].shape[1]
    filters = spread_ref.shape[0]
    half = rows * peers
    chans = pl.ds(pl.multiple_of(rank * width, width), width)
    held[:8, :] = jnp.zeros((8, width), jnp.float32)
    for step in range(peers):
        begin = pl.multiple_of(lax.rem(rank - step + peers, peers) * rows, rows)
        scale = column_of(lax.rsqrt(sums[step][...] * (1.0 / CHAN) + 1e-06))
        for first in range(0, width, LANES):
            lanes = slice(first, first + LANES)
            held[pl.ds(begin + 8, rows), lanes] = blocks[step][:rows, lanes].astype(jnp.float32) * scale
        parts = [blocks[step][rows:, i * rows : (i + 1) * rows] for i in range(filters // EXTRA)]
        spread_filter[pl.ds(begin, rows), :] = lax.dot_general(
            jnp.concatenate(parts, axis=0),
            spread_ref[...],
            (((0,), (0,)), ((), ())),
            preferred_element_type=jnp.float32,
        ).astype(jnp.bfloat16)
    taps = [[taps_ref[f, i : i + 1, chans].astype(jnp.float32) for i in range(TAPS)] for f in range(3)]
    for block in range(peers):
        begin = block * rows
        moved = [held[pl.ds(begin + 8 - i, rows), :] for i in range(TAPS)]
        features = []
        for feature in range(3):
            running = taps[feature][0] * moved[0]
            for i in range(1, TAPS):
                running = running + taps[feature][i] * moved[i]
            features.append(running)
        query[pl.ds(begin, rows), :] = features[0].astype(jnp.bfloat16)
        product[pl.ds(begin, rows), :] = (features[1] * features[2]).astype(jnp.bfloat16)
    spec[...] = jnp.dot(ahead_ref[...], product[...], preferred_element_type=jnp.float32)
    filt_spec[...] = jnp.dot(ahead_ref[...], spread_filter[...], preferred_element_type=jnp.float32)
    sig_re, sig_im = spec[:half, :], spec[half:, :]
    gain_re, gain_im = filt_spec[:half, :], filt_spec[half:, :]
    weighted[:half, :] = (sig_re * gain_re - sig_im * gain_im).astype(jnp.bfloat16)
    weighted[half:, :] = (sig_re * gain_im + sig_im * gain_re).astype(jnp.bfloat16)
    conv[...] = jnp.dot(return_ref[...], weighted[...], preferred_element_type=jnp.float32)
    skip = skip_ref[:, chans]
    for step in range(peers):
        begin = pl.multiple_of(lax.rem(rank + step, peers) * rows, rows)
        tokens = pl.ds(begin, rows)
        acts = blocks[(peers - step) % peers][:rows, :].astype(jnp.float32)
        gated = conv[tokens, :] + skip * product[tokens, :].astype(jnp.float32)
        outs[step][...] = (acts + query[tokens, :].astype(jnp.float32) * gated).astype(jnp.bfloat16)


def join_kernel(peers, place, *refs):
    out_ref = refs[peers]
    width = refs[0].shape[1]
    for step in range(peers):
        source = lax.rem(place[0] - step + peers, peers)
        chans = pl.ds(pl.multiple_of(source * width, width), width)
        out_ref[:, chans] = refs[step][...].astype(jnp.float32)


def on_device(kernel, place, args, outs, scratch=(), flops=0, limit=32):
    whole = pl.BlockSpec(memory_space=pltpu.VMEM)
    touched = sum(a.size * a.dtype.itemsize for a in (*args, *outs))
    return pl.pallas_call(
        kernel,
        out_shape=outs,
        in_specs=[pl.BlockSpec(memory_space=pltpu.SMEM)] + [whole] * len(args),
        out_specs=[whole] * len(outs),
        scratch_shapes=list(scratch),
        compiler_params=pltpu.CompilerParams(vmem_limit_bytes=limit * 2**20),
        cost_estimate=pl.CostEstimate(flops=flops, bytes_accessed=touched, transcendentals=0),
    )(place, *args)


def hop(x, sections, peers, by_section, by_ctx):
    route = [
        (s * peers + c, (s + by_section) % sections * peers + (c + by_ctx) % peers)
        for s in range(sections)
        for c in range(peers)
    ]
    return lax.ppermute(x, ("section", "ctx"), route)


def channel_local(section_input, long_filter, short_filter, skip_gain):
    acts = section_input[0]
    rows, chans = acts.shape
    sections, peers = lax.axis_size("section"), lax.axis_size("ctx")
    width, filters = chans // peers, long_filter.shape[2] // peers
    half = rows * peers
    place = lax.axis_index("ctx").astype(jnp.int32).reshape(1)
    bf16, f32 = jnp.bfloat16, jnp.float32
    message = jax.ShapeDtypeStruct((rows + EXTRA, width), bf16)
    *sent, sums = on_device(
        functools.partial(cut_kernel, peers),
        place,
        [acts, long_filter[0]],
        [message] * peers + [jax.ShapeDtypeStruct((8, rows), f32)],
        [pltpu.VMEM((long_filter.shape[2], rows), bf16)],
    )
    sums = sums + lax.ppermute(sums, "tp", [(0, 1), (1, 0)])
    got = [sent[0]] + [hop(sent[k], sections, peers, 0, k) for k in range(1, peers)]
    got_sums = [sums] + [hop(sums, sections, peers, 0, k) for k in range(1, peers)]
    ahead, back = odd_tables(half)
    scratch = [
        pltpu.VMEM((half + 8, width), f32),
        pltpu.VMEM((half, width), bf16),
        pltpu.VMEM((half, width), bf16),
        pltpu.VMEM((half, width), bf16),
        pltpu.VMEM((2 * half, width), f32),
        pltpu.VMEM((2 * half, width), f32),
        pltpu.VMEM((2 * half, width), bf16),
        pltpu.VMEM((half, width), f32),
    ]
    done = on_device(
        functools.partial(layer_kernel, peers),
        place,
        [
            *got,
            *got_sums,
            short_filter[0],
            skip_gain,
            jnp.asarray(ahead),
            jnp.asarray(back),
            jnp.asarray(spread_table(filters, width)),
        ],
        [jax.ShapeDtypeStruct((rows, width), bf16)] * peers,
        scratch,
        flops=12 * half * half * width,
    )
    arrived = [hop(done[k], sections, peers, 1, k) for k in range(peers)]
    (received,) = on_device(
        functools.partial(join_kernel, peers), place, arrived, [jax.ShapeDtypeStruct((rows, chans), f32)]
    )
    return received[None]


def fits_channel_plan(mesh, section_input, long_filter):
    peers, cores = mesh.shape["ctx"], mesh.shape["tp"]
    tokens = section_input.shape[1]
    width = section_input.shape[2] // (peers * cores)
    filters = long_filter.shape[2] // (peers * cores)
    return (
        tokens == peers * LANES
        and tokens <= 1024
        and width % LANES == 0
        and filters % EXTRA == 0
        and filters // EXTRA * LANES <= width
    )


def solution(mesh):
    in_specs = (
        P("section", "ctx", "tp"),
        P("section", "ctx", "tp"),
        P("section", None, None, "tp"),
        P("section", "tp"),
    )
    out_specs = P("section", "ctx", "tp")

    def layer(section_input, long_filter, short_filter, skip_gain):
        local = channel_local if fits_channel_plan(mesh, section_input, long_filter) else general_local
        mapped = jax.shard_map(local, mesh=mesh, in_specs=in_specs, out_specs=out_specs, check_vma=False)
        return mapped(section_input, long_filter, short_filter, skip_gain)

    return layer
```

```python
import functools

import jax
import jax.numpy as jnp
import ml_dtypes
import numpy as np
from jax import lax
from jax.experimental import pallas as pl
from jax.experimental.pallas import tpu as pltpu
from jax.sharding import PartitionSpec as P

CHAN = 4096
TAPS = 3
BLOCK = 128


TWO_PI = 6.283185307179586


def from_behind(block, axis, distance):
    devices = range(lax.axis_size(axis))
    route = [(i - distance, i) for i in devices if i - distance in devices]
    return lax.ppermute(block, axis, route)


def passed_along(x, axis, by):
    peers = lax.axis_size(axis)
    return lax.ppermute(x, axis, [(i, (i + by) % peers) for i in range(peers)])


def unit_pair(position, period):
    mirror = period - position
    folded = jnp.minimum(position, mirror)
    angle_value = folded.astype(jnp.float32) * (TWO_PI / period)
    cosine = jnp.where(4 * folded == period, 0.0, jnp.cos(angle_value))
    sine_part = jnp.where((folded == 0) | (2 * folded == period), 0.0, jnp.sin(angle_value))
    sine_part = jnp.where(position > mirror, -sine_part, sine_part)
    return (cosine, -sine_part)


def first_section(table_re, table_im, data):
    real_out = jnp.einsum("ka,abc->kbc", table_re, data, preferred_element_type=jnp.float32)
    imag_out = jnp.einsum("ka,abc->kbc", table_im, data, preferred_element_type=jnp.float32)
    return (real_out.astype(jnp.bfloat16), imag_out.astype(jnp.bfloat16))


def rotate(turn_re, turn_im, data_re, data_im):
    plain_re = data_re.astype(jnp.float32)
    plain_im = data_im.astype(jnp.float32)
    real_out = turn_re[:, :, None] * plain_re - turn_im[:, :, None] * plain_im
    imag_out = turn_re[:, :, None] * plain_im + turn_im[:, :, None] * plain_re
    return (real_out.astype(jnp.bfloat16), imag_out.astype(jnp.bfloat16))


def mix_rows(form, table_re, table_im, data_re, data_im):

    def product_of(left, right):
        return jnp.einsum(form, left, right, preferred_element_type=jnp.float32)

    real_out = product_of(table_re, data_re) - product_of(table_im, data_im)
    imag_out = product_of(table_re, data_im) + product_of(table_im, data_re)
    return (real_out, imag_out)


def apply_filter(spec_re, spec_im, filt_re, filt_im):
    rows_count, inner_width, channels = spec_re.shape
    filters = filt_re.shape[2]
    grouped_shape = (rows_count, inner_width, filters, channels // filters)
    grouped_re = spec_re.reshape(grouped_shape)
    grouped_im = spec_im.reshape(grouped_shape)
    gain_re = filt_re[..., None]
    gain_im = filt_im[..., None]
    out_re = (grouped_re * gain_re - grouped_im * gain_im).reshape(spec_re.shape)
    out_im = (grouped_re * gain_im + grouped_im * gain_re).reshape(spec_re.shape)
    return (out_re.astype(jnp.bfloat16), out_im.astype(jnp.bfloat16))


def spectral_middle(parts, local_freq, inner_re, inner_im, freq_total):
    sig_re, sig_im, kern_re, kern_im = parts
    inner_ids = jnp.arange(BLOCK, dtype=jnp.int32)
    turn_re, turn_im = unit_pair(local_freq[:, None] * inner_ids[None, :] % freq_total, freq_total)
    turned_re, turned_im = rotate(turn_re, turn_im, sig_re, sig_im)
    kturn_re, kturn_im = rotate(turn_re, turn_im, kern_re, kern_im)
    spec_re, spec_im = mix_rows("qb,rbc->rqc", inner_re, inner_im, turned_re, turned_im)
    filt_re, filt_im = mix_rows("qb,rbc->rqc", inner_re, inner_im, kturn_re, kturn_im)
    weight_re, weight_im = apply_filter(spec_re, spec_im, filt_re, filt_im)
    back_re, back_im = mix_rows("bq,rqc->rbc", inner_re, -inner_im, weight_re, weight_im)
    return rotate(turn_re, -turn_im, back_re, back_im)


def block_columns(signal, kernel):
    return (
        lax.all_to_all(signal, "ctx", split_axis=1, concat_axis=0, tiled=True),
        lax.all_to_all(kernel, "ctx", split_axis=1, concat_axis=0, tiled=True),
    )


def token_rows(conv_vals):
    return lax.all_to_all(conv_vals, "ctx", split_axis=0, concat_axis=1, tiled=True)


def general_local(section_input, long_filter, short_filter, skip_gain):
    acts_local = section_input[0]
    tok_rows, chan_local = acts_local.shape
    filt_local = long_filter.shape[2]
    n_ctx = lax.axis_size("ctx")
    ctx_rank = lax.axis_index("ctx")
    blocks_local = tok_rows // BLOCK
    half_span = blocks_local * n_ctx
    full_span = 2 * half_span
    freq_total = full_span * BLOCK
    rows_local = full_span // n_ctx
    partial_squares = jnp.sum(acts_local * acts_local, axis=1)
    total_squares = lax.psum(partial_squares, "tp")
    normed = (acts_local * lax.rsqrt(total_squares / CHAN + 1e-06)[:, None]).astype(jnp.bfloat16)
    earlier = from_behind(normed[tok_rows - (TAPS - 1) :], "ctx", 1)
    extended = jnp.concatenate([earlier, normed], axis=0)
    taps_all = short_filter[0].astype(jnp.float32)
    featured = []
    for feature_id in range(3):
        running = jnp.zeros((tok_rows, chan_local), jnp.float32)
        for offset in range(TAPS):
            begin_row = TAPS - 1 - offset
            running = (
                running
                + taps_all[feature_id, offset][None, :] * extended[begin_row : begin_row + tok_rows]
            )
        featured.append(running)
    query = featured[0].astype(jnp.bfloat16)
    product = (featured[1] * featured[2]).astype(jnp.bfloat16)
    block_ids = jnp.arange(half_span, dtype=jnp.int32)
    inner_ids = jnp.arange(BLOCK, dtype=jnp.int32)
    inner_re, inner_im = unit_pair(inner_ids[:, None] * inner_ids[None, :] % BLOCK, BLOCK)
    inner_re = inner_re.astype(jnp.bfloat16)
    inner_im = inner_im.astype(jnp.bfloat16)
    signal = product.reshape(blocks_local, BLOCK, chan_local)
    kernel = long_filter[0].reshape(blocks_local, BLOCK, filt_local)
    signal_cols, kernel_cols = block_columns(signal, kernel)
    freq_rows = jnp.arange(full_span, dtype=jnp.int32)
    outer_re, outer_im = unit_pair(freq_rows[:, None] * block_ids[None, :] % full_span, full_span)
    table_re = outer_re.astype(jnp.bfloat16)
    table_im = outer_im.astype(jnp.bfloat16)
    sig_re, sig_im = first_section(table_re, table_im, signal_cols)
    kern_re, kern_im = first_section(table_re, table_im, kernel_cols)
    got = (
        lax.all_to_all(sig_re, "ctx", split_axis=0, concat_axis=1, tiled=True),
        lax.all_to_all(sig_im, "ctx", split_axis=0, concat_axis=1, tiled=True),
        lax.all_to_all(kern_re, "ctx", split_axis=0, concat_axis=1, tiled=True),
        lax.all_to_all(kern_im, "ctx", split_axis=0, concat_axis=1, tiled=True),
    )
    local_freq = ctx_rank * rows_local + jnp.arange(rows_local, dtype=jnp.int32)
    back_re, back_im = spectral_middle(got, local_freq, inner_re, inner_im, freq_total)
    gathered_re, gathered_im = (
        lax.all_to_all(back_re, "ctx", split_axis=1, concat_axis=0, tiled=True),
        lax.all_to_all(back_im, "ctx", split_axis=1, concat_axis=0, tiled=True),
    )
    conv_vals = jnp.einsum("ka,kbc->abc", table_re, gathered_re, preferred_element_type=jnp.float32)
    conv_vals = conv_vals + jnp.einsum(
        "ka,kbc->abc", table_im, gathered_im, preferred_element_type=jnp.float32
    )
    conv_vals = (conv_vals * (1.0 / freq_total)).astype(jnp.bfloat16)
    conv_tokens = token_rows(conv_vals).reshape(tok_rows, chan_local)
    finished = acts_local + query.astype(jnp.float32) * (
        conv_tokens.astype(jnp.float32) + skip_gain[0][None, :] * product.astype(jnp.float32)
    )
    received = passed_along(finished.astype(jnp.bfloat16), "section", 1).astype(finished.dtype)
    return received[None]


EXTRA = 16
LANES = 128


def odd_tables(length):
    phase = (2 * np.arange(length)[:, None] + 1) * np.arange(length)[None, :] % (4 * length)
    turn = phase * (2.0 * np.pi / (4 * length))
    ahead = np.concatenate([np.cos(turn), -np.sin(turn)], axis=0)
    return ahead.astype(ml_dtypes.bfloat16), (ahead.T / length).astype(ml_dtypes.bfloat16)


def spread_table(filters, channels):
    owner = np.arange(channels) // (channels // filters)
    return (np.arange(filters)[:, None] == owner[None, :]).astype(ml_dtypes.bfloat16)


def column_of(row):
    return jnp.transpose(jnp.broadcast_to(row, (LANES, row.shape[1])))


def three_terms(x):
    terms = []
    for _ in range(3):
        terms.append(x.astype(jnp.bfloat16).astype(jnp.float32))
        x = x - terms[-1]
    return terms


def next_place(rank, step, peers):
    return lax.rem(rank + step + peers, peers)


def cut_kernel(peers, x_hbm, filt_hbm, *refs):
    outs, (x_ref, filt_ref, turned, sems) = refs[:peers], refs[peers:]
    rank = lax.axis_index("ctx")
    rows, chans = x_hbm.shape
    width = chans // peers
    filters = filt_hbm.shape[1] // peers
    pieces = sems.shape[0] - 1
    depth = rows // pieces
    copies = [
        pltpu.make_async_copy(
            x_hbm.at[pl.ds(i * depth, depth)], x_ref.at[pl.ds(i * depth, depth)], sems.at[i]
        )
        for i in range(pieces)
    ]
    copies.append(pltpu.make_async_copy(filt_hbm, filt_ref, sems.at[pieces]))
    for copy in copies:
        copy.start()
    columns = []
    for i in range(pieces):
        copies[i].wait()
        here = pl.ds(i * depth, depth)
        total = jnp.zeros((depth, LANES), jnp.float32)
        for step in range(peers):
            target = next_place(rank, step, peers)
            part = x_ref[here, pl.ds(pl.multiple_of(target * width, width), width)]
            outs[step][here, :] = part.astype(jnp.bfloat16)
            for first in range(0, width, LANES):
                total = total + part[:, first : first + LANES] * part[:, first : first + LANES]
        columns.append(jnp.sum(total, axis=1, keepdims=True))
    column = jnp.concatenate(columns, axis=0)
    row = jnp.transpose(jnp.broadcast_to(column, (rows, LANES)))[:EXTRA, :]
    nth = lax.broadcasted_iota(jnp.int32, (EXTRA, rows), 0)
    terms = three_terms(row)
    sums = jnp.where(nth == 0, terms[0], jnp.where(nth == 1, terms[1], jnp.where(nth == 2, terms[2], 0.0)))
    sums = sums.astype(jnp.bfloat16)
    copies[pieces].wait()
    turned[...] = jnp.transpose(filt_ref[...].astype(jnp.float32)).astype(jnp.bfloat16)
    for step in range(peers):
        target = next_place(rank, step, peers)
        own = turned[pl.ds(pl.multiple_of(target * filters, filters), filters), :]
        extra = [sums] + [own[first : first + EXTRA] for first in range(0, filters, EXTRA)]
        if width > rows * len(extra):
            extra.append(jnp.zeros((EXTRA, width - rows * len(extra)), jnp.bfloat16))
        outs[step][rows:, :] = jnp.concatenate(extra, axis=1)


def table_kernel(pieces, after, *refs):
    count = (len(refs) - 1) // 2
    tables, outs, sems = refs[:count], refs[count : 2 * count], refs[2 * count]
    copies = []
    for t in range(count):
        depth = tables[t].shape[0] // pieces
        for i in range(pieces):
            here = pl.ds(i * depth, depth)
            copies.append(pltpu.make_async_copy(tables[t].at[here], outs[t].at[here], sems.at[len(copies)]))
    for copy in copies:
        copy.start()
    for copy in copies:
        copy.wait()


def filter_kernel(peers, *refs):
    blocks = refs[:peers]
    ahead_ref, spread_ref, filt_spec, spread_filter = refs[peers:]
    rank = lax.axis_index("ctx")
    rows = blocks[0].shape[0] - EXTRA
    filters = spread_ref.shape[0]
    for step in range(peers):
        begin = pl.multiple_of(next_place(rank, -step, peers) * rows, rows)
        parts = [blocks[step][rows:, i * rows : (i + 1) * rows] for i in range(1, 1 + filters // EXTRA)]
        spread_filter[pl.ds(begin, rows), :] = lax.dot_general(
            jnp.concatenate(parts, axis=0),
            spread_ref[...],
            (((0,), (0,)), ((), ())),
            preferred_element_type=jnp.float32,
        ).astype(jnp.bfloat16)
    filt_spec[...] = jnp.dot(ahead_ref[...], spread_filter[...], preferred_element_type=jnp.float32)


def layer_kernel(peers, *refs):
    blocks = refs[:peers]
    other_sums, taps_ref, skip_ref, ahead_ref, return_ref, filt_spec = refs[peers : peers + 6]
    outs = refs[peers + 6 : 2 * peers + 6]
    held, query, product, spec, weighted, conv = refs[2 * peers + 6 :]
    rank = lax.axis_index("ctx")
    rows = blocks[0].shape[0] - EXTRA
    width = blocks[0].shape[1]
    half = rows * peers
    chans = pl.ds(pl.multiple_of(rank * width, width), width)
    held[:8, :] = jnp.zeros((8, width), jnp.float32)
    for step in range(peers):
        begin = pl.multiple_of(next_place(rank, -step, peers) * rows, rows)
        here = blocks[step][rows:, :rows].astype(jnp.float32)
        there = other_sums[step * EXTRA : (step + 1) * EXTRA, :].astype(jnp.float32)
        square = jnp.sum(here, axis=0, keepdims=True) + jnp.sum(there, axis=0, keepdims=True)
        scale = column_of(lax.rsqrt(square * (1.0 / CHAN) + 1e-06))
        for first in range(0, width, LANES):
            lanes = slice(first, first + LANES)
            held[pl.ds(begin + 8, rows), lanes] = blocks[step][:rows, lanes].astype(jnp.float32) * scale
    taps = [[taps_ref[f, i : i + 1, chans].astype(jnp.float32) for i in range(TAPS)] for f in range(3)]
    for block in range(peers):
        begin = block * rows
        moved = [held[pl.ds(begin + 8 - i, rows), :] for i in range(TAPS)]
        features = []
        for feature in range(3):
            running = taps[feature][0] * moved[0]
            for i in range(1, TAPS):
                running = running + taps[feature][i] * moved[i]
            features.append(running)
        query[pl.ds(begin, rows), :] = features[0].astype(jnp.bfloat16)
        product[pl.ds(begin, rows), :] = (features[1] * features[2]).astype(jnp.bfloat16)
    spec[...] = jnp.dot(ahead_ref[...], product[...], preferred_element_type=jnp.float32)
    sig_re, sig_im = spec[:half, :], spec[half:, :]
    gain_re, gain_im = filt_spec[:half, :], filt_spec[half:, :]
    weighted[:half, :] = (sig_re * gain_re - sig_im * gain_im).astype(jnp.bfloat16)
    weighted[half:, :] = (sig_re * gain_im + sig_im * gain_re).astype(jnp.bfloat16)
    conv[...] = jnp.dot(return_ref[...], weighted[...], preferred_element_type=jnp.float32)
    skip = skip_ref[:, chans]
    for step in range(peers):
        tokens = pl.ds(pl.multiple_of(next_place(rank, step, peers) * rows, rows), rows)
        acts = blocks[(peers - step) % peers][:rows, :].astype(jnp.float32)
        gated = conv[tokens, :] + skip * product[tokens, :].astype(jnp.float32)
        outs[step][...] = (acts + query[tokens, :].astype(jnp.float32) * gated).astype(jnp.bfloat16)


def join_kernel(peers, *refs):
    parts, out_hbm, wide, sems = refs[:peers], refs[peers], refs[peers + 1], refs[peers + 2]
    width = parts[0].shape[1]
    rank = lax.axis_index("ctx")
    copies = []
    for step in range(peers):
        wide[step, :, :] = parts[step][...].astype(jnp.float32)
        chans = pl.ds(pl.multiple_of(next_place(rank, -step, peers) * width, width), width)
        copies.append(pltpu.make_async_copy(wide.at[step], out_hbm.at[:, chans], sems.at[step]))
        copies[-1].start()
    for copy in copies:
        copy.wait()


def on_device(kernel, args, outs, scratch=(), in_hbm=(), out_hbm=False, flops=0, limit=32):
    whole = pl.BlockSpec(memory_space=pltpu.VMEM)
    far = pl.BlockSpec(memory_space=pltpu.HBM)
    touched = sum(a.size * a.dtype.itemsize for a in (*args, *outs))
    args = [pltpu.with_memory_space_constraint(a, pltpu.HBM) if i in in_hbm else a for i, a in enumerate(args)]
    return pl.pallas_call(
        kernel,
        out_shape=outs,
        in_specs=[far if i in in_hbm else whole for i in range(len(args))],
        out_specs=[far if out_hbm else whole] * len(outs),
        scratch_shapes=list(scratch),
        compiler_params=pltpu.CompilerParams(vmem_limit_bytes=limit * 2**20),
        cost_estimate=pl.CostEstimate(flops=flops, bytes_accessed=touched, transcendentals=0),
    )(*args)


def hop(x, sections, peers, by_section, by_ctx):
    route = [
        (s * peers + c, (s + by_section) % sections * peers + (c + by_ctx) % peers)
        for s in range(sections)
        for c in range(peers)
    ]
    return lax.ppermute(x, ("section", "ctx"), route)


def channel_local(section_input, long_filter, short_filter, skip_gain):
    acts = section_input[0]
    rows, chans = acts.shape
    sections, peers = lax.axis_size("section"), lax.axis_size("ctx")
    width, filters = chans // peers, long_filter.shape[2] // peers
    half = rows * peers
    bf16, f32 = jnp.bfloat16, jnp.float32
    pieces = 4
    sent = on_device(
        functools.partial(cut_kernel, peers),
        [acts, long_filter[0]],
        [jax.ShapeDtypeStruct((rows + EXTRA, width), bf16)] * peers,
        [
            pltpu.VMEM((rows, chans), f32),
            pltpu.VMEM(long_filter.shape[1:], bf16),
            pltpu.VMEM((long_filter.shape[2], rows), bf16),
            pltpu.SemaphoreType.DMA((pieces + 1,)),
        ],
        in_hbm=(0, 1),
    )
    got = [sent[0]] + [None] * (peers - 1)
    far_first = sorted(range(1, peers), key=lambda k: abs(2 * k - peers))
    for k in far_first:
        got[k] = hop(sent[k], sections, peers, 0, k)
    tables = [jnp.asarray(t) for t in odd_tables(half)]
    ahead, back = on_device(
        functools.partial(table_kernel, pieces),
        [sent[0], *tables],
        [jax.ShapeDtypeStruct(t.shape, bf16) for t in tables],
        [pltpu.SemaphoreType.DMA((2 * pieces,))],
        in_hbm=(1, 2),
    )
    own_sums = jnp.concatenate([g[rows:, :rows] for g in got], axis=0)
    other_sums = lax.ppermute(own_sums, "tp", [(0, 1), (1, 0)])
    (filt_spec,) = on_device(
        functools.partial(filter_kernel, peers),
        [*got, ahead, jnp.asarray(spread_table(filters, width))],
        [jax.ShapeDtypeStruct((2 * half, width), f32)],
        [pltpu.VMEM((half, width), bf16)],
        flops=4 * half * half * width,
    )
    done = on_device(
        functools.partial(layer_kernel, peers),
        [*got, other_sums, short_filter[0], skip_gain, ahead, back, filt_spec],
        [jax.ShapeDtypeStruct((rows, width), bf16)] * peers,
        [
            pltpu.VMEM((half + 8, width), f32),
            pltpu.VMEM((half, width), bf16),
            pltpu.VMEM((half, width), bf16),
            pltpu.VMEM((2 * half, width), f32),
            pltpu.VMEM((2 * half, width), bf16),
            pltpu.VMEM((half, width), f32),
        ],
        flops=8 * half * half * width,
    )
    arrived = [None] * peers
    for k in [*far_first, 0]:
        arrived[k] = hop(done[k], sections, peers, 1, k)
    (received,) = on_device(
        functools.partial(join_kernel, peers),
        arrived,
        [jax.ShapeDtypeStruct((rows, chans), f32)],
        [pltpu.VMEM((peers, rows, width), f32), pltpu.SemaphoreType.DMA((peers,))],
        out_hbm=True,
    )
    return received[None]


def fits_channel_plan(mesh, section_input, long_filter):
    peers, cores = mesh.shape["ctx"], mesh.shape["tp"]
    tokens = section_input.shape[1]
    width = section_input.shape[2] // (peers * cores)
    filters = long_filter.shape[2] // (peers * cores)
    return (
        tokens == peers * LANES
        and tokens <= 1024
        and width % LANES == 0
        and filters % EXTRA == 0
        and (1 + filters // EXTRA) * LANES <= width
    )


def solution(mesh):
    in_specs = (
        P("section", "ctx", "tp"),
        P("section", "ctx", "tp"),
        P("section", None, None, "tp"),
        P("section", "tp"),
    )
    out_specs = P("section", "ctx", "tp")

    def layer(section_input, long_filter, short_filter, skip_gain):
        local = channel_local if fits_channel_plan(mesh, section_input, long_filter) else general_local
        mapped = jax.shard_map(local, mesh=mesh, in_specs=in_specs, out_specs=out_specs, check_vma=False)
        return mapped(section_input, long_filter, short_filter, skip_gain)

    return layer
```

```python
import functools

import jax
import jax.numpy as jnp
import ml_dtypes
import numpy as np
from jax import lax
from jax.experimental import pallas as pl
from jax.experimental.pallas import tpu as pltpu
from jax.sharding import PartitionSpec as P

CHAN = 4096
TAPS = 3
BLOCK = 128


TWO_PI = 6.283185307179586


def from_behind(block, axis, distance):
    devices = range(lax.axis_size(axis))
    route = [(i - distance, i) for i in devices if i - distance in devices]
    return lax.ppermute(block, axis, route)


def passed_along(x, axis, by):
    peers = lax.axis_size(axis)
    return lax.ppermute(x, axis, [(i, (i + by) % peers) for i in range(peers)])


def unit_pair(position, period):
    mirror = period - position
    folded = jnp.minimum(position, mirror)
    angle_value = folded.astype(jnp.float32) * (TWO_PI / period)
    cosine = jnp.where(4 * folded == period, 0.0, jnp.cos(angle_value))
    sine_part = jnp.where((folded == 0) | (2 * folded == period), 0.0, jnp.sin(angle_value))
    sine_part = jnp.where(position > mirror, -sine_part, sine_part)
    return (cosine, -sine_part)


def first_section(table_re, table_im, data):
    real_out = jnp.einsum("ka,abc->kbc", table_re, data, preferred_element_type=jnp.float32)
    imag_out = jnp.einsum("ka,abc->kbc", table_im, data, preferred_element_type=jnp.float32)
    return (real_out.astype(jnp.bfloat16), imag_out.astype(jnp.bfloat16))


def rotate(turn_re, turn_im, data_re, data_im):
    plain_re = data_re.astype(jnp.float32)
    plain_im = data_im.astype(jnp.float32)
    real_out = turn_re[:, :, None] * plain_re - turn_im[:, :, None] * plain_im
    imag_out = turn_re[:, :, None] * plain_im + turn_im[:, :, None] * plain_re
    return (real_out.astype(jnp.bfloat16), imag_out.astype(jnp.bfloat16))


def mix_rows(form, table_re, table_im, data_re, data_im):

    def product_of(left, right):
        return jnp.einsum(form, left, right, preferred_element_type=jnp.float32)

    real_out = product_of(table_re, data_re) - product_of(table_im, data_im)
    imag_out = product_of(table_re, data_im) + product_of(table_im, data_re)
    return (real_out, imag_out)


def apply_filter(spec_re, spec_im, filt_re, filt_im):
    rows_count, inner_width, channels = spec_re.shape
    filters = filt_re.shape[2]
    grouped_shape = (rows_count, inner_width, filters, channels // filters)
    grouped_re = spec_re.reshape(grouped_shape)
    grouped_im = spec_im.reshape(grouped_shape)
    gain_re = filt_re[..., None]
    gain_im = filt_im[..., None]
    out_re = (grouped_re * gain_re - grouped_im * gain_im).reshape(spec_re.shape)
    out_im = (grouped_re * gain_im + grouped_im * gain_re).reshape(spec_re.shape)
    return (out_re.astype(jnp.bfloat16), out_im.astype(jnp.bfloat16))


def spectral_middle(parts, local_freq, inner_re, inner_im, freq_total):
    sig_re, sig_im, kern_re, kern_im = parts
    inner_ids = jnp.arange(BLOCK, dtype=jnp.int32)
    turn_re, turn_im = unit_pair(local_freq[:, None] * inner_ids[None, :] % freq_total, freq_total)
    turned_re, turned_im = rotate(turn_re, turn_im, sig_re, sig_im)
    kturn_re, kturn_im = rotate(turn_re, turn_im, kern_re, kern_im)
    spec_re, spec_im = mix_rows("qb,rbc->rqc", inner_re, inner_im, turned_re, turned_im)
    filt_re, filt_im = mix_rows("qb,rbc->rqc", inner_re, inner_im, kturn_re, kturn_im)
    weight_re, weight_im = apply_filter(spec_re, spec_im, filt_re, filt_im)
    back_re, back_im = mix_rows("bq,rqc->rbc", inner_re, -inner_im, weight_re, weight_im)
    return rotate(turn_re, -turn_im, back_re, back_im)


def block_columns(signal, kernel):
    return (
        lax.all_to_all(signal, "ctx", split_axis=1, concat_axis=0, tiled=True),
        lax.all_to_all(kernel, "ctx", split_axis=1, concat_axis=0, tiled=True),
    )


def token_rows(conv_vals):
    return lax.all_to_all(conv_vals, "ctx", split_axis=0, concat_axis=1, tiled=True)


def general_local(section_input, long_filter, short_filter, skip_gain):
    acts_local = section_input[0]
    tok_rows, chan_local = acts_local.shape
    filt_local = long_filter.shape[2]
    n_ctx = lax.axis_size("ctx")
    ctx_rank = lax.axis_index("ctx")
    blocks_local = tok_rows // BLOCK
    half_span = blocks_local * n_ctx
    full_span = 2 * half_span
    freq_total = full_span * BLOCK
    rows_local = full_span // n_ctx
    partial_squares = jnp.sum(acts_local * acts_local, axis=1)
    total_squares = lax.psum(partial_squares, "tp")
    normed = (acts_local * lax.rsqrt(total_squares / CHAN + 1e-06)[:, None]).astype(jnp.bfloat16)
    earlier = from_behind(normed[tok_rows - (TAPS - 1) :], "ctx", 1)
    extended = jnp.concatenate([earlier, normed], axis=0)
    taps_all = short_filter[0].astype(jnp.float32)
    featured = []
    for feature_id in range(3):
        running = jnp.zeros((tok_rows, chan_local), jnp.float32)
        for offset in range(TAPS):
            begin_row = TAPS - 1 - offset
            running = (
                running
                + taps_all[feature_id, offset][None, :] * extended[begin_row : begin_row + tok_rows]
            )
        featured.append(running)
    query = featured[0].astype(jnp.bfloat16)
    product = (featured[1] * featured[2]).astype(jnp.bfloat16)
    block_ids = jnp.arange(half_span, dtype=jnp.int32)
    inner_ids = jnp.arange(BLOCK, dtype=jnp.int32)
    inner_re, inner_im = unit_pair(inner_ids[:, None] * inner_ids[None, :] % BLOCK, BLOCK)
    inner_re = inner_re.astype(jnp.bfloat16)
    inner_im = inner_im.astype(jnp.bfloat16)
    signal = product.reshape(blocks_local, BLOCK, chan_local)
    kernel = long_filter[0].reshape(blocks_local, BLOCK, filt_local)
    signal_cols, kernel_cols = block_columns(signal, kernel)
    freq_rows = jnp.arange(full_span, dtype=jnp.int32)
    outer_re, outer_im = unit_pair(freq_rows[:, None] * block_ids[None, :] % full_span, full_span)
    table_re = outer_re.astype(jnp.bfloat16)
    table_im = outer_im.astype(jnp.bfloat16)
    sig_re, sig_im = first_section(table_re, table_im, signal_cols)
    kern_re, kern_im = first_section(table_re, table_im, kernel_cols)
    got = (
        lax.all_to_all(sig_re, "ctx", split_axis=0, concat_axis=1, tiled=True),
        lax.all_to_all(sig_im, "ctx", split_axis=0, concat_axis=1, tiled=True),
        lax.all_to_all(kern_re, "ctx", split_axis=0, concat_axis=1, tiled=True),
        lax.all_to_all(kern_im, "ctx", split_axis=0, concat_axis=1, tiled=True),
    )
    local_freq = ctx_rank * rows_local + jnp.arange(rows_local, dtype=jnp.int32)
    back_re, back_im = spectral_middle(got, local_freq, inner_re, inner_im, freq_total)
    gathered_re, gathered_im = (
        lax.all_to_all(back_re, "ctx", split_axis=1, concat_axis=0, tiled=True),
        lax.all_to_all(back_im, "ctx", split_axis=1, concat_axis=0, tiled=True),
    )
    conv_vals = jnp.einsum("ka,kbc->abc", table_re, gathered_re, preferred_element_type=jnp.float32)
    conv_vals = conv_vals + jnp.einsum(
        "ka,kbc->abc", table_im, gathered_im, preferred_element_type=jnp.float32
    )
    conv_vals = (conv_vals * (1.0 / freq_total)).astype(jnp.bfloat16)
    conv_tokens = token_rows(conv_vals).reshape(tok_rows, chan_local)
    finished = acts_local + query.astype(jnp.float32) * (
        conv_tokens.astype(jnp.float32) + skip_gain[0][None, :] * product.astype(jnp.float32)
    )
    received = passed_along(finished.astype(jnp.bfloat16), "section", 1).astype(finished.dtype)
    return received[None]


EXTRA = 16
LANES = 128
DEPTH = 64


def odd_tables(length):
    ahead, back = [], []
    for first in range(2):
        phase = (2 * np.arange(length // 2)[:, None] + 1) * np.arange(first, length, 2)[None, :] % (4 * length)
        turn = phase * (2.0 * np.pi / (4 * length))
        ahead.append(np.concatenate([np.cos(turn), -np.sin(turn)], axis=0))
        back.append(ahead[-1].T / length)
    return [np.concatenate(parts, axis=0).astype(ml_dtypes.bfloat16) for parts in (ahead, back)]


def spread_table(filters, channels):
    owner = np.arange(channels) // (channels // filters)
    return (np.arange(filters)[:, None] == owner[None, :]).astype(ml_dtypes.bfloat16)


def column_of(row):
    return jnp.transpose(jnp.broadcast_to(row, (LANES, row.shape[1])))


def three_terms(x):
    terms = []
    for _ in range(3):
        terms.append(x.astype(jnp.bfloat16).astype(jnp.float32))
        x = x - terms[-1]
    return terms


def next_place(rank, step, peers):
    return lax.rem(rank + step + peers, peers)


def cut_kernel(peers, x_hbm, filt_hbm, *refs):
    outs, (x_ref, filt_ref, plain, turned, sems) = refs[:peers], refs[peers:]
    rank = lax.axis_index("ctx")
    rows, chans = x_hbm.shape
    part, width = rows // 2, chans // peers
    filters = filt_hbm.shape[1] // peers
    tiles = width // LANES
    copies = [pltpu.make_async_copy(filt_hbm, filt_ref, sems.at[peers * tiles])]
    for step in range(peers):
        begin = next_place(rank, step, peers) * width
        for tile in range(tiles):
            lanes = pl.ds(pl.multiple_of(begin + tile * LANES, LANES), LANES)
            at = step * tiles + tile
            copies.append(pltpu.make_async_copy(x_hbm.at[:, lanes], x_ref.at[at], sems.at[at]))
    for copy in copies:
        copy.start()
    copies[0].wait()
    for at in range(plain.shape[0]):
        lanes = slice(at * LANES, (at + 1) * LANES)
        plain[at] = filt_ref[:, lanes].astype(jnp.float32)
        halves = [plain[at, pl.ds(odd, part, stride=2), :] for odd in range(2)]
        turned[lanes, :] = jnp.transpose(jnp.concatenate(halves, axis=0)).astype(jnp.bfloat16)
    base = tiles * rows
    for step in range(peers):
        own = pl.ds(pl.multiple_of(next_place(rank, step, peers) * filters, filters), filters)
        outs[step][base : base + filters, :] = turned[own, :]
    totals = [jnp.zeros((part, LANES), jnp.float32)] * 2
    for step in range(peers):
        for tile in range(tiles):
            at = step * tiles + tile
            copies[1 + at].wait()
            for odd in range(2):
                acts = x_ref[at, pl.ds(odd, part, stride=2), :]
                top = tile * rows + odd * part
                outs[step][top : top + part, :] = acts.astype(jnp.bfloat16)
                totals[odd] = totals[odd] + acts * acts
    column = jnp.sum(jnp.concatenate(totals, axis=0), axis=1, keepdims=True)
    row = jnp.transpose(jnp.broadcast_to(column, (rows, LANES)))[:EXTRA, :]
    nth = lax.broadcasted_iota(jnp.int32, (EXTRA, rows), 0)
    terms = three_terms(row)
    sums = jnp.where(nth == 0, terms[0], jnp.where(nth == 1, terms[1], jnp.where(nth == 2, terms[2], 0.0)))
    for step in range(peers):
        outs[step][base + filters :, :] = sums.astype(jnp.bfloat16)


def table_kernel(pieces, after, *refs):
    count = (len(refs) - 1) // 2
    tables, outs, sems = refs[:count], refs[count : 2 * count], refs[2 * count]
    copies = []
    for t in range(count):
        depth = tables[t].shape[0] // pieces
        for i in range(pieces):
            here = pl.ds(i * depth, depth)
            copies.append(pltpu.make_async_copy(tables[t].at[here], outs[t].at[here], sems.at[len(copies)]))
    for copy in copies:
        copy.start()
    for copy in copies:
        copy.wait()


def filter_kernel(peers, *refs):
    blocks = refs[:peers]
    ahead_ref, spread_ref, filt_spec, even, odd = refs[peers:]
    rank = lax.axis_index("ctx")
    filters, width = spread_ref.shape
    rows = blocks[0].shape[1]
    part = rows // 2
    half = part * peers
    base = width // LANES * rows
    for step in range(peers):
        here = pl.ds(pl.multiple_of(next_place(rank, -step, peers) * part, part), part)
        spread = lax.dot_general(
            blocks[step][base : base + filters, :],
            spread_ref[...],
            (((0,), (0,)), ((), ())),
            preferred_element_type=jnp.float32,
        ).astype(jnp.bfloat16)
        even[here, :] = spread[:part]
        odd[here, :] = spread[part:]
    for im in range(2):
        here = slice(im * half, (im + 1) * half)
        there = slice((im + 2) * half, (im + 3) * half)
        of_even = jnp.dot(ahead_ref[here, :], even[...], preferred_element_type=jnp.float32)
        of_odd = jnp.dot(ahead_ref[there, :], odd[...], preferred_element_type=jnp.float32)
        filt_spec[here, :] = of_even + of_odd
        filt_spec[there, :] = of_odd - of_even if im else of_even - of_odd


def layer_kernel(peers, *refs):
    blocks = refs[:peers]
    other_sums, taps_ref, skip_ref, ahead_ref, return_ref, filt_spec = refs[peers : peers + 6]
    outs = refs[peers + 6 : 2 * peers + 6]
    held, query, product, spec, weighted, conv = refs[2 * peers + 6 :]
    rank = lax.axis_index("ctx")
    rows, width = outs[0].shape
    part, half = rows // 2, rows * peers // 2
    base = blocks[0].shape[0] - EXTRA
    chans = pl.ds(pl.multiple_of(rank * width, width), width)
    taps = [[taps_ref[f, i : i + 1, chans].astype(jnp.float32) for i in range(TAPS)] for f in range(3)]
    skip = skip_ref[:, chans]
    held[:, :8, :] = jnp.zeros((2, 8, width), jnp.float32)
    for step in range(peers):
        here = blocks[step][base:, :].astype(jnp.float32)
        there = other_sums[step * EXTRA : (step + 1) * EXTRA, :].astype(jnp.float32)
        square = jnp.sum(here, axis=0, keepdims=True) + jnp.sum(there, axis=0, keepdims=True)
        scale = column_of(lax.rsqrt(square * (1.0 / CHAN) + 1e-06))
        begin = pl.multiple_of(next_place(rank, -step, peers) * part, part) + 8
        for tile in range(width // LANES):
            lanes = slice(tile * LANES, (tile + 1) * LANES)
            for odd in range(2):
                acts = blocks[step][tile * rows + odd * part : tile * rows + (odd + 1) * part, :]
                scaled = acts.astype(jnp.float32) * scale[odd * part : (odd + 1) * part]
                held[odd, pl.ds(pl.multiple_of(begin, 8), part), lanes] = scaled
    for first in range(0, width, LANES):
        lanes = slice(first, first + LANES)
        near = [[jnp.broadcast_to(tap[:, lanes], (DEPTH, LANES)) for tap in feature] for feature in taps]
        for top in range(0, half, DEPTH):
            now = [held[odd, 8 + top : 8 + top + DEPTH, lanes] for odd in range(2)]
            last = [held[odd, 7 + top : 7 + top + DEPTH, lanes] for odd in range(2)]
            for odd, moved in ((0, (now[0], last[1], last[0])), (1, (now[1], now[0], last[1]))):
                features = []
                for feature in near:
                    running = feature[0] * moved[0]
                    for i in range(1, TAPS):
                        running = running + feature[i] * moved[i]
                    features.append(running)
                query[odd, top : top + DEPTH, lanes] = features[0].astype(jnp.bfloat16)
                product[odd, top : top + DEPTH, lanes] = (features[1] * features[2]).astype(jnp.bfloat16)
    for odd in range(2):
        table = ahead_ref[2 * odd * half : 2 * (odd + 1) * half, :]
        spec[odd] = jnp.dot(table, product[odd], preferred_element_type=jnp.float32)
    for first in range(0, width, LANES):
        lanes = slice(first, first + LANES)
        for top in range(0, half, DEPTH):
            re, im = slice(top, top + DEPTH), slice(half + top, half + top + DEPTH)
            far_re, far_im = (slice(2 * half + at.start, 2 * half + at.stop) for at in (re, im))
            even_re, even_im = spec[0, re, lanes], spec[0, im, lanes]
            odd_re, odd_im = spec[1, re, lanes], spec[1, im, lanes]
            near_out = product_of(even_re + odd_re, even_im + odd_im, filt_spec[re, lanes], filt_spec[im, lanes])
            far_out = product_of(
                even_re - odd_re, odd_im - even_im, filt_spec[far_re, lanes], filt_spec[far_im, lanes]
            )
            weighted[0, re, lanes] = (near_out[0] + far_out[0]).astype(jnp.bfloat16)
            weighted[0, im, lanes] = (near_out[1] - far_out[1]).astype(jnp.bfloat16)
            weighted[1, re, lanes] = (near_out[0] - far_out[0]).astype(jnp.bfloat16)
            weighted[1, im, lanes] = (near_out[1] + far_out[1]).astype(jnp.bfloat16)
    for odd in range(2):
        table = return_ref[odd * half : (odd + 1) * half, :]
        conv[odd] = jnp.dot(table, weighted[odd], preferred_element_type=jnp.float32)
    for step in range(peers):
        tokens = pl.ds(pl.multiple_of(next_place(rank, step, peers) * part, part), part)
        for tile in range(width // LANES):
            lanes = slice(tile * LANES, (tile + 1) * LANES)
            for odd in range(2):
                own = tile * rows + odd * part
                acts = blocks[(peers - step) % peers][own : own + part, :].astype(jnp.float32)
                gated = conv[odd, tokens, lanes] + skip[:, lanes] * product[odd, tokens, lanes].astype(jnp.float32)
                finished = acts + query[odd, tokens, lanes].astype(jnp.float32) * gated
                outs[step][odd * part : (odd + 1) * part, lanes] = finished.astype(jnp.bfloat16)


def product_of(left_re, left_im, right_re, right_im):
    return left_re * right_re - left_im * right_im, left_re * right_im + left_im * right_re


def join_kernel(peers, steps, *refs):
    parts, (out_hbm, wide, sems) = refs[: len(steps)], refs[-3:]
    rows, width = parts[0].shape
    rank = lax.axis_index("ctx")
    tiles = width // LANES
    copies = []
    for i, step in enumerate(steps):
        begin = next_place(rank, -step, peers) * width
        for tile in range(tiles):
            at = i * tiles + tile
            for odd in range(2):
                part = parts[i][odd * (rows // 2) : (odd + 1) * (rows // 2), tile * LANES : (tile + 1) * LANES]
                wide[at, pl.ds(odd, rows // 2, stride=2), :] = part.astype(jnp.float32)
            lanes = pl.ds(pl.multiple_of(begin + tile * LANES, LANES), LANES)
            copies.append(pltpu.make_async_copy(wide.at[at], out_hbm.at[:, lanes], sems.at[at]))
            copies[-1].start()
    for copy in copies:
        copy.wait()


def on_device(kernel, args, outs, scratch=(), in_hbm=(), out_hbm=False, flops=0, limit=32, aliases=None):
    whole = pl.BlockSpec(memory_space=pltpu.VMEM)
    far = pl.BlockSpec(memory_space=pltpu.HBM)
    touched = sum(a.size * a.dtype.itemsize for a in (*args, *outs))
    args = [pltpu.with_memory_space_constraint(a, pltpu.HBM) if i in in_hbm else a for i, a in enumerate(args)]
    return pl.pallas_call(
        kernel,
        out_shape=outs,
        in_specs=[far if i in in_hbm else whole for i in range(len(args))],
        out_specs=[far if out_hbm else whole] * len(outs),
        scratch_shapes=list(scratch),
        input_output_aliases=aliases or {},
        compiler_params=pltpu.CompilerParams(vmem_limit_bytes=limit * 2**20),
        cost_estimate=pl.CostEstimate(flops=flops, bytes_accessed=touched, transcendentals=0),
    )(*args)


def hop(x, sections, peers, by_section, by_ctx):
    route = [
        (s * peers + c, (s + by_section) % sections * peers + (c + by_ctx) % peers)
        for s in range(sections)
        for c in range(peers)
    ]
    return lax.ppermute(x, ("section", "ctx"), route)


def channel_local(section_input, long_filter, short_filter, skip_gain):
    acts = section_input[0]
    rows, chans = acts.shape
    sections, peers = lax.axis_size("section"), lax.axis_size("ctx")
    width, filters = chans // peers, long_filter.shape[2] // peers
    length = rows * peers
    half = length // 2
    bf16, f32 = jnp.bfloat16, jnp.float32
    pieces = 4
    base = width // LANES * rows + filters
    sent = on_device(
        functools.partial(cut_kernel, peers),
        [acts, long_filter[0]],
        [jax.ShapeDtypeStruct((base + EXTRA, rows), bf16)] * peers,
        [
            pltpu.VMEM((chans // LANES, rows, LANES), f32),
            pltpu.VMEM(long_filter.shape[1:], bf16),
            pltpu.VMEM((long_filter.shape[2] // LANES, rows, LANES), f32),
            pltpu.VMEM((long_filter.shape[2], rows), bf16),
            pltpu.SemaphoreType.DMA((chans // LANES + 1,)),
        ],
        in_hbm=(0, 1),
    )
    got = [sent[0]] + [None] * (peers - 1)
    far_first = sorted(range(1, peers), key=lambda k: abs(2 * k - peers))
    for k in far_first:
        got[k] = hop(sent[k], sections, peers, 0, k)
    tables = [jnp.asarray(t) for t in odd_tables(length)]
    ahead, back = on_device(
        functools.partial(table_kernel, pieces),
        [sent[0], *tables],
        [jax.ShapeDtypeStruct(t.shape, bf16) for t in tables],
        [pltpu.SemaphoreType.DMA((2 * pieces,))],
        in_hbm=(1, 2),
    )
    own_sums = jnp.concatenate([g[base:] for g in got], axis=0)
    other_sums = lax.ppermute(own_sums, "tp", [(0, 1), (1, 0)])
    (filt_spec,) = on_device(
        functools.partial(filter_kernel, peers),
        [*got, ahead, jnp.asarray(spread_table(filters, width))],
        [jax.ShapeDtypeStruct((2 * length, width), f32)],
        [pltpu.VMEM((half, width), bf16)] * 2,
        flops=2 * length * length * width,
    )
    done = on_device(
        functools.partial(layer_kernel, peers),
        [*got, other_sums, short_filter[0], skip_gain, ahead, back, filt_spec],
        [jax.ShapeDtypeStruct((rows, width), bf16)] * peers,
        [
            pltpu.VMEM((2, half + 8, width), f32),
            pltpu.VMEM((2, half, width), bf16),
            pltpu.VMEM((2, half, width), bf16),
            pltpu.VMEM((2, length, width), f32),
            pltpu.VMEM((2, length, width), bf16),
            pltpu.VMEM((2, half, width), f32),
        ],
        flops=4 * length * length * width,
    )
    arrived = [None] * peers
    for k in [*far_first, 0]:
        arrived[k] = hop(done[k], sections, peers, 1, k)
    out = jax.ShapeDtypeStruct((rows, chans), f32)
    tiles = width // LANES

    def staging(count):
        return [pltpu.VMEM((count * tiles, rows, LANES), f32), pltpu.SemaphoreType.DMA((count * tiles,))]

    (received,) = on_device(
        functools.partial(join_kernel, peers, far_first),
        [arrived[k] for k in far_first],
        [out],
        staging(len(far_first)),
        out_hbm=True,
    )
    (received,) = on_device(
        functools.partial(join_kernel, peers, [0]),
        [arrived[0], received],
        [out],
        staging(1),
        in_hbm=(1,),
        out_hbm=True,
        aliases={1: 0},
    )
    return received[None]


def fits_channel_plan(mesh, section_input, long_filter):
    peers, cores = mesh.shape["ctx"], mesh.shape["tp"]
    tokens = section_input.shape[1]
    width = section_input.shape[2] // (peers * cores)
    filters = long_filter.shape[2] // (peers * cores)
    return (
        tokens == peers * LANES
        and tokens <= 1024
        and width % LANES == 0
        and filters % EXTRA == 0
        and long_filter.shape[2] // cores % LANES == 0
    )


def solution(mesh):
    in_specs = (
        P("section", "ctx", "tp"),
        P("section", "ctx", "tp"),
        P("section", None, None, "tp"),
        P("section", "tp"),
    )
    out_specs = P("section", "ctx", "tp")

    def layer(section_input, long_filter, short_filter, skip_gain):
        local = channel_local if fits_channel_plan(mesh, section_input, long_filter) else general_local
        mapped = jax.shard_map(local, mesh=mesh, in_specs=in_specs, out_specs=out_specs, check_vma=False)
        return mapped(section_input, long_filter, short_filter, skip_gain)

    return layer
```

```python
import functools

import jax
import jax.numpy as jnp
import ml_dtypes
import numpy as np
from jax import lax
from jax.experimental import pallas as pl
from jax.experimental.pallas import tpu as pltpu
from jax.sharding import PartitionSpec as P

CHAN = 4096
TAPS = 3
BLOCK = 128


TWO_PI = 6.283185307179586


def from_behind(block, axis, distance):
    devices = range(lax.axis_size(axis))
    route = [(i - distance, i) for i in devices if i - distance in devices]
    return lax.ppermute(block, axis, route)


def passed_along(x, axis, by):
    peers = lax.axis_size(axis)
    return lax.ppermute(x, axis, [(i, (i + by) % peers) for i in range(peers)])


def unit_pair(position, period):
    mirror = period - position
    folded = jnp.minimum(position, mirror)
    angle_value = folded.astype(jnp.float32) * (TWO_PI / period)
    cosine = jnp.where(4 * folded == period, 0.0, jnp.cos(angle_value))
    sine_part = jnp.where((folded == 0) | (2 * folded == period), 0.0, jnp.sin(angle_value))
    sine_part = jnp.where(position > mirror, -sine_part, sine_part)
    return (cosine, -sine_part)


def first_section(table_re, table_im, data):
    real_out = jnp.einsum("ka,abc->kbc", table_re, data, preferred_element_type=jnp.float32)
    imag_out = jnp.einsum("ka,abc->kbc", table_im, data, preferred_element_type=jnp.float32)
    return (real_out.astype(jnp.bfloat16), imag_out.astype(jnp.bfloat16))


def rotate(turn_re, turn_im, data_re, data_im):
    plain_re = data_re.astype(jnp.float32)
    plain_im = data_im.astype(jnp.float32)
    real_out = turn_re[:, :, None] * plain_re - turn_im[:, :, None] * plain_im
    imag_out = turn_re[:, :, None] * plain_im + turn_im[:, :, None] * plain_re
    return (real_out.astype(jnp.bfloat16), imag_out.astype(jnp.bfloat16))


def mix_rows(form, table_re, table_im, data_re, data_im):

    def product_of(left, right):
        return jnp.einsum(form, left, right, preferred_element_type=jnp.float32)

    real_out = product_of(table_re, data_re) - product_of(table_im, data_im)
    imag_out = product_of(table_re, data_im) + product_of(table_im, data_re)
    return (real_out, imag_out)


def apply_filter(spec_re, spec_im, filt_re, filt_im):
    rows_count, inner_width, channels = spec_re.shape
    filters = filt_re.shape[2]
    grouped_shape = (rows_count, inner_width, filters, channels // filters)
    grouped_re = spec_re.reshape(grouped_shape)
    grouped_im = spec_im.reshape(grouped_shape)
    gain_re = filt_re[..., None]
    gain_im = filt_im[..., None]
    out_re = (grouped_re * gain_re - grouped_im * gain_im).reshape(spec_re.shape)
    out_im = (grouped_re * gain_im + grouped_im * gain_re).reshape(spec_re.shape)
    return (out_re.astype(jnp.bfloat16), out_im.astype(jnp.bfloat16))


def spectral_middle(parts, local_freq, inner_re, inner_im, freq_total):
    sig_re, sig_im, kern_re, kern_im = parts
    inner_ids = jnp.arange(BLOCK, dtype=jnp.int32)
    turn_re, turn_im = unit_pair(local_freq[:, None] * inner_ids[None, :] % freq_total, freq_total)
    turned_re, turned_im = rotate(turn_re, turn_im, sig_re, sig_im)
    kturn_re, kturn_im = rotate(turn_re, turn_im, kern_re, kern_im)
    spec_re, spec_im = mix_rows("qb,rbc->rqc", inner_re, inner_im, turned_re, turned_im)
    filt_re, filt_im = mix_rows("qb,rbc->rqc", inner_re, inner_im, kturn_re, kturn_im)
    weight_re, weight_im = apply_filter(spec_re, spec_im, filt_re, filt_im)
    back_re, back_im = mix_rows("bq,rqc->rbc", inner_re, -inner_im, weight_re, weight_im)
    return rotate(turn_re, -turn_im, back_re, back_im)


def block_columns(signal, kernel):
    return (
        lax.all_to_all(signal, "ctx", split_axis=1, concat_axis=0, tiled=True),
        lax.all_to_all(kernel, "ctx", split_axis=1, concat_axis=0, tiled=True),
    )


def token_rows(conv_vals):
    return lax.all_to_all(conv_vals, "ctx", split_axis=0, concat_axis=1, tiled=True)


def general_local(section_input, long_filter, short_filter, skip_gain):
    acts_local = section_input[0]
    tok_rows, chan_local = acts_local.shape
    filt_local = long_filter.shape[2]
    n_ctx = lax.axis_size("ctx")
    ctx_rank = lax.axis_index("ctx")
    blocks_local = tok_rows // BLOCK
    half_span = blocks_local * n_ctx
    full_span = 2 * half_span
    freq_total = full_span * BLOCK
    rows_local = full_span // n_ctx
    partial_squares = jnp.sum(acts_local * acts_local, axis=1)
    total_squares = lax.psum(partial_squares, "tp")
    normed = (acts_local * lax.rsqrt(total_squares / CHAN + 1e-06)[:, None]).astype(jnp.bfloat16)
    earlier = from_behind(normed[tok_rows - (TAPS - 1) :], "ctx", 1)
    extended = jnp.concatenate([earlier, normed], axis=0)
    taps_all = short_filter[0].astype(jnp.float32)
    featured = []
    for feature_id in range(3):
        running = jnp.zeros((tok_rows, chan_local), jnp.float32)
        for offset in range(TAPS):
            begin_row = TAPS - 1 - offset
            running = (
                running
                + taps_all[feature_id, offset][None, :] * extended[begin_row : begin_row + tok_rows]
            )
        featured.append(running)
    query = featured[0].astype(jnp.bfloat16)
    product = (featured[1] * featured[2]).astype(jnp.bfloat16)
    block_ids = jnp.arange(half_span, dtype=jnp.int32)
    inner_ids = jnp.arange(BLOCK, dtype=jnp.int32)
    inner_re, inner_im = unit_pair(inner_ids[:, None] * inner_ids[None, :] % BLOCK, BLOCK)
    inner_re = inner_re.astype(jnp.bfloat16)
    inner_im = inner_im.astype(jnp.bfloat16)
    signal = product.reshape(blocks_local, BLOCK, chan_local)
    kernel = long_filter[0].reshape(blocks_local, BLOCK, filt_local)
    signal_cols, kernel_cols = block_columns(signal, kernel)
    freq_rows = jnp.arange(full_span, dtype=jnp.int32)
    outer_re, outer_im = unit_pair(freq_rows[:, None] * block_ids[None, :] % full_span, full_span)
    table_re = outer_re.astype(jnp.bfloat16)
    table_im = outer_im.astype(jnp.bfloat16)
    sig_re, sig_im = first_section(table_re, table_im, signal_cols)
    kern_re, kern_im = first_section(table_re, table_im, kernel_cols)
    got = (
        lax.all_to_all(sig_re, "ctx", split_axis=0, concat_axis=1, tiled=True),
        lax.all_to_all(sig_im, "ctx", split_axis=0, concat_axis=1, tiled=True),
        lax.all_to_all(kern_re, "ctx", split_axis=0, concat_axis=1, tiled=True),
        lax.all_to_all(kern_im, "ctx", split_axis=0, concat_axis=1, tiled=True),
    )
    local_freq = ctx_rank * rows_local + jnp.arange(rows_local, dtype=jnp.int32)
    back_re, back_im = spectral_middle(got, local_freq, inner_re, inner_im, freq_total)
    gathered_re, gathered_im = (
        lax.all_to_all(back_re, "ctx", split_axis=1, concat_axis=0, tiled=True),
        lax.all_to_all(back_im, "ctx", split_axis=1, concat_axis=0, tiled=True),
    )
    conv_vals = jnp.einsum("ka,kbc->abc", table_re, gathered_re, preferred_element_type=jnp.float32)
    conv_vals = conv_vals + jnp.einsum(
        "ka,kbc->abc", table_im, gathered_im, preferred_element_type=jnp.float32
    )
    conv_vals = (conv_vals * (1.0 / freq_total)).astype(jnp.bfloat16)
    conv_tokens = token_rows(conv_vals).reshape(tok_rows, chan_local)
    finished = acts_local + query.astype(jnp.float32) * (
        conv_tokens.astype(jnp.float32) + skip_gain[0][None, :] * product.astype(jnp.float32)
    )
    received = passed_along(finished.astype(jnp.bfloat16), "section", 1).astype(finished.dtype)
    return received[None]


EXTRA = 16
LANES = 128
DEPTH = 64


def odd_tables(length):
    ahead, back = [], []
    for first in range(2):
        phase = (2 * np.arange(length // 2)[:, None] + 1) * np.arange(first, length, 2)[None, :] % (4 * length)
        turn = phase * (2.0 * np.pi / (4 * length))
        ahead.append(np.concatenate([np.cos(turn), -np.sin(turn)], axis=0))
        back.append(ahead[-1].T / length)
    return [np.concatenate(parts, axis=0).astype(ml_dtypes.bfloat16) for parts in (ahead, back)]


def spread_table(filters, channels):
    owner = np.arange(channels) // (channels // filters)
    return (np.arange(filters)[:, None] == owner[None, :]).astype(ml_dtypes.bfloat16)


def column_of(row):
    return jnp.transpose(jnp.broadcast_to(row, (LANES, row.shape[1])))


def three_terms(x):
    terms = []
    for _ in range(3):
        terms.append(x.astype(jnp.bfloat16).astype(jnp.float32))
        x = x - terms[-1]
    return terms


def next_place(rank, step, peers):
    return lax.rem(rank + step + peers, peers)


def cut_kernel(peers, x_hbm, filt_hbm, *refs):
    outs, (sums_ref, x_ref, filt_ref, plain, turned, sems) = refs[:peers], refs[peers:]
    rank = lax.axis_index("ctx")
    rows, chans = x_hbm.shape
    part, width = rows // 2, chans // peers
    filters = filt_hbm.shape[1] // peers
    tiles = width // LANES
    copies = [pltpu.make_async_copy(filt_hbm, filt_ref, sems.at[peers * tiles])]
    for step in range(peers):
        begin = next_place(rank, step, peers) * width
        for tile in range(tiles):
            lanes = pl.ds(pl.multiple_of(begin + tile * LANES, LANES), LANES)
            at = step * tiles + tile
            copies.append(pltpu.make_async_copy(x_hbm.at[:, lanes], x_ref.at[at], sems.at[at]))
    for copy in copies:
        copy.start()
    copies[0].wait()
    for at in range(plain.shape[0]):
        lanes = slice(at * LANES, (at + 1) * LANES)
        plain[at] = filt_ref[:, lanes].astype(jnp.float32)
        halves = [plain[at, pl.ds(odd, part, stride=2), :] for odd in range(2)]
        turned[lanes, :] = jnp.transpose(jnp.concatenate(halves, axis=0)).astype(jnp.bfloat16)
    base = tiles * rows
    for step in range(peers):
        own = pl.ds(pl.multiple_of(next_place(rank, step, peers) * filters, filters), filters)
        outs[step][base : base + filters, :] = turned[own, :]
    totals = [jnp.zeros((part, LANES), jnp.float32)] * 2
    for step in range(peers):
        for tile in range(tiles):
            at = step * tiles + tile
            copies[1 + at].wait()
            for odd in range(2):
                acts = x_ref[at, pl.ds(odd, part, stride=2), :]
                top = tile * rows + odd * part
                outs[step][top : top + part, :] = acts.astype(jnp.bfloat16)
                totals[odd] = totals[odd] + acts * acts
    column = jnp.sum(jnp.concatenate(totals, axis=0), axis=1, keepdims=True)
    row = jnp.transpose(jnp.broadcast_to(column, (rows, LANES)))[:EXTRA, :]
    nth = lax.broadcasted_iota(jnp.int32, (EXTRA, rows), 0)
    terms = three_terms(row)
    sums = jnp.where(nth == 0, terms[0], jnp.where(nth == 1, terms[1], jnp.where(nth == 2, terms[2], 0.0)))
    sums_ref[...] = sums.astype(jnp.bfloat16)
    for step in range(peers):
        outs[step][base + filters :, :] = sums.astype(jnp.bfloat16)


def attach_kernel(count, *refs):
    messages, (own_ref, other_ref) = refs[:count], refs[count : count + 2]
    outs = refs[count + 2 :]
    both = own_ref[...].astype(jnp.float32) + pltpu.roll(other_ref[...].astype(jnp.float32), 3, 0)
    for out in outs:
        out[out.shape[0] - EXTRA :, :] = both.astype(jnp.bfloat16)


def table_kernel(pieces, after, *refs):
    count = (len(refs) - 1) // 2
    tables, outs, sems = refs[:count], refs[count : 2 * count], refs[2 * count]
    copies = []
    for t in range(count):
        parts = pieces if tables[t].shape[0] % (pieces * LANES) == 0 else 1
        depth = tables[t].shape[0] // parts
        for i in range(parts):
            here = pl.ds(i * depth, depth)
            copies.append(pltpu.make_async_copy(tables[t].at[here], outs[t].at[here], sems.at[len(copies)]))
    for copy in copies:
        copy.start()
    for copy in copies:
        copy.wait()


def scale_of(*sums):
    square = sum(jnp.sum(terms.astype(jnp.float32), axis=0, keepdims=True) for terms in sums)
    return column_of(lax.rsqrt(square * (1.0 / CHAN) + 1e-06))


def scale_block(block, scale, held):
    rows = block.shape[1]
    part = rows // 2
    for tile in range(held.shape[2] // LANES):
        for odd in range(2):
            own = tile * rows + odd * part
            acts = block[own : own + part, :].astype(jnp.float32) * scale[odd * part : (odd + 1) * part]
            held[odd, 8:, tile * LANES : (tile + 1) * LANES] = acts


def short_filters(held, depth, taps, lanes):
    now = [held[odd, 8 : 8 + depth, lanes] for odd in range(2)]
    last = [held[odd, 7 : 7 + depth, lanes] for odd in range(2)]
    results = []
    for moved in ((now[0], last[1], last[0]), (now[1], now[0], last[1])):
        features = []
        for feature in taps:
            running = feature[0][:, lanes] * moved[0]
            for i in range(1, TAPS):
                running = running + feature[i][:, lanes] * moved[i]
            features.append(running)
        results.append((features[0].astype(jnp.bfloat16), (features[1] * features[2]).astype(jnp.bfloat16)))
    return results


def read_taps(taps_ref, chans):
    return [[taps_ref[f, i : i + 1, chans].astype(jnp.float32) for i in range(TAPS)] for f in range(3)]


def spread_out(block, spread_ref):
    filters = spread_ref.shape[0]
    base = block.shape[0] - EXTRA - filters
    return lax.dot_general(
        block[base : base + filters, :],
        spread_ref[...],
        (((0,), (0,)), ((), ())),
        preferred_element_type=jnp.float32,
    ).astype(jnp.bfloat16)


def early_kernel(*refs):
    blocks, sums = refs[:2], (refs[2:4], refs[4:6])
    taps_ref, spread_ref, held, query, product, spread = refs[6:]
    width = held.shape[3]
    chans = pl.ds(pl.multiple_of(lax.axis_index("ctx") * width, width), width)
    taps = read_taps(taps_ref, chans)
    part = product.shape[2]
    for i in range(2):
        held[i, :, :8, :] = jnp.zeros((2, 8, width), jnp.float32)
        scale_block(blocks[i], scale_of(sums[i][0][...], sums[i][1][...]), held.at[i])
        for first in range(0, width, LANES):
            lanes = slice(first, first + LANES)
            for odd, results in enumerate(short_filters(held.at[i], part, taps, lanes)):
                query[i, odd, :, lanes], product[i, odd, :, lanes] = results
        spread[i] = spread_out(blocks[i], spread_ref)


def layer_kernel(peers, early, late, *refs):
    blocks = refs[:peers]
    taps_ref, skip_ref, ahead_ref, return_ref, spread_ref = refs[peers : peers + 5]
    early_held, early_query, early_product, early_spread = refs[peers + 5 : peers + 9]
    outs = refs[peers + 9 : 2 * peers + 9]
    held, top_held, query, product, spread, spec, filt_spec, weighted, conv = refs[2 * peers + 9 :]
    rank = lax.axis_index("ctx")
    rows, width = outs[0].shape
    part, half = rows // 2, rows * peers // 2
    top = top_held.shape[2] - 8
    chans = pl.ds(pl.multiple_of(rank * width, width), width)
    taps = read_taps(taps_ref, chans)
    skip = skip_ref[:, chans]
    places = [next_place(rank, -step, peers) for step in range(peers)]
    tokens = [pl.ds(pl.multiple_of(place * part, part), part) for place in places]
    tops = [pl.ds(pl.multiple_of(place * part, part), top) for place in places]

    for step in range(peers):
        both = early_spread[early.index(step)] if step in early else spread_out(blocks[step], spread_ref)
        for odd in range(2):
            spread[odd, tokens[step], :] = both[odd * part : (odd + 1) * part]
    for i, step in enumerate(late):
        scale_block(blocks[step], scale_of(blocks[step][blocks[step].shape[0] - EXTRA :, :]), held.at[i])
    for i, step in enumerate(early):
        top_held[i, :, 8:, :] = early_held[i, :, 8 : 8 + top, :]
    for step in range(peers):
        mine = held.at[late.index(step)] if step in late else top_held.at[early.index(step)]
        before = (step + 1) % peers
        theirs = held.at[late.index(before)] if before in late else early_held.at[early.index(before)]
        for odd in range(2):
            row = theirs[odd, 7 + part : 8 + part, :]
            mine[odd, 7:8, :] = jnp.where(places[step] > 0, row, 0.0)
    for i, step in enumerate(early):
        for odd in range(2):
            query[odd, tokens[step], :] = early_query[i, odd]
            product[odd, tokens[step], :] = early_product[i, odd]
    for first in range(0, width, LANES):
        lanes = slice(first, first + LANES)
        for step in range(peers):
            if step in late:
                source, depth, here = held.at[late.index(step)], part, tokens[step]
            else:
                source, depth, here = top_held.at[early.index(step)], top, tops[step]
            for odd, results in enumerate(short_filters(source, depth, taps, lanes)):
                query[odd, here, lanes], product[odd, here, lanes] = results
    for odd in range(2):
        table = ahead_ref[2 * odd * half : 2 * (odd + 1) * half, :]
        filt_spec[odd] = jnp.dot(table, spread[odd], preferred_element_type=jnp.float32)
        spec[odd] = jnp.dot(table, product[odd], preferred_element_type=jnp.float32)
    for first in range(0, width, LANES):
        lanes = slice(first, first + LANES)
        for begin in range(0, half, DEPTH):
            re, im = slice(begin, begin + DEPTH), slice(half + begin, half + begin + DEPTH)
            near, far = [], []
            for values in (spec, filt_spec):
                even_re, even_im = values[0, re, lanes], values[0, im, lanes]
                odd_re, odd_im = values[1, re, lanes], values[1, im, lanes]
                near += [even_re + odd_re, even_im + odd_im]
                far += [even_re - odd_re, odd_im - even_im]
            near_re, near_im = product_of(*near)
            far_re, far_im = product_of(*far)
            weighted[0, re, lanes] = (near_re + far_re).astype(jnp.bfloat16)
            weighted[0, im, lanes] = (near_im - far_im).astype(jnp.bfloat16)
            weighted[1, re, lanes] = (near_re - far_re).astype(jnp.bfloat16)
            weighted[1, im, lanes] = (near_im + far_im).astype(jnp.bfloat16)
    for odd in range(2):
        table = return_ref[odd * half : (odd + 1) * half, :]
        conv[odd] = jnp.dot(table, weighted[odd], preferred_element_type=jnp.float32)
    for step in range(peers):
        source = (peers - step) % peers
        here = tokens[source]
        for tile in range(width // LANES):
            lanes = slice(tile * LANES, (tile + 1) * LANES)
            for odd in range(2):
                own = tile * rows + odd * part
                acts = blocks[source][own : own + part, :].astype(jnp.float32)
                gated = conv[odd, here, lanes] + skip[:, lanes] * product[odd, here, lanes].astype(jnp.float32)
                finished = acts + query[odd, here, lanes].astype(jnp.float32) * gated
                outs[step][odd * part : (odd + 1) * part, lanes] = finished.astype(jnp.bfloat16)


def product_of(left_re, left_im, right_re, right_im):
    return left_re * right_re - left_im * right_im, left_re * right_im + left_im * right_re


def join_kernel(peers, steps, *refs):
    parts, (out_hbm, wide, sems) = refs[: len(steps)], refs[-3:]
    rows, width = parts[0].shape
    rank = lax.axis_index("ctx")
    tiles = width // LANES
    copies = []
    for i, step in enumerate(steps):
        begin = next_place(rank, -step, peers) * width
        for tile in range(tiles):
            at = i * tiles + tile
            for odd in range(2):
                part = parts[i][odd * (rows // 2) : (odd + 1) * (rows // 2), tile * LANES : (tile + 1) * LANES]
                wide[at, pl.ds(odd, rows // 2, stride=2), :] = part.astype(jnp.float32)
            lanes = pl.ds(pl.multiple_of(begin + tile * LANES, LANES), LANES)
            copies.append(pltpu.make_async_copy(wide.at[at], out_hbm.at[:, lanes], sems.at[at]))
            copies[-1].start()
    for copy in copies:
        copy.wait()


def on_device(kernel, args, outs, scratch=(), in_hbm=(), out_hbm=False, flops=0, limit=32, aliases=None):
    whole = pl.BlockSpec(memory_space=pltpu.VMEM)
    far = pl.BlockSpec(memory_space=pltpu.HBM)
    touched = sum(a.size * a.dtype.itemsize for a in (*args, *outs))
    args = [pltpu.with_memory_space_constraint(a, pltpu.HBM) if i in in_hbm else a for i, a in enumerate(args)]
    return pl.pallas_call(
        kernel,
        out_shape=outs,
        in_specs=[far if i in in_hbm else whole for i in range(len(args))],
        out_specs=[far if out_hbm else whole] * len(outs),
        scratch_shapes=list(scratch),
        input_output_aliases=aliases or {},
        compiler_params=pltpu.CompilerParams(vmem_limit_bytes=limit * 2**20),
        cost_estimate=pl.CostEstimate(flops=flops, bytes_accessed=touched, transcendentals=0),
    )(*args)


def hop(x, sections, peers, by_section, by_ctx):
    route = [
        (s * peers + c, (s + by_section) % sections * peers + (c + by_ctx) % peers)
        for s in range(sections)
        for c in range(peers)
    ]
    return lax.ppermute(x, ("section", "ctx"), route)


def channel_local(section_input, long_filter, short_filter, skip_gain):
    acts = section_input[0]
    rows, chans = acts.shape
    sections, peers = lax.axis_size("section"), lax.axis_size("ctx")
    width, filters = chans // peers, long_filter.shape[2] // peers
    length = rows * peers
    half = length // 2
    bf16, f32 = jnp.bfloat16, jnp.float32
    pieces = 4
    part, tail = rows // 2, width // LANES * rows + filters
    message = jax.ShapeDtypeStruct((tail + EXTRA, rows), bf16)
    *sent, own_sums = on_device(
        functools.partial(cut_kernel, peers),
        [acts, long_filter[0]],
        [message] * peers + [jax.ShapeDtypeStruct((EXTRA, rows), bf16)],
        [
            pltpu.VMEM((chans // LANES, rows, LANES), f32),
            pltpu.VMEM(long_filter.shape[1:], bf16),
            pltpu.VMEM((long_filter.shape[2] // LANES, rows, LANES), f32),
            pltpu.VMEM((long_filter.shape[2], rows), bf16),
            pltpu.SemaphoreType.DMA((chans // LANES + 1,)),
        ],
        in_hbm=(0, 1),
    )
    early, late = [0, 1], list(range(2, peers))
    got = [sent[0]] + [None] * (peers - 1)
    got[early[1]] = hop(sent[early[1]], sections, peers, 0, early[1])
    other_sums = lax.ppermute(own_sums, "tp", [(0, 1), (1, 0)])
    ready = on_device(
        functools.partial(attach_kernel, len(late)),
        [*(sent[k] for k in late), own_sums, other_sums],
        [message] * len(late),
        aliases={i: i for i in range(len(late))},
    )
    for k, x in zip(late, ready):
        got[k] = hop(x, sections, peers, 0, k)
    tables = [jnp.asarray(t) for t in (*odd_tables(length), spread_table(filters, width))]
    tables += [short_filter[0], skip_gain]
    ahead, back, spread, taps, skip = on_device(
        functools.partial(table_kernel, pieces),
        [other_sums, *tables],
        [jax.ShapeDtypeStruct(t.shape, t.dtype) for t in tables],
        [pltpu.SemaphoreType.DMA((pieces * len(tables),))],
        in_hbm=range(1, 1 + len(tables)),
    )
    far_sums = got[early[1]][tail:]
    far_other = lax.ppermute(far_sums, "tp", [(0, 1), (1, 0)])
    begun = on_device(
        early_kernel,
        [got[0], got[early[1]], own_sums, other_sums, far_sums, far_other, taps, spread],
        [
            jax.ShapeDtypeStruct((2, 2, part + 8, width), f32),
            jax.ShapeDtypeStruct((2, 2, part, width), bf16),
            jax.ShapeDtypeStruct((2, 2, part, width), bf16),
            jax.ShapeDtypeStruct((2, rows, width), bf16),
        ],
    )
    done = on_device(
        functools.partial(layer_kernel, peers, early, late),
        [*got, taps, skip, ahead, back, spread, *begun],
        [jax.ShapeDtypeStruct((rows, width), bf16)] * peers,
        [
            pltpu.VMEM((len(late), 2, part + 8, width), f32),
            pltpu.VMEM((2, 2, EXTRA + 8, width), f32),
            pltpu.VMEM((2, half, width), bf16),
            pltpu.VMEM((2, half, width), bf16),
            pltpu.VMEM((2, half, width), bf16),
            pltpu.VMEM((2, length, width), f32),
            pltpu.VMEM((2, length, width), f32),
            pltpu.VMEM((2, length, width), bf16),
            pltpu.VMEM((2, half, width), f32),
        ],
        flops=6 * length * length * width,
    )
    order = list(range(peers))
    arrived = {k: hop(done[k], sections, peers, 1, k) for k in order}
    out = jax.ShapeDtypeStruct((rows, chans), f32)
    tiles = width // LANES
    (received,) = on_device(
        functools.partial(join_kernel, peers, order),
        [arrived[k] for k in order],
        [out],
        [pltpu.VMEM((peers * tiles, rows, LANES), f32), pltpu.SemaphoreType.DMA((peers * tiles,))],
        out_hbm=True,
    )
    return received[None]


def fits_channel_plan(mesh, section_input, long_filter):
    peers, cores = mesh.shape["ctx"], mesh.shape["tp"]
    tokens = section_input.shape[1]
    width = section_input.shape[2] // (peers * cores)
    filters = long_filter.shape[2] // (peers * cores)
    return (
        peers > 2
        and tokens == peers * LANES
        and tokens <= 1024
        and width % LANES == 0
        and filters % EXTRA == 0
        and long_filter.shape[2] // cores % LANES == 0
    )


def solution(mesh):
    in_specs = (
        P("section", "ctx", "tp"),
        P("section", "ctx", "tp"),
        P("section", None, None, "tp"),
        P("section", "tp"),
    )
    out_specs = P("section", "ctx", "tp")

    def layer(section_input, long_filter, short_filter, skip_gain):
        local = channel_local if fits_channel_plan(mesh, section_input, long_filter) else general_local
        mapped = jax.shard_map(local, mesh=mesh, in_specs=in_specs, out_specs=out_specs, check_vma=False)
        return mapped(section_input, long_filter, short_filter, skip_gain)

    return layer
```

```python
import functools

import jax
import jax.numpy as jnp
import ml_dtypes
import numpy as np
from jax import lax
from jax.experimental import pallas as pl
from jax.experimental.pallas import tpu as pltpu
from jax.sharding import PartitionSpec as P

CHAN = 4096
TAPS = 3
BLOCK = 128


TWO_PI = 6.283185307179586


def from_behind(block, axis, distance):
    devices = range(lax.axis_size(axis))
    route = [(i - distance, i) for i in devices if i - distance in devices]
    return lax.ppermute(block, axis, route)


def passed_along(x, axis, by):
    peers = lax.axis_size(axis)
    return lax.ppermute(x, axis, [(i, (i + by) % peers) for i in range(peers)])


def unit_pair(position, period):
    mirror = period - position
    folded = jnp.minimum(position, mirror)
    angle_value = folded.astype(jnp.float32) * (TWO_PI / period)
    cosine = jnp.where(4 * folded == period, 0.0, jnp.cos(angle_value))
    sine_part = jnp.where((folded == 0) | (2 * folded == period), 0.0, jnp.sin(angle_value))
    sine_part = jnp.where(position > mirror, -sine_part, sine_part)
    return (cosine, -sine_part)


def first_section(table_re, table_im, data):
    real_out = jnp.einsum("ka,abc->kbc", table_re, data, preferred_element_type=jnp.float32)
    imag_out = jnp.einsum("ka,abc->kbc", table_im, data, preferred_element_type=jnp.float32)
    return (real_out.astype(jnp.bfloat16), imag_out.astype(jnp.bfloat16))


def rotate(turn_re, turn_im, data_re, data_im):
    plain_re = data_re.astype(jnp.float32)
    plain_im = data_im.astype(jnp.float32)
    real_out = turn_re[:, :, None] * plain_re - turn_im[:, :, None] * plain_im
    imag_out = turn_re[:, :, None] * plain_im + turn_im[:, :, None] * plain_re
    return (real_out.astype(jnp.bfloat16), imag_out.astype(jnp.bfloat16))


def mix_rows(form, table_re, table_im, data_re, data_im):

    def product_of(left, right):
        return jnp.einsum(form, left, right, preferred_element_type=jnp.float32)

    real_out = product_of(table_re, data_re) - product_of(table_im, data_im)
    imag_out = product_of(table_re, data_im) + product_of(table_im, data_re)
    return (real_out, imag_out)


def apply_filter(spec_re, spec_im, filt_re, filt_im):
    rows_count, inner_width, channels = spec_re.shape
    filters = filt_re.shape[2]
    grouped_shape = (rows_count, inner_width, filters, channels // filters)
    grouped_re = spec_re.reshape(grouped_shape)
    grouped_im = spec_im.reshape(grouped_shape)
    gain_re = filt_re[..., None]
    gain_im = filt_im[..., None]
    out_re = (grouped_re * gain_re - grouped_im * gain_im).reshape(spec_re.shape)
    out_im = (grouped_re * gain_im + grouped_im * gain_re).reshape(spec_re.shape)
    return (out_re.astype(jnp.bfloat16), out_im.astype(jnp.bfloat16))


def spectral_middle(parts, local_freq, inner_re, inner_im, freq_total):
    sig_re, sig_im, kern_re, kern_im = parts
    inner_ids = jnp.arange(BLOCK, dtype=jnp.int32)
    turn_re, turn_im = unit_pair(local_freq[:, None] * inner_ids[None, :] % freq_total, freq_total)
    turned_re, turned_im = rotate(turn_re, turn_im, sig_re, sig_im)
    kturn_re, kturn_im = rotate(turn_re, turn_im, kern_re, kern_im)
    spec_re, spec_im = mix_rows("qb,rbc->rqc", inner_re, inner_im, turned_re, turned_im)
    filt_re, filt_im = mix_rows("qb,rbc->rqc", inner_re, inner_im, kturn_re, kturn_im)
    weight_re, weight_im = apply_filter(spec_re, spec_im, filt_re, filt_im)
    back_re, back_im = mix_rows("bq,rqc->rbc", inner_re, -inner_im, weight_re, weight_im)
    return rotate(turn_re, -turn_im, back_re, back_im)


def block_columns(signal, kernel):
    return (
        lax.all_to_all(signal, "ctx", split_axis=1, concat_axis=0, tiled=True),
        lax.all_to_all(kernel, "ctx", split_axis=1, concat_axis=0, tiled=True),
    )


def token_rows(conv_vals):
    return lax.all_to_all(conv_vals, "ctx", split_axis=0, concat_axis=1, tiled=True)


def general_local(section_input, long_filter, short_filter, skip_gain):
    acts_local = section_input[0]
    tok_rows, chan_local = acts_local.shape
    filt_local = long_filter.shape[2]
    n_ctx = lax.axis_size("ctx")
    ctx_rank = lax.axis_index("ctx")
    blocks_local = tok_rows // BLOCK
    half_span = blocks_local * n_ctx
    full_span = 2 * half_span
    freq_total = full_span * BLOCK
    rows_local = full_span // n_ctx
    partial_squares = jnp.sum(acts_local * acts_local, axis=1)
    total_squares = lax.psum(partial_squares, "tp")
    normed = (acts_local * lax.rsqrt(total_squares / CHAN + 1e-06)[:, None]).astype(jnp.bfloat16)
    earlier = from_behind(normed[tok_rows - (TAPS - 1) :], "ctx", 1)
    extended = jnp.concatenate([earlier, normed], axis=0)
    taps_all = short_filter[0].astype(jnp.float32)
    featured = []
    for feature_id in range(3):
        running = jnp.zeros((tok_rows, chan_local), jnp.float32)
        for offset in range(TAPS):
            begin_row = TAPS - 1 - offset
            running = (
                running
                + taps_all[feature_id, offset][None, :] * extended[begin_row : begin_row + tok_rows]
            )
        featured.append(running)
    query = featured[0].astype(jnp.bfloat16)
    product = (featured[1] * featured[2]).astype(jnp.bfloat16)
    block_ids = jnp.arange(half_span, dtype=jnp.int32)
    inner_ids = jnp.arange(BLOCK, dtype=jnp.int32)
    inner_re, inner_im = unit_pair(inner_ids[:, None] * inner_ids[None, :] % BLOCK, BLOCK)
    inner_re = inner_re.astype(jnp.bfloat16)
    inner_im = inner_im.astype(jnp.bfloat16)
    signal = product.reshape(blocks_local, BLOCK, chan_local)
    kernel = long_filter[0].reshape(blocks_local, BLOCK, filt_local)
    signal_cols, kernel_cols = block_columns(signal, kernel)
    freq_rows = jnp.arange(full_span, dtype=jnp.int32)
    outer_re, outer_im = unit_pair(freq_rows[:, None] * block_ids[None, :] % full_span, full_span)
    table_re = outer_re.astype(jnp.bfloat16)
    table_im = outer_im.astype(jnp.bfloat16)
    sig_re, sig_im = first_section(table_re, table_im, signal_cols)
    kern_re, kern_im = first_section(table_re, table_im, kernel_cols)
    got = (
        lax.all_to_all(sig_re, "ctx", split_axis=0, concat_axis=1, tiled=True),
        lax.all_to_all(sig_im, "ctx", split_axis=0, concat_axis=1, tiled=True),
        lax.all_to_all(kern_re, "ctx", split_axis=0, concat_axis=1, tiled=True),
        lax.all_to_all(kern_im, "ctx", split_axis=0, concat_axis=1, tiled=True),
    )
    local_freq = ctx_rank * rows_local + jnp.arange(rows_local, dtype=jnp.int32)
    back_re, back_im = spectral_middle(got, local_freq, inner_re, inner_im, freq_total)
    gathered_re, gathered_im = (
        lax.all_to_all(back_re, "ctx", split_axis=1, concat_axis=0, tiled=True),
        lax.all_to_all(back_im, "ctx", split_axis=1, concat_axis=0, tiled=True),
    )
    conv_vals = jnp.einsum("ka,kbc->abc", table_re, gathered_re, preferred_element_type=jnp.float32)
    conv_vals = conv_vals + jnp.einsum(
        "ka,kbc->abc", table_im, gathered_im, preferred_element_type=jnp.float32
    )
    conv_vals = (conv_vals * (1.0 / freq_total)).astype(jnp.bfloat16)
    conv_tokens = token_rows(conv_vals).reshape(tok_rows, chan_local)
    finished = acts_local + query.astype(jnp.float32) * (
        conv_tokens.astype(jnp.float32) + skip_gain[0][None, :] * product.astype(jnp.float32)
    )
    received = passed_along(finished.astype(jnp.bfloat16), "section", 1).astype(finished.dtype)
    return received[None]


EXTRA = 16
LANES = 128
DEPTH = 64


def odd_tables(length):
    ahead, back = [], []
    for first in range(2):
        phase = (2 * np.arange(length // 2)[:, None] + 1) * np.arange(first, length, 2)[None, :] % (4 * length)
        turn = phase * (2.0 * np.pi / (4 * length))
        ahead.append(np.concatenate([np.cos(turn), -np.sin(turn)], axis=0))
        back.append(ahead[-1].T / length)
    return [np.concatenate(parts, axis=0).astype(ml_dtypes.bfloat16) for parts in (ahead, back)]


def spread_table(filters, channels):
    owner = np.arange(channels) // (channels // filters)
    return (np.arange(filters)[:, None] == owner[None, :]).astype(ml_dtypes.bfloat16)


def column_of(row):
    return jnp.transpose(jnp.broadcast_to(row, (LANES, row.shape[1])))


def three_terms(x):
    terms = []
    for _ in range(3):
        terms.append(x.astype(jnp.bfloat16).astype(jnp.float32))
        x = x - terms[-1]
    return terms


def next_place(rank, step, peers):
    return lax.rem(rank + step + peers, peers)


def cut_kernel(peers, x_hbm, filt_hbm, *refs):
    outs, (sums_ref, x_ref, filt_ref, plain, turned, sems) = refs[:peers], refs[peers:]
    rank = lax.axis_index("ctx")
    rows, chans = x_hbm.shape
    part, width = rows // 2, chans // peers
    filters = filt_hbm.shape[1] // peers
    tiles = width // LANES
    copies = [pltpu.make_async_copy(filt_hbm, filt_ref, sems.at[peers * tiles])]
    for step in range(peers):
        begin = next_place(rank, step, peers) * width
        for tile in range(tiles):
            lanes = pl.ds(pl.multiple_of(begin + tile * LANES, LANES), LANES)
            at = step * tiles + tile
            copies.append(pltpu.make_async_copy(x_hbm.at[:, lanes], x_ref.at[at], sems.at[at]))
    for copy in copies:
        copy.start()
    copies[0].wait()
    for at in range(plain.shape[0]):
        lanes = slice(at * LANES, (at + 1) * LANES)
        plain[at] = filt_ref[:, lanes].astype(jnp.float32)
        halves = [plain[at, pl.ds(odd, part, stride=2), :] for odd in range(2)]
        turned[lanes, :] = jnp.transpose(jnp.concatenate(halves, axis=0)).astype(jnp.bfloat16)
    base = tiles * rows
    for step in range(peers):
        own = pl.ds(pl.multiple_of(next_place(rank, step, peers) * filters, filters), filters)
        outs[step][base : base + filters, :] = turned[own, :]
    totals = [jnp.zeros((part, LANES), jnp.float32)] * 2
    for step in range(peers):
        for tile in range(tiles):
            at = step * tiles + tile
            copies[1 + at].wait()
            for odd in range(2):
                acts = x_ref[at, pl.ds(odd, part, stride=2), :]
                top = tile * rows + odd * part
                outs[step][top : top + part, :] = acts.astype(jnp.bfloat16)
                totals[odd] = totals[odd] + acts * acts
    column = jnp.sum(jnp.concatenate(totals, axis=0), axis=1, keepdims=True)
    row = jnp.transpose(jnp.broadcast_to(column, (rows, LANES)))[:EXTRA, :]
    nth = lax.broadcasted_iota(jnp.int32, (EXTRA, rows), 0)
    terms = three_terms(row)
    sums = jnp.where(nth == 0, terms[0], jnp.where(nth == 1, terms[1], jnp.where(nth == 2, terms[2], 0.0)))
    sums_ref[...] = sums.astype(jnp.bfloat16)
    for step in range(peers):
        outs[step][base + filters :, :] = sums.astype(jnp.bfloat16)


def attach_kernel(count, *refs):
    messages, (own_ref, other_ref) = refs[:count], refs[count : count + 2]
    outs = refs[count + 2 :]
    both = own_ref[...].astype(jnp.float32) + pltpu.roll(other_ref[...].astype(jnp.float32), 3, 0)
    for out in outs:
        out[out.shape[0] - EXTRA :, :] = both.astype(jnp.bfloat16)


def collect_kernel(count, *refs):
    out = refs[-1]
    for i in range(count):
        out[i * EXTRA : (i + 1) * EXTRA, :] = refs[i][refs[i].shape[0] - EXTRA :, :]


def table_kernel(pieces, after, *refs):
    count = (len(refs) - 1) // 2
    tables, outs, sems = refs[:count], refs[count : 2 * count], refs[2 * count]
    copies = []
    for t in range(count):
        parts = pieces if tables[t].shape[0] % (pieces * LANES) == 0 else 1
        depth = tables[t].shape[0] // parts
        for i in range(parts):
            here = pl.ds(i * depth, depth)
            copies.append(pltpu.make_async_copy(tables[t].at[here], outs[t].at[here], sems.at[len(copies)]))
    for copy in copies:
        copy.start()
    for copy in copies:
        copy.wait()


def scale_of(*sums):
    square = sum(jnp.sum(terms.astype(jnp.float32), axis=0, keepdims=True) for terms in sums)
    return column_of(lax.rsqrt(square * (1.0 / CHAN) + 1e-06))


def scale_block(block, scale, held):
    rows = block.shape[1]
    part = rows // 2
    for tile in range(held.shape[2] // LANES):
        for odd in range(2):
            own = tile * rows + odd * part
            acts = block[own : own + part, :].astype(jnp.float32) * scale[odd * part : (odd + 1) * part]
            held[odd, 8:, tile * LANES : (tile + 1) * LANES] = acts


def short_filters(held, depth, taps, lanes):
    now = [held[odd, 8 : 8 + depth, lanes] for odd in range(2)]
    last = [held[odd, 7 : 7 + depth, lanes] for odd in range(2)]
    results = []
    for moved in ((now[0], last[1], last[0]), (now[1], now[0], last[1])):
        features = []
        for feature in taps:
            running = feature[0][:, lanes] * moved[0]
            for i in range(1, TAPS):
                running = running + feature[i][:, lanes] * moved[i]
            features.append(running)
        results.append((features[0].astype(jnp.bfloat16), (features[1] * features[2]).astype(jnp.bfloat16)))
    return results


def read_taps(taps_ref, chans):
    return [[taps_ref[f, i : i + 1, chans].astype(jnp.float32) for i in range(TAPS)] for f in range(3)]


def spread_out(block, spread_ref):
    filters = spread_ref.shape[0]
    base = block.shape[0] - EXTRA - filters
    return lax.dot_general(
        block[base : base + filters, :],
        spread_ref[...],
        (((0,), (0,)), ((), ())),
        preferred_element_type=jnp.float32,
    ).astype(jnp.bfloat16)


def lead_in(held, before, inside):
    for odd in range(2):
        row = before[odd, before.shape[1] - 1 :, :]
        held[odd, 7:8, :] = jnp.where(inside, row, 0.0)


def early_kernel(peers, early, *refs):
    count = len(early)
    blocks, halves = refs[:count], refs[count : 3 * count]
    taps_ref, spread_ref, held, query, product, spread = refs[3 * count :]
    width, part = held.shape[3], held.shape[2] - 8
    rank = lax.axis_index("ctx")
    chans = pl.ds(pl.multiple_of(rank * width, width), width)
    taps = read_taps(taps_ref, chans)
    for i in range(count):
        held[i, :, :8, :] = jnp.zeros((2, 8, width), jnp.float32)
        scale_block(blocks[i], scale_of(halves[2 * i][...], halves[2 * i + 1][...]), held.at[i])
    for i, step in enumerate(early):
        before = (step + 1) % peers
        if before in early:
            lead_in(held.at[i], held.at[early.index(before)], next_place(rank, -step, peers) > 0)
    tokens = [pl.ds(pl.multiple_of(next_place(rank, -step, peers) * part, part), part) for step in early]
    for first in range(0, width, LANES):
        lanes = slice(first, first + LANES)
        for i in range(count):
            for odd, results in enumerate(short_filters(held.at[i], part, taps, lanes)):
                query[odd, tokens[i], lanes], product[odd, tokens[i], lanes] = results
    for i in range(count):
        both = spread_out(blocks[i], spread_ref)
        for odd in range(2):
            spread[odd, tokens[i], :] = both[odd * part : (odd + 1) * part]


def layer_kernel(peers, early, late, *refs):
    blocks = refs[:peers]
    taps_ref, skip_ref, ahead_ref, return_ref, spread_ref = refs[peers : peers + 5]
    early_held = refs[peers + 5]
    outs = refs[peers + 9 : 2 * peers + 9]
    query, product, spread, held, top_held, spec, filt_spec, weighted, conv = refs[2 * peers + 9 :]
    rank = lax.axis_index("ctx")
    rows, width = outs[0].shape
    part, half = rows // 2, rows * peers // 2
    top = top_held.shape[2] - 8
    chans = pl.ds(pl.multiple_of(rank * width, width), width)
    taps = read_taps(taps_ref, chans)
    skip = skip_ref[:, chans]
    places = [next_place(rank, -step, peers) for step in range(peers)]
    tokens = [pl.ds(pl.multiple_of(place * part, part), part) for place in places]
    tops = [pl.ds(pl.multiple_of(place * part, part), top) for place in places]

    for step in late:
        both = spread_out(blocks[step], spread_ref)
        for odd in range(2):
            spread[odd, tokens[step], :] = both[odd * part : (odd + 1) * part]
    for i, step in enumerate(late):
        scale_block(blocks[step], scale_of(blocks[step][blocks[step].shape[0] - EXTRA :, :]), held.at[i])
    sources = [(held.at[i], part, step) for i, step in enumerate(late)]
    lacking = [step for step in early if (step + 1) % peers in late]
    for i, step in enumerate(lacking):
        top_held[i, :, 8:, :] = early_held[early.index(step), :, 8 : 8 + top, :]
        sources.append((top_held.at[i], top, step))
    for source, _, step in sources:
        before = (step + 1) % peers
        theirs = held.at[late.index(before)] if before in late else early_held.at[early.index(before)]
        lead_in(source, theirs, places[step] > 0)
    for first in range(0, width, LANES):
        lanes = slice(first, first + LANES)
        for source, depth, step in sources:
            here = tokens[step] if depth == part else tops[step]
            for odd, results in enumerate(short_filters(source, depth, taps, lanes)):
                query[odd, here, lanes], product[odd, here, lanes] = results
    for odd in range(2):
        table = ahead_ref[2 * odd * half : 2 * (odd + 1) * half, :]
        filt_spec[odd] = jnp.dot(table, spread[odd], preferred_element_type=jnp.float32)
        spec[odd] = jnp.dot(table, product[odd], preferred_element_type=jnp.float32)
    for first in range(0, width, LANES):
        lanes = slice(first, first + LANES)
        for begin in range(0, half, DEPTH):
            re, im = slice(begin, begin + DEPTH), slice(half + begin, half + begin + DEPTH)
            near, far = [], []
            for values in (spec, filt_spec):
                even_re, even_im = values[0, re, lanes], values[0, im, lanes]
                odd_re, odd_im = values[1, re, lanes], values[1, im, lanes]
                near += [even_re + odd_re, even_im + odd_im]
                far += [even_re - odd_re, odd_im - even_im]
            near_re, near_im = product_of(*near)
            far_re, far_im = product_of(*far)
            weighted[0, re, lanes] = (near_re + far_re).astype(jnp.bfloat16)
            weighted[0, im, lanes] = (near_im - far_im).astype(jnp.bfloat16)
            weighted[1, re, lanes] = (near_re - far_re).astype(jnp.bfloat16)
            weighted[1, im, lanes] = (near_im + far_im).astype(jnp.bfloat16)
    for odd in range(2):
        table = return_ref[odd * half : (odd + 1) * half, :]
        conv[odd] = jnp.dot(table, weighted[odd], preferred_element_type=jnp.float32)
    for step in range(peers):
        source = (peers - step) % peers
        here = tokens[source]
        for tile in range(width // LANES):
            lanes = slice(tile * LANES, (tile + 1) * LANES)
            for odd in range(2):
                own = tile * rows + odd * part
                acts = blocks[source][own : own + part, :].astype(jnp.float32)
                gated = conv[odd, here, lanes] + skip[:, lanes] * product[odd, here, lanes].astype(jnp.float32)
                finished = acts + query[odd, here, lanes].astype(jnp.float32) * gated
                outs[step][odd * part : (odd + 1) * part, lanes] = finished.astype(jnp.bfloat16)


def product_of(left_re, left_im, right_re, right_im):
    return left_re * right_re - left_im * right_im, left_re * right_im + left_im * right_re


def join_kernel(peers, steps, *refs):
    parts, (out_hbm, wide, sems) = refs[: len(steps)], refs[-3:]
    rows, width = parts[0].shape
    rank = lax.axis_index("ctx")
    tiles = width // LANES
    copies = []
    for i, step in enumerate(steps):
        begin = next_place(rank, -step, peers) * width
        for tile in range(tiles):
            at = i * tiles + tile
            for odd in range(2):
                part = parts[i][odd * (rows // 2) : (odd + 1) * (rows // 2), tile * LANES : (tile + 1) * LANES]
                wide[at, pl.ds(odd, rows // 2, stride=2), :] = part.astype(jnp.float32)
            lanes = pl.ds(pl.multiple_of(begin + tile * LANES, LANES), LANES)
            copies.append(pltpu.make_async_copy(wide.at[at], out_hbm.at[:, lanes], sems.at[at]))
            copies[-1].start()
    for copy in copies:
        copy.wait()


def on_device(kernel, args, outs, scratch=(), in_hbm=(), out_hbm=False, flops=0, limit=32, aliases=None):
    whole = pl.BlockSpec(memory_space=pltpu.VMEM)
    far = pl.BlockSpec(memory_space=pltpu.HBM)
    touched = sum(a.size * a.dtype.itemsize for a in (*args, *outs))
    args = [pltpu.with_memory_space_constraint(a, pltpu.HBM) if i in in_hbm else a for i, a in enumerate(args)]
    return pl.pallas_call(
        kernel,
        out_shape=outs,
        in_specs=[far if i in in_hbm else whole for i in range(len(args))],
        out_specs=[far if out_hbm else whole] * len(outs),
        scratch_shapes=list(scratch),
        input_output_aliases=aliases or {},
        compiler_params=pltpu.CompilerParams(vmem_limit_bytes=limit * 2**20),
        cost_estimate=pl.CostEstimate(flops=flops, bytes_accessed=touched, transcendentals=0),
    )(*args)


def hop(x, sections, peers, by_section, by_ctx):
    route = [
        (s * peers + c, (s + by_section) % sections * peers + (c + by_ctx) % peers)
        for s in range(sections)
        for c in range(peers)
    ]
    return lax.ppermute(x, ("section", "ctx"), route)


def channel_local(section_input, long_filter, short_filter, skip_gain):
    acts = section_input[0]
    rows, chans = acts.shape
    sections, peers = lax.axis_size("section"), lax.axis_size("ctx")
    width, filters = chans // peers, long_filter.shape[2] // peers
    length = rows * peers
    half = length // 2
    bf16, f32 = jnp.bfloat16, jnp.float32
    pieces = 4
    part, tail = rows // 2, width // LANES * rows + filters
    message = jax.ShapeDtypeStruct((tail + EXTRA, rows), bf16)
    *sent, own_sums = on_device(
        functools.partial(cut_kernel, peers),
        [acts, long_filter[0]],
        [message] * peers + [jax.ShapeDtypeStruct((EXTRA, rows), bf16)],
        [
            pltpu.VMEM((chans // LANES, rows, LANES), f32),
            pltpu.VMEM(long_filter.shape[1:], bf16),
            pltpu.VMEM((long_filter.shape[2] // LANES, rows, LANES), f32),
            pltpu.VMEM((long_filter.shape[2], rows), bf16),
            pltpu.SemaphoreType.DMA((chans // LANES + 1,)),
        ],
        in_hbm=(0, 1),
    )
    early, late = [0, 1], list(range(peers - 1, 1, -1))
    got = {0: sent[0]}
    for k in early[1:]:
        got[k] = hop(sent[k], sections, peers, 0, k)
    other_sums = lax.ppermute(own_sums, "tp", [(0, 1), (1, 0)])
    ready = on_device(
        functools.partial(attach_kernel, len(late)),
        [*(sent[k] for k in late), own_sums, other_sums],
        [message] * len(late),
        aliases={i: i for i in range(len(late))},
    )
    for k, x in zip(late, ready):
        got[k] = hop(x, sections, peers, 0, k)
    tables = [jnp.asarray(t) for t in (*odd_tables(length), spread_table(filters, width))]
    tables += [short_filter[0], skip_gain]
    ahead, back, spread, taps, skip = on_device(
        functools.partial(table_kernel, pieces),
        [other_sums, *tables],
        [jax.ShapeDtypeStruct(t.shape, t.dtype) for t in tables],
        [pltpu.SemaphoreType.DMA((pieces * len(tables),))],
        in_hbm=range(1, 1 + len(tables)),
    )
    (halves,) = on_device(
        functools.partial(collect_kernel, len(early) - 1),
        [*(got[k] for k in early[1:]), ready[0]],
        [jax.ShapeDtypeStruct(((len(early) - 1) * EXTRA, rows), bf16)],
    )
    others = lax.ppermute(halves, "tp", [(0, 1), (1, 0)])
    pairs = [own_sums, other_sums]
    for i in range(len(early) - 1):
        pairs += [half_sums[i * EXTRA : (i + 1) * EXTRA] for half_sums in (halves, others)]
    begun = on_device(
        functools.partial(early_kernel, peers, early),
        [*(got[k] for k in early), *pairs, taps, spread],
        [
            jax.ShapeDtypeStruct((len(early), 2, part + 8, width), f32),
            *[jax.ShapeDtypeStruct((2, half, width), bf16)] * 3,
        ],
    )
    done = on_device(
        functools.partial(layer_kernel, peers, early, late),
        [*(got[k] for k in range(peers)), taps, skip, ahead, back, spread, *begun],
        [
            *[jax.ShapeDtypeStruct((rows, width), bf16)] * peers,
            *[jax.ShapeDtypeStruct((2, half, width), bf16)] * 3,
        ],
        [
            pltpu.VMEM((len(late), 2, part + 8, width), f32),
            pltpu.VMEM((2, 2, EXTRA + 8, width), f32),
            pltpu.VMEM((2, length, width), f32),
            pltpu.VMEM((2, length, width), f32),
            pltpu.VMEM((2, length, width), bf16),
            pltpu.VMEM((2, half, width), f32),
        ],
        flops=6 * length * length * width,
        aliases={peers + 6 + i: peers + i for i in range(3)},
    )
    order = sorted(range(peers), key=lambda k: (k % 2, k))
    arrived = {k: hop(done[k], sections, peers, 1, k) for k in order}
    out = jax.ShapeDtypeStruct((rows, chans), f32)
    tiles = width // LANES
    (received,) = on_device(
        functools.partial(join_kernel, peers, order),
        [arrived[k] for k in order],
        [out],
        [pltpu.VMEM((peers * tiles, rows, LANES), f32), pltpu.SemaphoreType.DMA((peers * tiles,))],
        out_hbm=True,
    )
    return received[None]


def fits_channel_plan(mesh, section_input, long_filter):
    peers, cores = mesh.shape["ctx"], mesh.shape["tp"]
    tokens = section_input.shape[1]
    width = section_input.shape[2] // (peers * cores)
    filters = long_filter.shape[2] // (peers * cores)
    return (
        peers > 2
        and tokens == peers * LANES
        and tokens <= 1024
        and width % LANES == 0
        and filters % EXTRA == 0
        and long_filter.shape[2] // cores % LANES == 0
    )


def solution(mesh):
    in_specs = (
        P("section", "ctx", "tp"),
        P("section", "ctx", "tp"),
        P("section", None, None, "tp"),
        P("section", "tp"),
    )
    out_specs = P("section", "ctx", "tp")

    def layer(section_input, long_filter, short_filter, skip_gain):
        local = channel_local if fits_channel_plan(mesh, section_input, long_filter) else general_local
        mapped = jax.shard_map(local, mesh=mesh, in_specs=in_specs, out_specs=out_specs, check_vma=False)
        return mapped(section_input, long_filter, short_filter, skip_gain)

    return layer
```

```python
import functools

import jax
import jax.numpy as jnp
import ml_dtypes
import numpy as np
from jax import lax
from jax.experimental import pallas as pl
from jax.experimental.pallas import tpu as pltpu
from jax.sharding import PartitionSpec as P

CHAN = 4096
TAPS = 3
BLOCK = 128


TWO_PI = 6.283185307179586


def from_behind(block, axis, distance):
    devices = range(lax.axis_size(axis))
    route = [(i - distance, i) for i in devices if i - distance in devices]
    return lax.ppermute(block, axis, route)


def passed_along(x, axis, by):
    peers = lax.axis_size(axis)
    return lax.ppermute(x, axis, [(i, (i + by) % peers) for i in range(peers)])


def unit_pair(position, period):
    mirror = period - position
    folded = jnp.minimum(position, mirror)
    angle_value = folded.astype(jnp.float32) * (TWO_PI / period)
    cosine = jnp.where(4 * folded == period, 0.0, jnp.cos(angle_value))
    sine_part = jnp.where((folded == 0) | (2 * folded == period), 0.0, jnp.sin(angle_value))
    sine_part = jnp.where(position > mirror, -sine_part, sine_part)
    return (cosine, -sine_part)


def first_section(table_re, table_im, data):
    real_out = jnp.einsum("ka,abc->kbc", table_re, data, preferred_element_type=jnp.float32)
    imag_out = jnp.einsum("ka,abc->kbc", table_im, data, preferred_element_type=jnp.float32)
    return (real_out.astype(jnp.bfloat16), imag_out.astype(jnp.bfloat16))


def rotate(turn_re, turn_im, data_re, data_im):
    plain_re = data_re.astype(jnp.float32)
    plain_im = data_im.astype(jnp.float32)
    real_out = turn_re[:, :, None] * plain_re - turn_im[:, :, None] * plain_im
    imag_out = turn_re[:, :, None] * plain_im + turn_im[:, :, None] * plain_re
    return (real_out.astype(jnp.bfloat16), imag_out.astype(jnp.bfloat16))


def mix_rows(form, table_re, table_im, data_re, data_im):

    def product_of(left, right):
        return jnp.einsum(form, left, right, preferred_element_type=jnp.float32)

    real_out = product_of(table_re, data_re) - product_of(table_im, data_im)
    imag_out = product_of(table_re, data_im) + product_of(table_im, data_re)
    return (real_out, imag_out)


def apply_filter(spec_re, spec_im, filt_re, filt_im):
    rows_count, inner_width, channels = spec_re.shape
    filters = filt_re.shape[2]
    grouped_shape = (rows_count, inner_width, filters, channels // filters)
    grouped_re = spec_re.reshape(grouped_shape)
    grouped_im = spec_im.reshape(grouped_shape)
    gain_re = filt_re[..., None]
    gain_im = filt_im[..., None]
    out_re = (grouped_re * gain_re - grouped_im * gain_im).reshape(spec_re.shape)
    out_im = (grouped_re * gain_im + grouped_im * gain_re).reshape(spec_re.shape)
    return (out_re.astype(jnp.bfloat16), out_im.astype(jnp.bfloat16))


def spectral_middle(parts, local_freq, inner_re, inner_im, freq_total):
    sig_re, sig_im, kern_re, kern_im = parts
    inner_ids = jnp.arange(BLOCK, dtype=jnp.int32)
    turn_re, turn_im = unit_pair(local_freq[:, None] * inner_ids[None, :] % freq_total, freq_total)
    turned_re, turned_im = rotate(turn_re, turn_im, sig_re, sig_im)
    kturn_re, kturn_im = rotate(turn_re, turn_im, kern_re, kern_im)
    spec_re, spec_im = mix_rows("qb,rbc->rqc", inner_re, inner_im, turned_re, turned_im)
    filt_re, filt_im = mix_rows("qb,rbc->rqc", inner_re, inner_im, kturn_re, kturn_im)
    weight_re, weight_im = apply_filter(spec_re, spec_im, filt_re, filt_im)
    back_re, back_im = mix_rows("bq,rqc->rbc", inner_re, -inner_im, weight_re, weight_im)
    return rotate(turn_re, -turn_im, back_re, back_im)


def block_columns(signal, kernel):
    return (
        lax.all_to_all(signal, "ctx", split_axis=1, concat_axis=0, tiled=True),
        lax.all_to_all(kernel, "ctx", split_axis=1, concat_axis=0, tiled=True),
    )


def token_rows(conv_vals):
    return lax.all_to_all(conv_vals, "ctx", split_axis=0, concat_axis=1, tiled=True)


def general_local(section_input, long_filter, short_filter, skip_gain):
    acts_local = section_input[0]
    tok_rows, chan_local = acts_local.shape
    filt_local = long_filter.shape[2]
    n_ctx = lax.axis_size("ctx")
    ctx_rank = lax.axis_index("ctx")
    blocks_local = tok_rows // BLOCK
    half_span = blocks_local * n_ctx
    full_span = 2 * half_span
    freq_total = full_span * BLOCK
    rows_local = full_span // n_ctx
    partial_squares = jnp.sum(acts_local * acts_local, axis=1)
    total_squares = lax.psum(partial_squares, "tp")
    normed = (acts_local * lax.rsqrt(total_squares / CHAN + 1e-06)[:, None]).astype(jnp.bfloat16)
    earlier = from_behind(normed[tok_rows - (TAPS - 1) :], "ctx", 1)
    extended = jnp.concatenate([earlier, normed], axis=0)
    taps_all = short_filter[0].astype(jnp.float32)
    featured = []
    for feature_id in range(3):
        running = jnp.zeros((tok_rows, chan_local), jnp.float32)
        for offset in range(TAPS):
            begin_row = TAPS - 1 - offset
            running = (
                running
                + taps_all[feature_id, offset][None, :] * extended[begin_row : begin_row + tok_rows]
            )
        featured.append(running)
    query = featured[0].astype(jnp.bfloat16)
    product = (featured[1] * featured[2]).astype(jnp.bfloat16)
    block_ids = jnp.arange(half_span, dtype=jnp.int32)
    inner_ids = jnp.arange(BLOCK, dtype=jnp.int32)
    inner_re, inner_im = unit_pair(inner_ids[:, None] * inner_ids[None, :] % BLOCK, BLOCK)
    inner_re = inner_re.astype(jnp.bfloat16)
    inner_im = inner_im.astype(jnp.bfloat16)
    signal = product.reshape(blocks_local, BLOCK, chan_local)
    kernel = long_filter[0].reshape(blocks_local, BLOCK, filt_local)
    signal_cols, kernel_cols = block_columns(signal, kernel)
    freq_rows = jnp.arange(full_span, dtype=jnp.int32)
    outer_re, outer_im = unit_pair(freq_rows[:, None] * block_ids[None, :] % full_span, full_span)
    table_re = outer_re.astype(jnp.bfloat16)
    table_im = outer_im.astype(jnp.bfloat16)
    sig_re, sig_im = first_section(table_re, table_im, signal_cols)
    kern_re, kern_im = first_section(table_re, table_im, kernel_cols)
    got = (
        lax.all_to_all(sig_re, "ctx", split_axis=0, concat_axis=1, tiled=True),
        lax.all_to_all(sig_im, "ctx", split_axis=0, concat_axis=1, tiled=True),
        lax.all_to_all(kern_re, "ctx", split_axis=0, concat_axis=1, tiled=True),
        lax.all_to_all(kern_im, "ctx", split_axis=0, concat_axis=1, tiled=True),
    )
    local_freq = ctx_rank * rows_local + jnp.arange(rows_local, dtype=jnp.int32)
    back_re, back_im = spectral_middle(got, local_freq, inner_re, inner_im, freq_total)
    gathered_re, gathered_im = (
        lax.all_to_all(back_re, "ctx", split_axis=1, concat_axis=0, tiled=True),
        lax.all_to_all(back_im, "ctx", split_axis=1, concat_axis=0, tiled=True),
    )
    conv_vals = jnp.einsum("ka,kbc->abc", table_re, gathered_re, preferred_element_type=jnp.float32)
    conv_vals = conv_vals + jnp.einsum(
        "ka,kbc->abc", table_im, gathered_im, preferred_element_type=jnp.float32
    )
    conv_vals = (conv_vals * (1.0 / freq_total)).astype(jnp.bfloat16)
    conv_tokens = token_rows(conv_vals).reshape(tok_rows, chan_local)
    finished = acts_local + query.astype(jnp.float32) * (
        conv_tokens.astype(jnp.float32) + skip_gain[0][None, :] * product.astype(jnp.float32)
    )
    received = passed_along(finished.astype(jnp.bfloat16), "section", 1).astype(finished.dtype)
    return received[None]


EXTRA = 16
LANES = 128
DEPTH = 64


def odd_tables(length):
    ahead, back = [], []
    for first in range(2):
        phase = (2 * np.arange(length // 2)[:, None] + 1) * np.arange(first, length, 2)[None, :] % (4 * length)
        turn = phase * (2.0 * np.pi / (4 * length))
        ahead.append(np.concatenate([np.cos(turn), -np.sin(turn)], axis=0))
        back.append(ahead[-1].T / length)
    return [np.concatenate(parts, axis=0).astype(ml_dtypes.bfloat16) for parts in (ahead, back)]


def spread_table(filters, channels):
    owner = np.arange(channels) // (channels // filters)
    return (np.arange(filters)[:, None] == owner[None, :]).astype(ml_dtypes.bfloat16)


def column_of(row):
    return jnp.transpose(jnp.broadcast_to(row, (LANES, row.shape[1])))


def three_terms(x):
    terms = []
    for _ in range(3):
        terms.append(x.astype(jnp.bfloat16).astype(jnp.float32))
        x = x - terms[-1]
    return terms


def next_place(rank, step, peers):
    return lax.rem(rank + step + peers, peers)


def cut_kernel(peers, x_hbm, filt_hbm, *refs):
    outs, (sums_ref, x_ref, filt_ref, plain, turned, sems) = refs[:peers], refs[peers:]
    rank = lax.axis_index("ctx")
    rows, chans = x_hbm.shape
    part, width = rows // 2, chans // peers
    filters = filt_hbm.shape[1] // peers
    tiles = width // LANES
    copies = [pltpu.make_async_copy(filt_hbm, filt_ref, sems.at[peers * tiles])]
    for step in range(peers):
        begin = next_place(rank, step, peers) * width
        for tile in range(tiles):
            lanes = pl.ds(pl.multiple_of(begin + tile * LANES, LANES), LANES)
            at = step * tiles + tile
            copies.append(pltpu.make_async_copy(x_hbm.at[:, lanes], x_ref.at[at], sems.at[at]))
    for copy in copies:
        copy.start()
    copies[0].wait()
    for at in range(plain.shape[0]):
        lanes = slice(at * LANES, (at + 1) * LANES)
        plain[at] = filt_ref[:, lanes].astype(jnp.float32)
        halves = [plain[at, pl.ds(odd, part, stride=2), :] for odd in range(2)]
        turned[lanes, :] = jnp.transpose(jnp.concatenate(halves, axis=0)).astype(jnp.bfloat16)
    base = tiles * rows
    for step in range(peers):
        own = pl.ds(pl.multiple_of(next_place(rank, step, peers) * filters, filters), filters)
        outs[step][base : base + filters, :] = turned[own, :]
    totals = [jnp.zeros((part, LANES), jnp.float32)] * 2
    for step in range(peers):
        for tile in range(tiles):
            at = step * tiles + tile
            copies[1 + at].wait()
            for odd in range(2):
                acts = x_ref[at, pl.ds(odd, part, stride=2), :]
                top = tile * rows + odd * part
                outs[step][top : top + part, :] = acts.astype(jnp.bfloat16)
                totals[odd] = totals[odd] + acts * acts
    column = jnp.sum(jnp.concatenate(totals, axis=0), axis=1, keepdims=True)
    row = jnp.transpose(jnp.broadcast_to(column, (rows, LANES)))[:EXTRA, :]
    nth = lax.broadcasted_iota(jnp.int32, (EXTRA, rows), 0)
    terms = three_terms(row)
    sums = jnp.where(nth == 0, terms[0], jnp.where(nth == 1, terms[1], jnp.where(nth == 2, terms[2], 0.0)))
    sums_ref[...] = sums.astype(jnp.bfloat16)
    for step in range(peers):
        outs[step][base + filters :, :] = sums.astype(jnp.bfloat16)


def attach_kernel(count, *refs):
    messages, (own_ref, other_ref) = refs[:count], refs[count : count + 2]
    outs = refs[count + 2 :]
    both = own_ref[...].astype(jnp.float32) + pltpu.roll(other_ref[...].astype(jnp.float32), 3, 0)
    for out in outs:
        out[out.shape[0] - EXTRA :, :] = both.astype(jnp.bfloat16)


def collect_kernel(count, *refs):
    out = refs[-1]
    for i in range(count):
        out[i * EXTRA : (i + 1) * EXTRA, :] = refs[i][refs[i].shape[0] - EXTRA :, :]


def table_kernel(pieces, after, *refs):
    count = (len(refs) - 1) // 2
    tables, outs, sems = refs[:count], refs[count : 2 * count], refs[2 * count]
    copies = []
    for t in range(count):
        parts = pieces if tables[t].shape[0] % (pieces * LANES) == 0 else 1
        depth = tables[t].shape[0] // parts
        for i in range(parts):
            here = pl.ds(i * depth, depth)
            copies.append(pltpu.make_async_copy(tables[t].at[here], outs[t].at[here], sems.at[len(copies)]))
    for copy in copies:
        copy.start()
    for copy in copies:
        copy.wait()


def scale_of(*sums):
    square = sum(jnp.sum(terms.astype(jnp.float32), axis=0, keepdims=True) for terms in sums)
    return column_of(lax.rsqrt(square * (1.0 / CHAN) + 1e-06))


def scale_block(block, scale, held):
    rows = block.shape[1]
    part = rows // 2
    for tile in range(held.shape[2] // LANES):
        for odd in range(2):
            own = tile * rows + odd * part
            acts = block[own : own + part, :].astype(jnp.float32) * scale[odd * part : (odd + 1) * part]
            held[odd, 8:, tile * LANES : (tile + 1) * LANES] = acts


def short_filters(held, depth, taps, lanes):
    now = [held[odd, 8 : 8 + depth, lanes] for odd in range(2)]
    last = [held[odd, 7 : 7 + depth, lanes] for odd in range(2)]
    results = []
    for moved in ((now[0], last[1], last[0]), (now[1], now[0], last[1])):
        features = []
        for feature in taps:
            running = feature[0][:, lanes] * moved[0]
            for i in range(1, TAPS):
                running = running + feature[i][:, lanes] * moved[i]
            features.append(running)
        results.append((features[0].astype(jnp.bfloat16), (features[1] * features[2]).astype(jnp.bfloat16)))
    return results


def read_taps(taps_ref, chans):
    return [[taps_ref[f, i : i + 1, chans].astype(jnp.float32) for i in range(TAPS)] for f in range(3)]


def spread_out(block, spread_ref):
    filters = spread_ref.shape[0]
    base = block.shape[0] - EXTRA - filters
    return lax.dot_general(
        block[base : base + filters, :],
        spread_ref[...],
        (((0,), (0,)), ((), ())),
        preferred_element_type=jnp.float32,
    ).astype(jnp.bfloat16)


def lead_in(held, before, inside):
    for odd in range(2):
        row = before[odd, before.shape[1] - 1 :, :]
        held[odd, 7:8, :] = jnp.where(inside, row, 0.0)


def early_kernel(peers, early, *refs):
    count = len(early)
    blocks, halves = refs[:count], refs[count : 3 * count]
    taps_ref, spread_ref, held, query, product, spread = refs[3 * count :]
    width, part = held.shape[3], held.shape[2] - 8
    rank = lax.axis_index("ctx")
    chans = pl.ds(pl.multiple_of(rank * width, width), width)
    taps = read_taps(taps_ref, chans)
    for i in range(count):
        held[i, :, :8, :] = jnp.zeros((2, 8, width), jnp.float32)
        scale_block(blocks[i], scale_of(halves[2 * i][...], halves[2 * i + 1][...]), held.at[i])
    for i, step in enumerate(early):
        before = (step + 1) % peers
        if before in early:
            lead_in(held.at[i], held.at[early.index(before)], next_place(rank, -step, peers) > 0)
    tokens = [pl.ds(pl.multiple_of(next_place(rank, -step, peers) * part, part), part) for step in early]
    for first in range(0, width, LANES):
        lanes = slice(first, first + LANES)
        for i in range(count):
            for odd, results in enumerate(short_filters(held.at[i], part, taps, lanes)):
                query[odd, tokens[i], lanes], product[odd, tokens[i], lanes] = results
    for i in range(count):
        both = spread_out(blocks[i], spread_ref)
        for odd in range(2):
            spread[odd, tokens[i], :] = both[odd * part : (odd + 1) * part]


def layer_kernel(peers, early, late, *refs):
    blocks = refs[:peers]
    taps_ref, skip_ref, ahead_ref, return_ref, spread_ref = refs[peers : peers + 5]
    early_held = refs[peers + 5]
    outs = refs[peers + 9 : 2 * peers + 9]
    query, product, spread, held, top_held, spec, filt_spec, weighted, conv = refs[2 * peers + 9 :]
    rank = lax.axis_index("ctx")
    rows, width = outs[0].shape
    part, half = rows // 2, rows * peers // 2
    top = top_held.shape[2] - 8
    chans = pl.ds(pl.multiple_of(rank * width, width), width)
    taps = read_taps(taps_ref, chans)
    skip = skip_ref[:, chans]
    places = [next_place(rank, -step, peers) for step in range(peers)]
    tokens = [pl.ds(pl.multiple_of(place * part, part), part) for place in places]
    tops = [pl.ds(pl.multiple_of(place * part, part), top) for place in places]

    for step in late:
        both = spread_out(blocks[step], spread_ref)
        for odd in range(2):
            spread[odd, tokens[step], :] = both[odd * part : (odd + 1) * part]
    for i, step in enumerate(late):
        scale_block(blocks[step], scale_of(blocks[step][blocks[step].shape[0] - EXTRA :, :]), held.at[i])
    sources = [(held.at[i], part, step) for i, step in enumerate(late)]
    lacking = [step for step in early if (step + 1) % peers in late]
    for i, step in enumerate(lacking):
        top_held[i, :, 8:, :] = early_held[early.index(step), :, 8 : 8 + top, :]
        sources.append((top_held.at[i], top, step))
    for source, _, step in sources:
        before = (step + 1) % peers
        theirs = held.at[late.index(before)] if before in late else early_held.at[early.index(before)]
        lead_in(source, theirs, places[step] > 0)
    for first in range(0, width, LANES):
        lanes = slice(first, first + LANES)
        for source, depth, step in sources:
            here = tokens[step] if depth == part else tops[step]
            for odd, results in enumerate(short_filters(source, depth, taps, lanes)):
                query[odd, here, lanes], product[odd, here, lanes] = results
    for odd in range(2):
        table = ahead_ref[2 * odd * half : 2 * (odd + 1) * half, :]
        filt_spec[odd] = jnp.dot(table, spread[odd], preferred_element_type=jnp.float32)
        spec[odd] = jnp.dot(table, product[odd], preferred_element_type=jnp.float32)
    for first in range(0, width, LANES):
        lanes = slice(first, first + LANES)
        for begin in range(0, half, DEPTH):
            re, im = slice(begin, begin + DEPTH), slice(half + begin, half + begin + DEPTH)
            near, far = [], []
            for values in (spec, filt_spec):
                even_re, even_im = values[0, re, lanes], values[0, im, lanes]
                odd_re, odd_im = values[1, re, lanes], values[1, im, lanes]
                near += [even_re + odd_re, even_im + odd_im]
                far += [even_re - odd_re, odd_im - even_im]
            near_re, near_im = product_of(*near)
            far_re, far_im = product_of(*far)
            weighted[0, re, lanes] = (near_re + far_re).astype(jnp.bfloat16)
            weighted[0, im, lanes] = (near_im - far_im).astype(jnp.bfloat16)
            weighted[1, re, lanes] = (near_re - far_re).astype(jnp.bfloat16)
            weighted[1, im, lanes] = (near_im + far_im).astype(jnp.bfloat16)
    for odd in range(2):
        table = return_ref[odd * half : (odd + 1) * half, :]
        conv[odd] = jnp.dot(table, weighted[odd], preferred_element_type=jnp.float32)
    for step in range(peers):
        source = (peers - step) % peers
        here = tokens[source]
        for tile in range(width // LANES):
            lanes = slice(tile * LANES, (tile + 1) * LANES)
            for odd in range(2):
                own = tile * rows + odd * part
                acts = blocks[source][own : own + part, :].astype(jnp.float32)
                gated = conv[odd, here, lanes] + skip[:, lanes] * product[odd, here, lanes].astype(jnp.float32)
                finished = acts + query[odd, here, lanes].astype(jnp.float32) * gated
                outs[step][odd * part : (odd + 1) * part, lanes] = finished.astype(jnp.bfloat16)


def product_of(left_re, left_im, right_re, right_im):
    return left_re * right_re - left_im * right_im, left_re * right_im + left_im * right_re


def join_kernel(peers, steps, *refs):
    parts, (out_hbm, wide, sems) = refs[: len(steps)], refs[-3:]
    rows, width = parts[0].shape
    rank = lax.axis_index("ctx")
    tiles = width // LANES
    copies = []
    for i, step in enumerate(steps):
        begin = next_place(rank, -step, peers) * width
        for tile in range(tiles):
            at = i * tiles + tile
            for odd in range(2):
                part = parts[i][odd * (rows // 2) : (odd + 1) * (rows // 2), tile * LANES : (tile + 1) * LANES]
                wide[at, pl.ds(odd, rows // 2, stride=2), :] = part.astype(jnp.float32)
            lanes = pl.ds(pl.multiple_of(begin + tile * LANES, LANES), LANES)
            copies.append(pltpu.make_async_copy(wide.at[at], out_hbm.at[:, lanes], sems.at[at]))
            copies[-1].start()
    for copy in copies:
        copy.wait()


def on_device(kernel, args, outs, scratch=(), in_hbm=(), out_hbm=False, flops=0, limit=32, aliases=None):
    whole = pl.BlockSpec(memory_space=pltpu.VMEM)
    far = pl.BlockSpec(memory_space=pltpu.HBM)
    touched = sum(a.size * a.dtype.itemsize for a in (*args, *outs))
    args = [pltpu.with_memory_space_constraint(a, pltpu.HBM) if i in in_hbm else a for i, a in enumerate(args)]
    return pl.pallas_call(
        kernel,
        out_shape=outs,
        in_specs=[far if i in in_hbm else whole for i in range(len(args))],
        out_specs=[far if out_hbm else whole] * len(outs),
        scratch_shapes=list(scratch),
        input_output_aliases=aliases or {},
        compiler_params=pltpu.CompilerParams(vmem_limit_bytes=limit * 2**20),
        cost_estimate=pl.CostEstimate(flops=flops, bytes_accessed=touched, transcendentals=0),
    )(*args)


def hop(x, sections, peers, by_section, by_ctx):
    route = [
        (s * peers + c, (s + by_section) % sections * peers + (c + by_ctx) % peers)
        for s in range(sections)
        for c in range(peers)
    ]
    return lax.ppermute(x, ("section", "ctx"), route)


def channel_local(section_input, long_filter, short_filter, skip_gain):
    acts = section_input[0]
    rows, chans = acts.shape
    sections, peers = lax.axis_size("section"), lax.axis_size("ctx")
    width, filters = chans // peers, long_filter.shape[2] // peers
    length = rows * peers
    half = length // 2
    bf16, f32 = jnp.bfloat16, jnp.float32
    pieces = 4
    part, tail = rows // 2, width // LANES * rows + filters
    message = jax.ShapeDtypeStruct((tail + EXTRA, rows), bf16)
    *sent, own_sums = on_device(
        functools.partial(cut_kernel, peers),
        [acts, long_filter[0]],
        [message] * peers + [jax.ShapeDtypeStruct((EXTRA, rows), bf16)],
        [
            pltpu.VMEM((chans // LANES, rows, LANES), f32),
            pltpu.VMEM(long_filter.shape[1:], bf16),
            pltpu.VMEM((long_filter.shape[2] // LANES, rows, LANES), f32),
            pltpu.VMEM((long_filter.shape[2], rows), bf16),
            pltpu.SemaphoreType.DMA((chans // LANES + 1,)),
        ],
        in_hbm=(0, 1),
    )
    early, late = [0, 1], list(range(peers - 1, 1, -1))
    got = {0: sent[0]}
    for k in early[1:]:
        got[k] = hop(sent[k], sections, peers, 0, k)
    other_sums = lax.ppermute(own_sums, "tp", [(0, 1), (1, 0)])
    ready = on_device(
        functools.partial(attach_kernel, len(late)),
        [*(sent[k] for k in late), own_sums, other_sums],
        [message] * len(late),
        aliases={i: i for i in range(len(late))},
    )
    for k, x in zip(late, ready):
        got[k] = hop(x, sections, peers, 0, k)
    tables = [jnp.asarray(t) for t in (*odd_tables(length), spread_table(filters, width))]
    tables += [short_filter[0], skip_gain]
    ahead, back, spread, taps, skip = on_device(
        functools.partial(table_kernel, pieces),
        [other_sums, *tables],
        [jax.ShapeDtypeStruct(t.shape, t.dtype) for t in tables],
        [pltpu.SemaphoreType.DMA((pieces * len(tables),))],
        in_hbm=range(1, 1 + len(tables)),
    )
    (halves,) = on_device(
        functools.partial(collect_kernel, len(early) - 1),
        [*(got[k] for k in early[1:]), ready[0]],
        [jax.ShapeDtypeStruct(((len(early) - 1) * EXTRA, rows), bf16)],
    )
    others = lax.ppermute(halves, "tp", [(0, 1), (1, 0)])
    pairs = [own_sums, other_sums]
    for i in range(len(early) - 1):
        pairs += [half_sums[i * EXTRA : (i + 1) * EXTRA] for half_sums in (halves, others)]
    begun = on_device(
        functools.partial(early_kernel, peers, early),
        [*(got[k] for k in early), *pairs, taps, spread],
        [
            jax.ShapeDtypeStruct((len(early), 2, part + 8, width), f32),
            *[jax.ShapeDtypeStruct((2, half, width), bf16)] * 3,
        ],
    )
    done = on_device(
        functools.partial(layer_kernel, peers, early, late),
        [*(got[k] for k in range(peers)), taps, skip, ahead, back, spread, *begun],
        [
            *[jax.ShapeDtypeStruct((rows, width), bf16)] * peers,
            *[jax.ShapeDtypeStruct((2, half, width), bf16)] * 3,
        ],
        [
            pltpu.VMEM((len(late), 2, part + 8, width), f32),
            pltpu.VMEM((2, 2, EXTRA + 8, width), f32),
            pltpu.VMEM((2, length, width), f32),
            pltpu.VMEM((2, length, width), f32),
            pltpu.VMEM((2, length, width), bf16),
            pltpu.VMEM((2, half, width), f32),
        ],
        flops=6 * length * length * width,
        aliases={peers + 6 + i: peers + i for i in range(3)},
    )
    order = sorted(range(peers), key=lambda k: (k % 2, k))
    arrived = {k: hop(done[k], sections, peers, 1, k) for k in order}
    out = jax.ShapeDtypeStruct((rows, chans), f32)
    tiles = width // LANES
    received = None
    for steps in (order[: peers // 2], order[peers // 2 :]):
        (received,) = on_device(
            functools.partial(join_kernel, peers, steps),
            [arrived[k] for k in steps] + ([] if received is None else [received]),
            [out],
            [pltpu.VMEM((len(steps) * tiles, rows, LANES), f32), pltpu.SemaphoreType.DMA((len(steps) * tiles,))],
            in_hbm=(len(steps),),
            out_hbm=True,
            aliases={} if received is None else {len(steps): 0},
        )
    return received[None]


def fits_channel_plan(mesh, section_input, long_filter):
    peers, cores = mesh.shape["ctx"], mesh.shape["tp"]
    tokens = section_input.shape[1]
    width = section_input.shape[2] // (peers * cores)
    filters = long_filter.shape[2] // (peers * cores)
    return (
        peers > 2
        and tokens == peers * LANES
        and tokens <= 1024
        and width % LANES == 0
        and filters % EXTRA == 0
        and long_filter.shape[2] // cores % LANES == 0
    )


def solution(mesh):
    in_specs = (
        P("section", "ctx", "tp"),
        P("section", "ctx", "tp"),
        P("section", None, None, "tp"),
        P("section", "tp"),
    )
    out_specs = P("section", "ctx", "tp")

    def layer(section_input, long_filter, short_filter, skip_gain):
        local = channel_local if fits_channel_plan(mesh, section_input, long_filter) else general_local
        mapped = jax.shard_map(local, mesh=mesh, in_specs=in_specs, out_specs=out_specs, check_vma=False)
        return mapped(section_input, long_filter, short_filter, skip_gain)

    return layer
```

```python
import functools

import jax
import jax.numpy as jnp
import ml_dtypes
import numpy as np
from jax import lax
from jax.experimental import pallas as pl
from jax.experimental.pallas import tpu as pltpu
from jax.sharding import PartitionSpec as P

CHAN = 4096
TAPS = 3
BLOCK = 128


TWO_PI = 6.283185307179586


def from_behind(block, axis, distance):
    devices = range(lax.axis_size(axis))
    route = [(i - distance, i) for i in devices if i - distance in devices]
    return lax.ppermute(block, axis, route)


def passed_along(x, axis, by):
    peers = lax.axis_size(axis)
    return lax.ppermute(x, axis, [(i, (i + by) % peers) for i in range(peers)])


def unit_pair(position, period):
    mirror = period - position
    folded = jnp.minimum(position, mirror)
    angle_value = folded.astype(jnp.float32) * (TWO_PI / period)
    cosine = jnp.where(4 * folded == period, 0.0, jnp.cos(angle_value))
    sine_part = jnp.where((folded == 0) | (2 * folded == period), 0.0, jnp.sin(angle_value))
    sine_part = jnp.where(position > mirror, -sine_part, sine_part)
    return (cosine, -sine_part)


def first_section(table_re, table_im, data):
    real_out = jnp.einsum("ka,abc->kbc", table_re, data, preferred_element_type=jnp.float32)
    imag_out = jnp.einsum("ka,abc->kbc", table_im, data, preferred_element_type=jnp.float32)
    return (real_out.astype(jnp.bfloat16), imag_out.astype(jnp.bfloat16))


def rotate(turn_re, turn_im, data_re, data_im):
    plain_re = data_re.astype(jnp.float32)
    plain_im = data_im.astype(jnp.float32)
    real_out = turn_re[:, :, None] * plain_re - turn_im[:, :, None] * plain_im
    imag_out = turn_re[:, :, None] * plain_im + turn_im[:, :, None] * plain_re
    return (real_out.astype(jnp.bfloat16), imag_out.astype(jnp.bfloat16))


def mix_rows(form, table_re, table_im, data_re, data_im):

    def product_of(left, right):
        return jnp.einsum(form, left, right, preferred_element_type=jnp.float32)

    real_out = product_of(table_re, data_re) - product_of(table_im, data_im)
    imag_out = product_of(table_re, data_im) + product_of(table_im, data_re)
    return (real_out, imag_out)


def apply_filter(spec_re, spec_im, filt_re, filt_im):
    rows_count, inner_width, channels = spec_re.shape
    filters = filt_re.shape[2]
    grouped_shape = (rows_count, inner_width, filters, channels // filters)
    grouped_re = spec_re.reshape(grouped_shape)
    grouped_im = spec_im.reshape(grouped_shape)
    gain_re = filt_re[..., None]
    gain_im = filt_im[..., None]
    out_re = (grouped_re * gain_re - grouped_im * gain_im).reshape(spec_re.shape)
    out_im = (grouped_re * gain_im + grouped_im * gain_re).reshape(spec_re.shape)
    return (out_re.astype(jnp.bfloat16), out_im.astype(jnp.bfloat16))


def spectral_middle(parts, local_freq, inner_re, inner_im, freq_total):
    sig_re, sig_im, kern_re, kern_im = parts
    inner_ids = jnp.arange(BLOCK, dtype=jnp.int32)
    turn_re, turn_im = unit_pair(local_freq[:, None] * inner_ids[None, :] % freq_total, freq_total)
    turned_re, turned_im = rotate(turn_re, turn_im, sig_re, sig_im)
    kturn_re, kturn_im = rotate(turn_re, turn_im, kern_re, kern_im)
    spec_re, spec_im = mix_rows("qb,rbc->rqc", inner_re, inner_im, turned_re, turned_im)
    filt_re, filt_im = mix_rows("qb,rbc->rqc", inner_re, inner_im, kturn_re, kturn_im)
    weight_re, weight_im = apply_filter(spec_re, spec_im, filt_re, filt_im)
    back_re, back_im = mix_rows("bq,rqc->rbc", inner_re, -inner_im, weight_re, weight_im)
    return rotate(turn_re, -turn_im, back_re, back_im)


def block_columns(signal, kernel):
    return (
        lax.all_to_all(signal, "ctx", split_axis=1, concat_axis=0, tiled=True),
        lax.all_to_all(kernel, "ctx", split_axis=1, concat_axis=0, tiled=True),
    )


def token_rows(conv_vals):
    return lax.all_to_all(conv_vals, "ctx", split_axis=0, concat_axis=1, tiled=True)


def general_local(section_input, long_filter, short_filter, skip_gain):
    acts_local = section_input[0]
    tok_rows, chan_local = acts_local.shape
    filt_local = long_filter.shape[2]
    n_ctx = lax.axis_size("ctx")
    ctx_rank = lax.axis_index("ctx")
    blocks_local = tok_rows // BLOCK
    half_span = blocks_local * n_ctx
    full_span = 2 * half_span
    freq_total = full_span * BLOCK
    rows_local = full_span // n_ctx
    partial_squares = jnp.sum(acts_local * acts_local, axis=1)
    total_squares = lax.psum(partial_squares, "tp")
    normed = (acts_local * lax.rsqrt(total_squares / CHAN + 1e-06)[:, None]).astype(jnp.bfloat16)
    earlier = from_behind(normed[tok_rows - (TAPS - 1) :], "ctx", 1)
    extended = jnp.concatenate([earlier, normed], axis=0)
    taps_all = short_filter[0].astype(jnp.float32)
    featured = []
    for feature_id in range(3):
        running = jnp.zeros((tok_rows, chan_local), jnp.float32)
        for offset in range(TAPS):
            begin_row = TAPS - 1 - offset
            running = (
                running
                + taps_all[feature_id, offset][None, :] * extended[begin_row : begin_row + tok_rows]
            )
        featured.append(running)
    query = featured[0].astype(jnp.bfloat16)
    product = (featured[1] * featured[2]).astype(jnp.bfloat16)
    block_ids = jnp.arange(half_span, dtype=jnp.int32)
    inner_ids = jnp.arange(BLOCK, dtype=jnp.int32)
    inner_re, inner_im = unit_pair(inner_ids[:, None] * inner_ids[None, :] % BLOCK, BLOCK)
    inner_re = inner_re.astype(jnp.bfloat16)
    inner_im = inner_im.astype(jnp.bfloat16)
    signal = product.reshape(blocks_local, BLOCK, chan_local)
    kernel = long_filter[0].reshape(blocks_local, BLOCK, filt_local)
    signal_cols, kernel_cols = block_columns(signal, kernel)
    freq_rows = jnp.arange(full_span, dtype=jnp.int32)
    outer_re, outer_im = unit_pair(freq_rows[:, None] * block_ids[None, :] % full_span, full_span)
    table_re = outer_re.astype(jnp.bfloat16)
    table_im = outer_im.astype(jnp.bfloat16)
    sig_re, sig_im = first_section(table_re, table_im, signal_cols)
    kern_re, kern_im = first_section(table_re, table_im, kernel_cols)
    got = (
        lax.all_to_all(sig_re, "ctx", split_axis=0, concat_axis=1, tiled=True),
        lax.all_to_all(sig_im, "ctx", split_axis=0, concat_axis=1, tiled=True),
        lax.all_to_all(kern_re, "ctx", split_axis=0, concat_axis=1, tiled=True),
        lax.all_to_all(kern_im, "ctx", split_axis=0, concat_axis=1, tiled=True),
    )
    local_freq = ctx_rank * rows_local + jnp.arange(rows_local, dtype=jnp.int32)
    back_re, back_im = spectral_middle(got, local_freq, inner_re, inner_im, freq_total)
    gathered_re, gathered_im = (
        lax.all_to_all(back_re, "ctx", split_axis=1, concat_axis=0, tiled=True),
        lax.all_to_all(back_im, "ctx", split_axis=1, concat_axis=0, tiled=True),
    )
    conv_vals = jnp.einsum("ka,kbc->abc", table_re, gathered_re, preferred_element_type=jnp.float32)
    conv_vals = conv_vals + jnp.einsum(
        "ka,kbc->abc", table_im, gathered_im, preferred_element_type=jnp.float32
    )
    conv_vals = (conv_vals * (1.0 / freq_total)).astype(jnp.bfloat16)
    conv_tokens = token_rows(conv_vals).reshape(tok_rows, chan_local)
    finished = acts_local + query.astype(jnp.float32) * (
        conv_tokens.astype(jnp.float32) + skip_gain[0][None, :] * product.astype(jnp.float32)
    )
    received = passed_along(finished.astype(jnp.bfloat16), "section", 1).astype(finished.dtype)
    return received[None]


EXTRA = 16
LANES = 128
DEPTH = 64


def odd_tables(length):
    ahead, back = [], []
    for first in range(2):
        phase = (2 * np.arange(length // 2)[:, None] + 1) * np.arange(first, length, 2)[None, :] % (4 * length)
        turn = phase * (2.0 * np.pi / (4 * length))
        ahead.append(np.concatenate([np.cos(turn), -np.sin(turn)], axis=0))
        back.append(ahead[-1].T / length)
    return [np.concatenate(parts, axis=0).astype(ml_dtypes.bfloat16) for parts in (ahead, back)]


def spread_table(filters, channels):
    owner = np.arange(channels) // (channels // filters)
    return (np.arange(filters)[:, None] == owner[None, :]).astype(ml_dtypes.bfloat16)


def column_of(row):
    return jnp.transpose(jnp.broadcast_to(row, (LANES, row.shape[1])))


def three_terms(x):
    terms = []
    for _ in range(3):
        terms.append(x.astype(jnp.bfloat16).astype(jnp.float32))
        x = x - terms[-1]
    return terms


def next_place(rank, step, peers):
    return lax.rem(rank + step + peers, peers)


def cut_kernel(peers, x_hbm, filt_hbm, *refs):
    outs, (sums_ref, x_ref, filt_ref, plain, turned, sems) = refs[:peers], refs[peers:]
    rank = lax.axis_index("ctx")
    rows, chans = x_hbm.shape
    part, width = rows // 2, chans // peers
    filters = filt_hbm.shape[1] // peers
    tiles = width // LANES
    copies = [pltpu.make_async_copy(filt_hbm, filt_ref, sems.at[peers * tiles])]
    for step in range(peers):
        begin = next_place(rank, step, peers) * width
        for tile in range(tiles):
            lanes = pl.ds(pl.multiple_of(begin + tile * LANES, LANES), LANES)
            at = step * tiles + tile
            copies.append(pltpu.make_async_copy(x_hbm.at[:, lanes], x_ref.at[at], sems.at[at]))
    for copy in copies:
        copy.start()
    copies[0].wait()
    for at in range(plain.shape[0]):
        lanes = slice(at * LANES, (at + 1) * LANES)
        plain[at] = filt_ref[:, lanes].astype(jnp.float32)
        halves = [plain[at, pl.ds(odd, part, stride=2), :] for odd in range(2)]
        turned[lanes, :] = jnp.transpose(jnp.concatenate(halves, axis=0)).astype(jnp.bfloat16)
    base = tiles * rows
    for step in range(peers):
        own = pl.ds(pl.multiple_of(next_place(rank, step, peers) * filters, filters), filters)
        outs[step][base : base + filters, :] = turned[own, :]
    totals = [jnp.zeros((part, LANES), jnp.float32)] * 2
    for step in range(peers):
        for tile in range(tiles):
            at = step * tiles + tile
            copies[1 + at].wait()
            for odd in range(2):
                acts = x_ref[at, pl.ds(odd, part, stride=2), :]
                top = tile * rows + odd * part
                outs[step][top : top + part, :] = acts.astype(jnp.bfloat16)
                totals[odd] = totals[odd] + acts * acts
    row = jnp.sum(jnp.transpose(jnp.concatenate(totals, axis=0)), axis=0, keepdims=True)
    row = jnp.broadcast_to(row, (EXTRA, rows))
    nth = lax.broadcasted_iota(jnp.int32, (EXTRA, rows), 0)
    terms = three_terms(row)
    sums = jnp.where(nth == 0, terms[0], jnp.where(nth == 1, terms[1], jnp.where(nth == 2, terms[2], 0.0)))
    sums_ref[...] = sums.astype(jnp.bfloat16)
    for step in range(peers):
        outs[step][base + filters :, :] = sums.astype(jnp.bfloat16)


def attach_kernel(count, *refs):
    messages, (own_ref, other_ref) = refs[:count], refs[count : count + 2]
    outs = refs[count + 2 :]
    both = own_ref[...].astype(jnp.float32) + pltpu.roll(other_ref[...].astype(jnp.float32), 3, 0)
    for out in outs:
        out[out.shape[0] - EXTRA :, :] = both.astype(jnp.bfloat16)


def collect_kernel(count, *refs):
    out = refs[-1]
    for i in range(count):
        out[i * EXTRA : (i + 1) * EXTRA, :] = refs[i][refs[i].shape[0] - EXTRA :, :]


def table_kernel(pieces, after, *refs):
    count = (len(refs) - 1) // 2
    tables, outs, sems = refs[:count], refs[count : 2 * count], refs[2 * count]
    copies = []
    for t in range(count):
        parts = pieces if tables[t].shape[0] % (pieces * LANES) == 0 else 1
        depth = tables[t].shape[0] // parts
        for i in range(parts):
            here = pl.ds(i * depth, depth)
            copies.append(pltpu.make_async_copy(tables[t].at[here], outs[t].at[here], sems.at[len(copies)]))
    for copy in copies:
        copy.start()
    for copy in copies:
        copy.wait()


def scale_of(*sums):
    square = sum(jnp.sum(terms.astype(jnp.float32), axis=0, keepdims=True) for terms in sums)
    return column_of(lax.rsqrt(square * (1.0 / CHAN) + 1e-06))


def scale_block(block, scale, held):
    rows = block.shape[1]
    part = rows // 2
    for tile in range(held.shape[2] // LANES):
        for odd in range(2):
            own = tile * rows + odd * part
            acts = block[own : own + part, :].astype(jnp.float32) * scale[odd * part : (odd + 1) * part]
            held[odd, 8:, tile * LANES : (tile + 1) * LANES] = acts


def short_filters(held, depth, taps, lanes):
    now = [held[odd, 8 : 8 + depth, lanes] for odd in range(2)]
    last = [held[odd, 7 : 7 + depth, lanes] for odd in range(2)]
    results = []
    for moved in ((now[0], last[1], last[0]), (now[1], now[0], last[1])):
        features = []
        for feature in taps:
            running = feature[0][:, lanes] * moved[0]
            for i in range(1, TAPS):
                running = running + feature[i][:, lanes] * moved[i]
            features.append(running)
        results.append((features[0].astype(jnp.bfloat16), (features[1] * features[2]).astype(jnp.bfloat16)))
    return results


def read_taps(taps_ref, chans):
    return [[taps_ref[f, i : i + 1, chans].astype(jnp.float32) for i in range(TAPS)] for f in range(3)]


def spread_out(block, spread_ref):
    filters = spread_ref.shape[0]
    base = block.shape[0] - EXTRA - filters
    return lax.dot_general(
        block[base : base + filters, :],
        spread_ref[...],
        (((0,), (0,)), ((), ())),
        preferred_element_type=jnp.float32,
    ).astype(jnp.bfloat16)


def lead_in(held, before, inside):
    for odd in range(2):
        row = before[odd, before.shape[1] - 1 :, :]
        held[odd, 7:8, :] = jnp.where(inside, row, 0.0)


def early_kernel(peers, early, *refs):
    count = len(early)
    blocks, halves = refs[:count], refs[count : 3 * count]
    taps_ref, spread_ref, held, query, product, spread = refs[3 * count :]
    width, part = held.shape[3], held.shape[2] - 8
    rank = lax.axis_index("ctx")
    chans = pl.ds(pl.multiple_of(rank * width, width), width)
    taps = read_taps(taps_ref, chans)
    for i in range(count):
        held[i, :, :8, :] = jnp.zeros((2, 8, width), jnp.float32)
        scale_block(blocks[i], scale_of(halves[2 * i][...], halves[2 * i + 1][...]), held.at[i])
    for i, step in enumerate(early):
        before = (step + 1) % peers
        if before in early:
            lead_in(held.at[i], held.at[early.index(before)], next_place(rank, -step, peers) > 0)
    tokens = [pl.ds(pl.multiple_of(next_place(rank, -step, peers) * part, part), part) for step in early]
    for first in range(0, width, LANES):
        lanes = slice(first, first + LANES)
        for i in range(count):
            for odd, results in enumerate(short_filters(held.at[i], part, taps, lanes)):
                query[odd, tokens[i], lanes], product[odd, tokens[i], lanes] = results
    for i in range(count):
        both = spread_out(blocks[i], spread_ref)
        for odd in range(2):
            spread[odd, tokens[i], :] = both[odd * part : (odd + 1) * part]


def layer_kernel(peers, early, late, *refs):
    blocks = refs[:peers]
    taps_ref, skip_ref, ahead_ref, return_ref, spread_ref = refs[peers : peers + 5]
    early_held = refs[peers + 5]
    outs = refs[peers + 9 : 2 * peers + 9]
    query, product, spread, held, top_held, spec, filt_spec, weighted, conv = refs[2 * peers + 9 :]
    rank = lax.axis_index("ctx")
    rows, width = outs[0].shape
    part, half = rows // 2, rows * peers // 2
    top = top_held.shape[2] - 8
    chans = pl.ds(pl.multiple_of(rank * width, width), width)
    taps = read_taps(taps_ref, chans)
    skip = skip_ref[:, chans]
    places = [next_place(rank, -step, peers) for step in range(peers)]
    tokens = [pl.ds(pl.multiple_of(place * part, part), part) for place in places]
    tops = [pl.ds(pl.multiple_of(place * part, part), top) for place in places]

    for step in late:
        both = spread_out(blocks[step], spread_ref)
        for odd in range(2):
            spread[odd, tokens[step], :] = both[odd * part : (odd + 1) * part]
    for i, step in enumerate(late):
        scale_block(blocks[step], scale_of(blocks[step][blocks[step].shape[0] - EXTRA :, :]), held.at[i])
    sources = [(held.at[i], part, step) for i, step in enumerate(late)]
    lacking = [step for step in early if (step + 1) % peers in late]
    for i, step in enumerate(lacking):
        top_held[i, :, 8:, :] = early_held[early.index(step), :, 8 : 8 + top, :]
        sources.append((top_held.at[i], top, step))
    for source, _, step in sources:
        before = (step + 1) % peers
        theirs = held.at[late.index(before)] if before in late else early_held.at[early.index(before)]
        lead_in(source, theirs, places[step] > 0)
    for first in range(0, width, LANES):
        lanes = slice(first, first + LANES)
        for source, depth, step in sources:
            here = tokens[step] if depth == part else tops[step]
            for odd, results in enumerate(short_filters(source, depth, taps, lanes)):
                query[odd, here, lanes], product[odd, here, lanes] = results
    for odd in range(2):
        table = ahead_ref[2 * odd * half : 2 * (odd + 1) * half, :]
        filt_spec[odd] = jnp.dot(table, spread[odd], preferred_element_type=jnp.float32)
        spec[odd] = jnp.dot(table, product[odd], preferred_element_type=jnp.float32)
    for first in range(0, width, LANES):
        lanes = slice(first, first + LANES)
        for begin in range(0, half, DEPTH):
            re, im = slice(begin, begin + DEPTH), slice(half + begin, half + begin + DEPTH)
            near, far = [], []
            for values in (spec, filt_spec):
                even_re, even_im = values[0, re, lanes], values[0, im, lanes]
                odd_re, odd_im = values[1, re, lanes], values[1, im, lanes]
                near += [even_re + odd_re, even_im + odd_im]
                far += [even_re - odd_re, odd_im - even_im]
            near_re, near_im = product_of(*near)
            far_re, far_im = product_of(*far)
            weighted[0, re, lanes] = (near_re + far_re).astype(jnp.bfloat16)
            weighted[0, im, lanes] = (near_im - far_im).astype(jnp.bfloat16)
            weighted[1, re, lanes] = (near_re - far_re).astype(jnp.bfloat16)
            weighted[1, im, lanes] = (near_im + far_im).astype(jnp.bfloat16)
    for odd in range(2):
        table = return_ref[odd * half : (odd + 1) * half, :]
        conv[odd] = jnp.dot(table, weighted[odd], preferred_element_type=jnp.float32)
        for step in range(peers):
            source = (peers - step) % peers
            here = tokens[source]
            for tile in range(width // LANES):
                lanes = slice(tile * LANES, (tile + 1) * LANES)
                own = tile * rows + odd * part
                acts = blocks[source][own : own + part, :].astype(jnp.float32)
                gated = conv[odd, here, lanes] + skip[:, lanes] * product[odd, here, lanes].astype(jnp.float32)
                finished = acts + query[odd, here, lanes].astype(jnp.float32) * gated
                outs[step][odd * part : (odd + 1) * part, lanes] = finished.astype(jnp.bfloat16)


def product_of(left_re, left_im, right_re, right_im):
    return left_re * right_re - left_im * right_im, left_re * right_im + left_im * right_re


def join_kernel(peers, steps, *refs):
    parts, (out_hbm, wide, sems) = refs[: len(steps)], refs[-3:]
    rows, width = parts[0].shape
    rank = lax.axis_index("ctx")
    tiles = width // LANES
    copies = []
    for i, step in enumerate(steps):
        begin = next_place(rank, -step, peers) * width
        for tile in range(tiles):
            at = i * tiles + tile
            for odd in range(2):
                part = parts[i][odd * (rows // 2) : (odd + 1) * (rows // 2), tile * LANES : (tile + 1) * LANES]
                wide[at, pl.ds(odd, rows // 2, stride=2), :] = part.astype(jnp.float32)
            lanes = pl.ds(pl.multiple_of(begin + tile * LANES, LANES), LANES)
            copies.append(pltpu.make_async_copy(wide.at[at], out_hbm.at[:, lanes], sems.at[at]))
            copies[-1].start()
    for copy in copies:
        copy.wait()


def on_device(kernel, args, outs, scratch=(), in_hbm=(), out_hbm=False, flops=0, limit=32, aliases=None):
    whole = pl.BlockSpec(memory_space=pltpu.VMEM)
    far = pl.BlockSpec(memory_space=pltpu.HBM)
    touched = sum(a.size * a.dtype.itemsize for a in (*args, *outs))
    args = [pltpu.with_memory_space_constraint(a, pltpu.HBM) if i in in_hbm else a for i, a in enumerate(args)]
    return pl.pallas_call(
        kernel,
        out_shape=outs,
        in_specs=[far if i in in_hbm else whole for i in range(len(args))],
        out_specs=[far if out_hbm else whole] * len(outs),
        scratch_shapes=list(scratch),
        input_output_aliases=aliases or {},
        compiler_params=pltpu.CompilerParams(vmem_limit_bytes=limit * 2**20),
        cost_estimate=pl.CostEstimate(flops=flops, bytes_accessed=touched, transcendentals=0),
    )(*args)


def hop(x, sections, peers, by_section, by_ctx):
    route = [
        (s * peers + c, (s + by_section) % sections * peers + (c + by_ctx) % peers)
        for s in range(sections)
        for c in range(peers)
    ]
    return lax.ppermute(x, ("section", "ctx"), route)


def channel_local(section_input, long_filter, short_filter, skip_gain):
    acts = section_input[0]
    rows, chans = acts.shape
    sections, peers = lax.axis_size("section"), lax.axis_size("ctx")
    width, filters = chans // peers, long_filter.shape[2] // peers
    length = rows * peers
    half = length // 2
    bf16, f32 = jnp.bfloat16, jnp.float32
    pieces = 4
    part, tail = rows // 2, width // LANES * rows + filters
    message = jax.ShapeDtypeStruct((tail + EXTRA, rows), bf16)
    *sent, own_sums = on_device(
        functools.partial(cut_kernel, peers),
        [acts, long_filter[0]],
        [message] * peers + [jax.ShapeDtypeStruct((EXTRA, rows), bf16)],
        [
            pltpu.VMEM((chans // LANES, rows, LANES), f32),
            pltpu.VMEM(long_filter.shape[1:], bf16),
            pltpu.VMEM((long_filter.shape[2] // LANES, rows, LANES), f32),
            pltpu.VMEM((long_filter.shape[2], rows), bf16),
            pltpu.SemaphoreType.DMA((chans // LANES + 1,)),
        ],
        in_hbm=(0, 1),
    )
    early, late = [0, 1], list(range(peers - 1, 1, -1))
    got = {0: sent[0]}
    for k in early[1:]:
        got[k] = hop(sent[k], sections, peers, 0, k)
    other_sums = lax.ppermute(own_sums, "tp", [(0, 1), (1, 0)])
    ready = on_device(
        functools.partial(attach_kernel, len(late)),
        [*(sent[k] for k in late), own_sums, other_sums],
        [message] * len(late),
        aliases={i: i for i in range(len(late))},
    )
    for k, x in zip(late, ready):
        got[k] = hop(x, sections, peers, 0, k)
    tables = [jnp.asarray(t) for t in (*odd_tables(length), spread_table(filters, width))]
    tables += [short_filter[0], skip_gain]
    ahead, back, spread, taps, skip = on_device(
        functools.partial(table_kernel, pieces),
        [other_sums, *tables],
        [jax.ShapeDtypeStruct(t.shape, t.dtype) for t in tables],
        [pltpu.SemaphoreType.DMA((pieces * len(tables),))],
        in_hbm=range(1, 1 + len(tables)),
    )
    (halves,) = on_device(
        functools.partial(collect_kernel, len(early) - 1),
        [*(got[k] for k in early[1:]), ready[0]],
        [jax.ShapeDtypeStruct(((len(early) - 1) * EXTRA, rows), bf16)],
    )
    others = lax.ppermute(halves, "tp", [(0, 1), (1, 0)])
    pairs = [own_sums, other_sums]
    for i in range(len(early) - 1):
        pairs += [half_sums[i * EXTRA : (i + 1) * EXTRA] for half_sums in (halves, others)]
    begun = on_device(
        functools.partial(early_kernel, peers, early),
        [*(got[k] for k in early), *pairs, taps, spread],
        [
            jax.ShapeDtypeStruct((len(early), 2, part + 8, width), f32),
            *[jax.ShapeDtypeStruct((2, half, width), bf16)] * 3,
        ],
    )
    done = on_device(
        functools.partial(layer_kernel, peers, early, late),
        [*(got[k] for k in range(peers)), taps, skip, ahead, back, spread, *begun],
        [
            *[jax.ShapeDtypeStruct((rows, width), bf16)] * peers,
            *[jax.ShapeDtypeStruct((2, half, width), bf16)] * 3,
        ],
        [
            pltpu.VMEM((len(late), 2, part + 8, width), f32),
            pltpu.VMEM((2, 2, EXTRA + 8, width), f32),
            pltpu.VMEM((2, length, width), f32),
            pltpu.VMEM((2, length, width), f32),
            pltpu.VMEM((2, length, width), bf16),
            pltpu.VMEM((2, half, width), f32),
        ],
        flops=6 * length * length * width,
        aliases={peers + 6 + i: peers + i for i in range(3)},
    )
    order = sorted(range(peers), key=lambda k: (k % 2, k))
    arrived = {k: hop(done[k], sections, peers, 1, k) for k in order}
    out = jax.ShapeDtypeStruct((rows, chans), f32)
    tiles = width // LANES
    received = None
    for steps in (order[: peers // 2], order[peers // 2 :]):
        (received,) = on_device(
            functools.partial(join_kernel, peers, steps),
            [arrived[k] for k in steps] + ([] if received is None else [received]),
            [out],
            [pltpu.VMEM((len(steps) * tiles, rows, LANES), f32), pltpu.SemaphoreType.DMA((len(steps) * tiles,))],
            in_hbm=(len(steps),),
            out_hbm=True,
            aliases={} if received is None else {len(steps): 0},
        )
    return received[None]


def fits_channel_plan(mesh, section_input, long_filter):
    peers, cores = mesh.shape["ctx"], mesh.shape["tp"]
    tokens = section_input.shape[1]
    width = section_input.shape[2] // (peers * cores)
    filters = long_filter.shape[2] // (peers * cores)
    return (
        peers > 2
        and tokens == peers * LANES
        and tokens <= 1024
        and width % LANES == 0
        and filters % EXTRA == 0
        and long_filter.shape[2] // cores % LANES == 0
    )


def solution(mesh):
    in_specs = (
        P("section", "ctx", "tp"),
        P("section", "ctx", "tp"),
        P("section", None, None, "tp"),
        P("section", "tp"),
    )
    out_specs = P("section", "ctx", "tp")

    def layer(section_input, long_filter, short_filter, skip_gain):
        local = channel_local if fits_channel_plan(mesh, section_input, long_filter) else general_local
        mapped = jax.shard_map(local, mesh=mesh, in_specs=in_specs, out_specs=out_specs, check_vma=False)
        return mapped(section_input, long_filter, short_filter, skip_gain)

    return layer
```

```python
import functools

import jax
import jax.numpy as jnp
import ml_dtypes
import numpy as np
from jax import lax
from jax.experimental import pallas as pl
from jax.experimental.pallas import tpu as pltpu
from jax.sharding import PartitionSpec as P

CHAN = 4096
TAPS = 3
BLOCK = 128


TWO_PI = 6.283185307179586


def from_behind(block, axis, distance):
    devices = range(lax.axis_size(axis))
    route = [(i - distance, i) for i in devices if i - distance in devices]
    return lax.ppermute(block, axis, route)


def passed_along(x, axis, by):
    peers = lax.axis_size(axis)
    return lax.ppermute(x, axis, [(i, (i + by) % peers) for i in range(peers)])


def unit_pair(position, period):
    mirror = period - position
    folded = jnp.minimum(position, mirror)
    angle_value = folded.astype(jnp.float32) * (TWO_PI / period)
    cosine = jnp.where(4 * folded == period, 0.0, jnp.cos(angle_value))
    sine_part = jnp.where((folded == 0) | (2 * folded == period), 0.0, jnp.sin(angle_value))
    sine_part = jnp.where(position > mirror, -sine_part, sine_part)
    return (cosine, -sine_part)


def first_section(table_re, table_im, data):
    real_out = jnp.einsum("ka,abc->kbc", table_re, data, preferred_element_type=jnp.float32)
    imag_out = jnp.einsum("ka,abc->kbc", table_im, data, preferred_element_type=jnp.float32)
    return (real_out.astype(jnp.bfloat16), imag_out.astype(jnp.bfloat16))


def rotate(turn_re, turn_im, data_re, data_im):
    plain_re = data_re.astype(jnp.float32)
    plain_im = data_im.astype(jnp.float32)
    real_out = turn_re[:, :, None] * plain_re - turn_im[:, :, None] * plain_im
    imag_out = turn_re[:, :, None] * plain_im + turn_im[:, :, None] * plain_re
    return (real_out.astype(jnp.bfloat16), imag_out.astype(jnp.bfloat16))


def mix_rows(form, table_re, table_im, data_re, data_im):

    def product_of(left, right):
        return jnp.einsum(form, left, right, preferred_element_type=jnp.float32)

    real_out = product_of(table_re, data_re) - product_of(table_im, data_im)
    imag_out = product_of(table_re, data_im) + product_of(table_im, data_re)
    return (real_out, imag_out)


def apply_filter(spec_re, spec_im, filt_re, filt_im):
    rows_count, inner_width, channels = spec_re.shape
    filters = filt_re.shape[2]
    grouped_shape = (rows_count, inner_width, filters, channels // filters)
    grouped_re = spec_re.reshape(grouped_shape)
    grouped_im = spec_im.reshape(grouped_shape)
    gain_re = filt_re[..., None]
    gain_im = filt_im[..., None]
    out_re = (grouped_re * gain_re - grouped_im * gain_im).reshape(spec_re.shape)
    out_im = (grouped_re * gain_im + grouped_im * gain_re).reshape(spec_re.shape)
    return (out_re.astype(jnp.bfloat16), out_im.astype(jnp.bfloat16))


def spectral_middle(parts, local_freq, inner_re, inner_im, freq_total):
    sig_re, sig_im, kern_re, kern_im = parts
    inner_ids = jnp.arange(BLOCK, dtype=jnp.int32)
    turn_re, turn_im = unit_pair(local_freq[:, None] * inner_ids[None, :] % freq_total, freq_total)
    turned_re, turned_im = rotate(turn_re, turn_im, sig_re, sig_im)
    kturn_re, kturn_im = rotate(turn_re, turn_im, kern_re, kern_im)
    spec_re, spec_im = mix_rows("qb,rbc->rqc", inner_re, inner_im, turned_re, turned_im)
    filt_re, filt_im = mix_rows("qb,rbc->rqc", inner_re, inner_im, kturn_re, kturn_im)
    weight_re, weight_im = apply_filter(spec_re, spec_im, filt_re, filt_im)
    back_re, back_im = mix_rows("bq,rqc->rbc", inner_re, -inner_im, weight_re, weight_im)
    return rotate(turn_re, -turn_im, back_re, back_im)


def block_columns(signal, kernel):
    return (
        lax.all_to_all(signal, "ctx", split_axis=1, concat_axis=0, tiled=True),
        lax.all_to_all(kernel, "ctx", split_axis=1, concat_axis=0, tiled=True),
    )


def token_rows(conv_vals):
    return lax.all_to_all(conv_vals, "ctx", split_axis=0, concat_axis=1, tiled=True)


def general_local(section_input, long_filter, short_filter, skip_gain):
    acts_local = section_input[0]
    tok_rows, chan_local = acts_local.shape
    filt_local = long_filter.shape[2]
    n_ctx = lax.axis_size("ctx")
    ctx_rank = lax.axis_index("ctx")
    blocks_local = tok_rows // BLOCK
    half_span = blocks_local * n_ctx
    full_span = 2 * half_span
    freq_total = full_span * BLOCK
    rows_local = full_span // n_ctx
    partial_squares = jnp.sum(acts_local * acts_local, axis=1)
    total_squares = lax.psum(partial_squares, "tp")
    normed = (acts_local * lax.rsqrt(total_squares / CHAN + 1e-06)[:, None]).astype(jnp.bfloat16)
    earlier = from_behind(normed[tok_rows - (TAPS - 1) :], "ctx", 1)
    extended = jnp.concatenate([earlier, normed], axis=0)
    taps_all = short_filter[0].astype(jnp.float32)
    featured = []
    for feature_id in range(3):
        running = jnp.zeros((tok_rows, chan_local), jnp.float32)
        for offset in range(TAPS):
            begin_row = TAPS - 1 - offset
            running = (
                running
                + taps_all[feature_id, offset][None, :] * extended[begin_row : begin_row + tok_rows]
            )
        featured.append(running)
    query = featured[0].astype(jnp.bfloat16)
    product = (featured[1] * featured[2]).astype(jnp.bfloat16)
    block_ids = jnp.arange(half_span, dtype=jnp.int32)
    inner_ids = jnp.arange(BLOCK, dtype=jnp.int32)
    inner_re, inner_im = unit_pair(inner_ids[:, None] * inner_ids[None, :] % BLOCK, BLOCK)
    inner_re = inner_re.astype(jnp.bfloat16)
    inner_im = inner_im.astype(jnp.bfloat16)
    signal = product.reshape(blocks_local, BLOCK, chan_local)
    kernel = long_filter[0].reshape(blocks_local, BLOCK, filt_local)
    signal_cols, kernel_cols = block_columns(signal, kernel)
    freq_rows = jnp.arange(full_span, dtype=jnp.int32)
    outer_re, outer_im = unit_pair(freq_rows[:, None] * block_ids[None, :] % full_span, full_span)
    table_re = outer_re.astype(jnp.bfloat16)
    table_im = outer_im.astype(jnp.bfloat16)
    sig_re, sig_im = first_section(table_re, table_im, signal_cols)
    kern_re, kern_im = first_section(table_re, table_im, kernel_cols)
    got = (
        lax.all_to_all(sig_re, "ctx", split_axis=0, concat_axis=1, tiled=True),
        lax.all_to_all(sig_im, "ctx", split_axis=0, concat_axis=1, tiled=True),
        lax.all_to_all(kern_re, "ctx", split_axis=0, concat_axis=1, tiled=True),
        lax.all_to_all(kern_im, "ctx", split_axis=0, concat_axis=1, tiled=True),
    )
    local_freq = ctx_rank * rows_local + jnp.arange(rows_local, dtype=jnp.int32)
    back_re, back_im = spectral_middle(got, local_freq, inner_re, inner_im, freq_total)
    gathered_re, gathered_im = (
        lax.all_to_all(back_re, "ctx", split_axis=1, concat_axis=0, tiled=True),
        lax.all_to_all(back_im, "ctx", split_axis=1, concat_axis=0, tiled=True),
    )
    conv_vals = jnp.einsum("ka,kbc->abc", table_re, gathered_re, preferred_element_type=jnp.float32)
    conv_vals = conv_vals + jnp.einsum(
        "ka,kbc->abc", table_im, gathered_im, preferred_element_type=jnp.float32
    )
    conv_vals = (conv_vals * (1.0 / freq_total)).astype(jnp.bfloat16)
    conv_tokens = token_rows(conv_vals).reshape(tok_rows, chan_local)
    finished = acts_local + query.astype(jnp.float32) * (
        conv_tokens.astype(jnp.float32) + skip_gain[0][None, :] * product.astype(jnp.float32)
    )
    received = passed_along(finished.astype(jnp.bfloat16), "section", 1).astype(finished.dtype)
    return received[None]


EXTRA = 16
LANES = 128
DEPTH = 64


def odd_tables(length):
    ahead, back = [], []
    for first in range(2):
        phase = (2 * np.arange(length // 2)[:, None] + 1) * np.arange(first, length, 2)[None, :] % (4 * length)
        turn = phase * (2.0 * np.pi / (4 * length))
        ahead.append(np.concatenate([np.cos(turn), -np.sin(turn)], axis=0))
        back.append(ahead[-1].T / length)
    return [np.concatenate(parts, axis=0).astype(ml_dtypes.bfloat16) for parts in (ahead, back)]


def spread_table(filters, channels):
    owner = np.arange(channels) // (channels // filters)
    return (np.arange(filters)[:, None] == owner[None, :]).astype(ml_dtypes.bfloat16)


def column_of(row):
    return jnp.transpose(jnp.broadcast_to(row, (LANES, row.shape[1])))


def three_terms(x):
    terms = []
    for _ in range(3):
        terms.append(x.astype(jnp.bfloat16).astype(jnp.float32))
        x = x - terms[-1]
    return terms


def next_place(rank, step, peers):
    return lax.rem(rank + step + peers, peers)


def cut_kernel(peers, x_hbm, filt_hbm, *refs):
    outs, (sums_ref, x_ref, filt_ref, plain, turned, sems) = refs[:peers], refs[peers:]
    rank = lax.axis_index("ctx")
    rows, chans = x_hbm.shape
    part, width = rows // 2, chans // peers
    filters = filt_hbm.shape[1] // peers
    tiles = width // LANES
    copies = [pltpu.make_async_copy(filt_hbm, filt_ref, sems.at[peers * tiles])]
    for step in range(peers):
        begin = next_place(rank, step, peers) * width
        for tile in range(tiles):
            lanes = pl.ds(pl.multiple_of(begin + tile * LANES, LANES), LANES)
            at = step * tiles + tile
            copies.append(pltpu.make_async_copy(x_hbm.at[:, lanes], x_ref.at[at], sems.at[at]))
    for i, copy in enumerate(copies):
        copy.start(priority=i % 2)
    copies[0].wait()
    for at in range(plain.shape[0]):
        lanes = slice(at * LANES, (at + 1) * LANES)
        plain[at] = filt_ref[:, lanes].astype(jnp.float32)
        halves = [plain[at, pl.ds(odd, part, stride=2), :] for odd in range(2)]
        turned[lanes, :] = jnp.transpose(jnp.concatenate(halves, axis=0)).astype(jnp.bfloat16)
    base = tiles * rows
    for step in range(peers):
        own = pl.ds(pl.multiple_of(next_place(rank, step, peers) * filters, filters), filters)
        outs[step][base : base + filters, :] = turned[own, :]
    totals = [jnp.zeros((part, LANES), jnp.float32)] * 2
    for step in range(peers):
        for tile in range(tiles):
            at = step * tiles + tile
            copies[1 + at].wait()
            for odd in range(2):
                acts = x_ref[at, pl.ds(odd, part, stride=2), :]
                top = tile * rows + odd * part
                outs[step][top : top + part, :] = acts.astype(jnp.bfloat16)
                totals[odd] = totals[odd] + acts * acts
    column = jnp.sum(jnp.concatenate(totals, axis=0), axis=1, keepdims=True)
    row = jnp.transpose(jnp.broadcast_to(column, (rows, LANES)))[:EXTRA, :]
    nth = lax.broadcasted_iota(jnp.int32, (EXTRA, rows), 0)
    terms = three_terms(row)
    sums = jnp.where(nth == 0, terms[0], jnp.where(nth == 1, terms[1], jnp.where(nth == 2, terms[2], 0.0)))
    sums_ref[...] = sums.astype(jnp.bfloat16)
    for step in range(peers):
        outs[step][base + filters :, :] = sums.astype(jnp.bfloat16)


def attach_kernel(count, *refs):
    messages, (own_ref, other_ref) = refs[:count], refs[count : count + 2]
    outs = refs[count + 2 :]
    both = own_ref[...].astype(jnp.float32) + pltpu.roll(other_ref[...].astype(jnp.float32), 3, 0)
    for out in outs:
        out[out.shape[0] - EXTRA :, :] = both.astype(jnp.bfloat16)


def collect_kernel(count, *refs):
    out = refs[-1]
    for i in range(count):
        out[i * EXTRA : (i + 1) * EXTRA, :] = refs[i][refs[i].shape[0] - EXTRA :, :]


def table_kernel(pieces, after, *refs):
    count = (len(refs) - 1) // 2
    tables, outs, sems = refs[:count], refs[count : 2 * count], refs[2 * count]
    copies = []
    for t in range(count):
        parts = pieces if tables[t].shape[0] % (pieces * LANES) == 0 else 1
        depth = tables[t].shape[0] // parts
        for i in range(parts):
            here = pl.ds(i * depth, depth)
            copies.append(pltpu.make_async_copy(tables[t].at[here], outs[t].at[here], sems.at[len(copies)]))
    for copy in copies:
        copy.start()
    for copy in copies:
        copy.wait()


def scale_of(*sums):
    square = sum(jnp.sum(terms.astype(jnp.float32), axis=0, keepdims=True) for terms in sums)
    return column_of(lax.rsqrt(square * (1.0 / CHAN) + 1e-06))


def scale_block(block, scale, held):
    rows = block.shape[1]
    part = rows // 2
    for tile in range(held.shape[2] // LANES):
        for odd in range(2):
            own = tile * rows + odd * part
            acts = block[own : own + part, :].astype(jnp.float32) * scale[odd * part : (odd + 1) * part]
            held[odd, 8:, tile * LANES : (tile + 1) * LANES] = acts


def short_filters(held, depth, taps, lanes):
    now = [held[odd, 8 : 8 + depth, lanes] for odd in range(2)]
    last = [held[odd, 7 : 7 + depth, lanes] for odd in range(2)]
    results = []
    for moved in ((now[0], last[1], last[0]), (now[1], now[0], last[1])):
        features = []
        for feature in taps:
            running = feature[0][:, lanes] * moved[0]
            for i in range(1, TAPS):
                running = running + feature[i][:, lanes] * moved[i]
            features.append(running)
        results.append((features[0].astype(jnp.bfloat16), (features[1] * features[2]).astype(jnp.bfloat16)))
    return results


def read_taps(taps_ref, chans):
    return [[taps_ref[f, i : i + 1, chans].astype(jnp.float32) for i in range(TAPS)] for f in range(3)]


def spread_out(block, spread_ref):
    filters = spread_ref.shape[0]
    base = block.shape[0] - EXTRA - filters
    return lax.dot_general(
        block[base : base + filters, :],
        spread_ref[...],
        (((0,), (0,)), ((), ())),
        preferred_element_type=jnp.float32,
    ).astype(jnp.bfloat16)


def lead_in(held, before, inside):
    for odd in range(2):
        row = before[odd, before.shape[1] - 1 :, :]
        held[odd, 7:8, :] = jnp.where(inside, row, 0.0)


def early_kernel(peers, early, *refs):
    count = len(early)
    blocks, halves = refs[:count], refs[count : 3 * count]
    taps_ref, spread_ref, held, query, product, spread = refs[3 * count :]
    width, part = held.shape[3], held.shape[2] - 8
    rank = lax.axis_index("ctx")
    chans = pl.ds(pl.multiple_of(rank * width, width), width)
    taps = read_taps(taps_ref, chans)
    for i in range(count):
        held[i, :, :8, :] = jnp.zeros((2, 8, width), jnp.float32)
        scale_block(blocks[i], scale_of(halves[2 * i][...], halves[2 * i + 1][...]), held.at[i])
    for i, step in enumerate(early):
        before = (step + 1) % peers
        if before in early:
            lead_in(held.at[i], held.at[early.index(before)], next_place(rank, -step, peers) > 0)
    tokens = [pl.ds(pl.multiple_of(next_place(rank, -step, peers) * part, part), part) for step in early]
    for first in range(0, width, LANES):
        lanes = slice(first, first + LANES)
        for i in range(count):
            for odd, results in enumerate(short_filters(held.at[i], part, taps, lanes)):
                query[odd, tokens[i], lanes], product[odd, tokens[i], lanes] = results
    for i in range(count):
        both = spread_out(blocks[i], spread_ref)
        for odd in range(2):
            spread[odd, tokens[i], :] = both[odd * part : (odd + 1) * part]


def layer_kernel(peers, early, late, *refs):
    blocks = refs[:peers]
    taps_ref, skip_ref, ahead_ref, return_ref, spread_ref = refs[peers : peers + 5]
    early_held = refs[peers + 5]
    outs = refs[peers + 9 : 2 * peers + 9]
    query, product, spread, held, top_held, spec, filt_spec, weighted, conv = refs[2 * peers + 9 :]
    rank = lax.axis_index("ctx")
    rows, width = outs[0].shape
    part, half = rows // 2, rows * peers // 2
    top = top_held.shape[2] - 8
    chans = pl.ds(pl.multiple_of(rank * width, width), width)
    taps = read_taps(taps_ref, chans)
    skip = skip_ref[:, chans]
    places = [next_place(rank, -step, peers) for step in range(peers)]
    tokens = [pl.ds(pl.multiple_of(place * part, part), part) for place in places]
    tops = [pl.ds(pl.multiple_of(place * part, part), top) for place in places]

    for step in late:
        both = spread_out(blocks[step], spread_ref)
        for odd in range(2):
            spread[odd, tokens[step], :] = both[odd * part : (odd + 1) * part]
    for i, step in enumerate(late):
        scale_block(blocks[step], scale_of(blocks[step][blocks[step].shape[0] - EXTRA :, :]), held.at[i])
    sources = [(held.at[i], part, step) for i, step in enumerate(late)]
    lacking = [step for step in early if (step + 1) % peers in late]
    for i, step in enumerate(lacking):
        top_held[i, :, 8:, :] = early_held[early.index(step), :, 8 : 8 + top, :]
        sources.append((top_held.at[i], top, step))
    for source, _, step in sources:
        before = (step + 1) % peers
        theirs = held.at[late.index(before)] if before in late else early_held.at[early.index(before)]
        lead_in(source, theirs, places[step] > 0)
    for first in range(0, width, LANES):
        lanes = slice(first, first + LANES)
        for source, depth, step in sources:
            here = tokens[step] if depth == part else tops[step]
            for odd, results in enumerate(short_filters(source, depth, taps, lanes)):
                query[odd, here, lanes], product[odd, here, lanes] = results
    for odd in range(2):
        table = ahead_ref[2 * odd * half : 2 * (odd + 1) * half, :]
        filt_spec[odd] = jnp.dot(table, spread[odd], preferred_element_type=jnp.float32)
        spec[odd] = jnp.dot(table, product[odd], preferred_element_type=jnp.float32)
    for first in range(0, width, LANES):
        lanes = slice(first, first + LANES)
        for begin in range(0, half, DEPTH):
            re, im = slice(begin, begin + DEPTH), slice(half + begin, half + begin + DEPTH)
            near, far = [], []
            for values in (spec, filt_spec):
                even_re, even_im = values[0, re, lanes], values[0, im, lanes]
                odd_re, odd_im = values[1, re, lanes], values[1, im, lanes]
                near += [even_re + odd_re, even_im + odd_im]
                far += [even_re - odd_re, odd_im - even_im]
            near_re, near_im = product_of(*near)
            far_re, far_im = product_of(*far)
            weighted[0, re, lanes] = (near_re + far_re).astype(jnp.bfloat16)
            weighted[0, im, lanes] = (near_im - far_im).astype(jnp.bfloat16)
            weighted[1, re, lanes] = (near_re - far_re).astype(jnp.bfloat16)
            weighted[1, im, lanes] = (near_im + far_im).astype(jnp.bfloat16)
    for odd in range(2):
        table = return_ref[odd * half : (odd + 1) * half, :]
        conv[odd] = jnp.dot(table, weighted[odd], preferred_element_type=jnp.float32)
    for step in range(peers):
        source = (peers - step) % peers
        here = tokens[source]
        for tile in range(width // LANES):
            lanes = slice(tile * LANES, (tile + 1) * LANES)
            for odd in range(2):
                own = tile * rows + odd * part
                acts = blocks[source][own : own + part, :].astype(jnp.float32)
                gated = conv[odd, here, lanes] + skip[:, lanes] * product[odd, here, lanes].astype(jnp.float32)
                finished = acts + query[odd, here, lanes].astype(jnp.float32) * gated
                outs[step][odd * part : (odd + 1) * part, lanes] = finished.astype(jnp.bfloat16)


def product_of(left_re, left_im, right_re, right_im):
    return left_re * right_re - left_im * right_im, left_re * right_im + left_im * right_re


def join_kernel(peers, steps, *refs):
    parts, (out_hbm, wide, sems) = refs[: len(steps)], refs[-3:]
    rows, width = parts[0].shape
    rank = lax.axis_index("ctx")
    tiles = width // LANES
    copies = []
    for i, step in enumerate(steps):
        begin = next_place(rank, -step, peers) * width
        for tile in range(tiles):
            at = i * tiles + tile
            for odd in range(2):
                part = parts[i][odd * (rows // 2) : (odd + 1) * (rows // 2), tile * LANES : (tile + 1) * LANES]
                wide[at, pl.ds(odd, rows // 2, stride=2), :] = part.astype(jnp.float32)
            lanes = pl.ds(pl.multiple_of(begin + tile * LANES, LANES), LANES)
            copies.append(pltpu.make_async_copy(wide.at[at], out_hbm.at[:, lanes], sems.at[at]))
            copies[-1].start(priority=at % 2)
    for copy in copies:
        copy.wait()


def on_device(kernel, args, outs, scratch=(), in_hbm=(), out_hbm=False, flops=0, limit=32, aliases=None):
    whole = pl.BlockSpec(memory_space=pltpu.VMEM)
    far = pl.BlockSpec(memory_space=pltpu.HBM)
    touched = sum(a.size * a.dtype.itemsize for a in (*args, *outs))
    args = [pltpu.with_memory_space_constraint(a, pltpu.HBM) if i in in_hbm else a for i, a in enumerate(args)]
    return pl.pallas_call(
        kernel,
        out_shape=outs,
        in_specs=[far if i in in_hbm else whole for i in range(len(args))],
        out_specs=[far if out_hbm else whole] * len(outs),
        scratch_shapes=list(scratch),
        input_output_aliases=aliases or {},
        compiler_params=pltpu.CompilerParams(vmem_limit_bytes=limit * 2**20),
        cost_estimate=pl.CostEstimate(flops=flops, bytes_accessed=touched, transcendentals=0),
    )(*args)


def hop(x, sections, peers, by_section, by_ctx):
    route = [
        (s * peers + c, (s + by_section) % sections * peers + (c + by_ctx) % peers)
        for s in range(sections)
        for c in range(peers)
    ]
    return lax.ppermute(x, ("section", "ctx"), route)


def channel_local(section_input, long_filter, short_filter, skip_gain):
    acts = section_input[0]
    rows, chans = acts.shape
    sections, peers = lax.axis_size("section"), lax.axis_size("ctx")
    width, filters = chans // peers, long_filter.shape[2] // peers
    length = rows * peers
    half = length // 2
    bf16, f32 = jnp.bfloat16, jnp.float32
    pieces = 4
    part, tail = rows // 2, width // LANES * rows + filters
    message = jax.ShapeDtypeStruct((tail + EXTRA, rows), bf16)
    *sent, own_sums = on_device(
        functools.partial(cut_kernel, peers),
        [acts, long_filter[0]],
        [message] * peers + [jax.ShapeDtypeStruct((EXTRA, rows), bf16)],
        [
            pltpu.VMEM((chans // LANES, rows, LANES), f32),
            pltpu.VMEM(long_filter.shape[1:], bf16),
            pltpu.VMEM((long_filter.shape[2] // LANES, rows, LANES), f32),
            pltpu.VMEM((long_filter.shape[2], rows), bf16),
            pltpu.SemaphoreType.DMA((chans // LANES + 1,)),
        ],
        in_hbm=(0, 1),
    )
    early, late = [0, 1], list(range(peers - 1, 1, -1))
    got = {0: sent[0]}
    for k in early[1:]:
        got[k] = hop(sent[k], sections, peers, 0, k)
    other_sums = lax.ppermute(own_sums, "tp", [(0, 1), (1, 0)])
    ready = on_device(
        functools.partial(attach_kernel, len(late)),
        [*(sent[k] for k in late), own_sums, other_sums],
        [message] * len(late),
        aliases={i: i for i in range(len(late))},
    )
    for k, x in zip(late, ready):
        got[k] = hop(x, sections, peers, 0, k)
    tables = [jnp.asarray(t) for t in (*odd_tables(length), spread_table(filters, width))]
    tables += [short_filter[0], skip_gain]
    ahead, back, spread, taps, skip = on_device(
        functools.partial(table_kernel, pieces),
        [other_sums, *tables],
        [jax.ShapeDtypeStruct(t.shape, t.dtype) for t in tables],
        [pltpu.SemaphoreType.DMA((pieces * len(tables),))],
        in_hbm=range(1, 1 + len(tables)),
    )
    (halves,) = on_device(
        functools.partial(collect_kernel, len(early) - 1),
        [*(got[k] for k in early[1:]), ready[0]],
        [jax.ShapeDtypeStruct(((len(early) - 1) * EXTRA, rows), bf16)],
    )
    others = lax.ppermute(halves, "tp", [(0, 1), (1, 0)])
    pairs = [own_sums, other_sums]
    for i in range(len(early) - 1):
        pairs += [half_sums[i * EXTRA : (i + 1) * EXTRA] for half_sums in (halves, others)]
    begun = on_device(
        functools.partial(early_kernel, peers, early),
        [*(got[k] for k in early), *pairs, taps, spread],
        [
            jax.ShapeDtypeStruct((len(early), 2, part + 8, width), f32),
            *[jax.ShapeDtypeStruct((2, half, width), bf16)] * 3,
        ],
    )
    done = on_device(
        functools.partial(layer_kernel, peers, early, late),
        [*(got[k] for k in range(peers)), taps, skip, ahead, back, spread, *begun],
        [
            *[jax.ShapeDtypeStruct((rows, width), bf16)] * peers,
            *[jax.ShapeDtypeStruct((2, half, width), bf16)] * 3,
        ],
        [
            pltpu.VMEM((len(late), 2, part + 8, width), f32),
            pltpu.VMEM((2, 2, EXTRA + 8, width), f32),
            pltpu.VMEM((2, length, width), f32),
            pltpu.VMEM((2, length, width), f32),
            pltpu.VMEM((2, length, width), bf16),
            pltpu.VMEM((2, half, width), f32),
        ],
        flops=6 * length * length * width,
        aliases={peers + 6 + i: peers + i for i in range(3)},
    )
    order = sorted(range(peers), key=lambda k: (k % 2, k))
    arrived = {k: hop(done[k], sections, peers, 1, k) for k in order}
    out = jax.ShapeDtypeStruct((rows, chans), f32)
    tiles = width // LANES
    received = None
    for steps in (order[: peers // 2], order[peers // 2 :]):
        (received,) = on_device(
            functools.partial(join_kernel, peers, steps),
            [arrived[k] for k in steps] + ([] if received is None else [received]),
            [out],
            [pltpu.VMEM((len(steps) * tiles, rows, LANES), f32), pltpu.SemaphoreType.DMA((len(steps) * tiles,))],
            in_hbm=(len(steps),),
            out_hbm=True,
            aliases={} if received is None else {len(steps): 0},
        )
    return received[None]


def fits_channel_plan(mesh, section_input, long_filter):
    peers, cores = mesh.shape["ctx"], mesh.shape["tp"]
    tokens = section_input.shape[1]
    width = section_input.shape[2] // (peers * cores)
    filters = long_filter.shape[2] // (peers * cores)
    return (
        peers > 2
        and tokens == peers * LANES
        and tokens <= 1024
        and width % LANES == 0
        and filters % EXTRA == 0
        and long_filter.shape[2] // cores % LANES == 0
    )


def solution(mesh):
    in_specs = (
        P("section", "ctx", "tp"),
        P("section", "ctx", "tp"),
        P("section", None, None, "tp"),
        P("section", "tp"),
    )
    out_specs = P("section", "ctx", "tp")

    def layer(section_input, long_filter, short_filter, skip_gain):
        local = channel_local if fits_channel_plan(mesh, section_input, long_filter) else general_local
        mapped = jax.shard_map(local, mesh=mesh, in_specs=in_specs, out_specs=out_specs, check_vma=False)
        return mapped(section_input, long_filter, short_filter, skip_gain)

    return layer
```
